32 devices in a mesh: section: 8 (over y, x, core), dp: 4 (over z).
Axes of the slice: x: 2, y: 2, z: 4, core: 2. Of those that a mesh axis runs over, the one named last changes fastest.
Arguments:
- token_ids: int32 [8, 4, 256], P(None, 'dp'), may hold values from 0 to 26
- order: int32 [8, 4, 256], P(None, 'dp'), may hold values from 0 to 255, each once within a row
- timesteps: int32 [8, 4], P(None, 'dp'), may hold values from 0 to 255
- table: float32 [28, 512], replicated, may hold values from -0.5 to 0.5
- norm_gain: float32 [8, 2, 512], P('section', None, 'dp'), may hold values from 0.5 to 1.5
- norm_bias: float32 [8, 2, 512], P('section', None, 'dp'), may hold values from -1.8 to 1.8
- w_qkv: float32 [8, 512, 1536], P('section', 'dp'), may hold values from -0.25 to 0.25
- w_out: float32 [8, 512, 512], P('section', 'dp'), may hold values from -1 to 1
- w_in: float32 [8, 512, 2048], P('section', 'dp'), may hold values from -0.25 to 0.25
- w_down: float32 [8, 2048, 512], P('section', 'dp'), may hold values from -0.125 to 0.125
Outputs:
- table_grad: float32 [28, 512], P(None, 'section')
- gain_grad: float32 [8, 2, 512], P('section', None, 'dp')
- bias_grad: float32 [8, 2, 512], P('section', None, 'dp')
- w_qkv_grad: float32 [8, 512, 1536], P('section', 'dp')
- w_out_grad: float32 [8, 512, 512], P('section', 'dp')
- w_in_grad: float32 [8, 512, 2048], P('section', 'dp')
- w_down_grad: float32 [8, 2048, 512], P('section', 'dp')
The draws below stay inside these ranges and needn't reach their ends.
All inputs are finite; a program needn't handle non-finite values.
Results may differ from the reference program's by a relative error of at most 0.012.
The reference program's roundings to bfloat16 on the way count: a program that leaves them out, or rounds other values in their place, can miss the bound.
Values may be sent and summed in bfloat16 or wider, within the bound.
A program may use at most 128 MiB of HBM per device.

```python
import math
import jax
import jax.numpy as jnp
import numpy as np
from jax import lax

D = 512
HEADS = 8
HEAD_DIM = 64
FF = 2048
VOCAB = 28
LENGTH = 256
MICRO = 8
LAYERS = 8
BATCH = 4


def plant(values, key, low, largest):
    longest = values.shape.index(max(values.shape))
    spots = []
    for shift in (0, 1):
        where = [jax.random.randint(jax.random.fold_in(key, axis), (), 0, length) for axis, length in enumerate(values.shape)]
        where[longest] = (where[longest] + shift) % values.shape[longest]
        spots.append(tuple(where))
    return values.at[spots[0]].set(low).at[spots[1]].set(largest)


def block_scale(key, dims, shards, least, largest):
    def one(position, shards_of):
        heights = jax.random.uniform(jax.random.fold_in(jax.random.fold_in(key, 6), position), (shards_of,), jnp.float32, least / len(shards), largest / len(shards))
        return jnp.repeat(jnp.exp(heights), dims[position] // shards_of).reshape((-1,) + (1,) * (len(dims) - position - 1))

    gain = one(*shards[0])
    for cut in shards[1:]:
        gain = gain * one(*cut)
    return gain


def rank_table(number_of, slope):
    loads = [(1 << 20) // math.isqrt(standing ** slope) + 1 for standing in range(1, number_of + 1)]
    width = 1 + sum(loads) // (1 << 30)
    return np.cumsum(np.array([max(1, weight // width) for weight in loads]))


def ranked(stream_key, dims, count, slope):
    table = rank_table(count, slope)
    lot = jax.random.randint(jax.random.fold_in(stream_key, 1), dims, 0, int(table[count - 1]))
    grade = jnp.searchsorted(jnp.asarray(table, jnp.int32), lot, side="right")
    return jax.random.permutation(jax.random.fold_in(stream_key, 2), count)[grade].astype(jnp.int32)


def noise(key, shape, width, bound, cuts=(), kind=jnp.bfloat16):
    result = jax.random.normal(key, shape, jnp.float32) * width
    if len(cuts) > 0:
        result = block_scale(key, shape, cuts, -0.22, 0.18) * result
    return jnp.clip(result, min=-bound, max=bound).astype(kind)


def setup_inputs(seed: int = 0) -> dict:
    splits = jax.random.split(jax.random.key(seed), 11)
    token_ids = plant(ranked(splits[0], (MICRO, BATCH, LENGTH), 27, 2), jax.random.fold_in(splits[0], 3), 0, 26).astype(jnp.int32)
    order = jax.vmap(lambda own: jax.random.permutation(own, LENGTH))(jax.random.split(splits[1], MICRO * BATCH)).reshape((MICRO, BATCH, LENGTH)).astype(jnp.int32)
    timesteps = plant(jax.random.randint(splits[2], (MICRO, BATCH), 0, LENGTH), jax.random.fold_in(splits[2], 1), 0, LENGTH - 1).astype(jnp.int32)
    table = noise(splits[3], (VOCAB, D), 128 ** -0.5, 0.5, (), jnp.float32)
    norm_gain = jnp.clip(1.0 + 0.1 * jax.random.normal(splits[4], (LAYERS, 2, D), jnp.float32), 0.5, 1.5)
    norm_bias = noise(splits[5], (LAYERS, 2, D), 0.3, 1.8, ((0, 8), (2, 4)), jnp.float32)
    w_qkv = noise(splits[6], (LAYERS, D, 3 * D), D ** -0.5, 0.25, ((0, 8), (1, 4)), jnp.float32)
    w_out = noise(splits[7], (LAYERS, D, D), (D // 16) ** -0.5, 1.0, ((0, 8), (1, 4)), jnp.float32)
    w_in = noise(splits[8], (LAYERS, D, FF), D ** -0.5, 0.25, ((0, 8), (1, 4)), jnp.float32)
    w_down = noise(splits[9], (LAYERS, FF, D), FF ** -0.5, 0.125, ((0, 8), (1, 4)), jnp.float32)
    return {"token_ids": token_ids, "order": order, "timesteps": timesteps, "table": table, "norm_gain": norm_gain, "norm_bias": norm_bias, "w_qkv": w_qkv, "w_out": w_out, "w_in": w_in, "w_down": w_down}


@jax.custom_vjp
def low(v):
    return lax.optimization_barrier(v.astype(jnp.bfloat16)).astype(jnp.float32)

@jax.custom_vjp
def low_back(v):
    return v

def low_keep(v):
    return (low(v), None)

def low_pass(kept, grad):
    return (grad,)

def back_keep(v):
    return (v, None)

def back_low(kept, grad):
    return (low(grad),)
low.defvjp(low_keep, low_pass)
low_back.defvjp(back_keep, back_low)
EPSILON = 1e-05
EMBED_GAIN = 16.0

def unit_rows(values):
    average = lax.optimization_barrier(jnp.mean(values, axis=-1, keepdims=True))
    centered = values - average
    variance = lax.optimization_barrier(jnp.mean(centered * centered, axis=-1, keepdims=True))
    return centered * lax.rsqrt(variance + EPSILON)

def layer_norm(values, gain_row, offset):
    return unit_rows(values) * gain_row + offset

def block_forward(hidden, gain_pair, bias_pair, w_qkv, w_out, w_in, w_down):
    highest = lax.Precision.HIGHEST
    seq_count, length = (hidden.shape[0], hidden.shape[1])
    score_scale = 1.0 / math.sqrt(HEAD_DIM)
    normed = low(layer_norm(hidden, gain_pair[0], bias_pair[0]))
    packed = low_back(low(jnp.einsum('btd,de->bte', normed, w_qkv, precision=highest)))
    heads_view = packed.reshape(seq_count, length, 3, HEADS, HEAD_DIM)
    query_rows, key_rows, value_rows = (heads_view[:, :, 0], heads_view[:, :, 1], heads_view[:, :, 2])
    scores = low_back(jnp.einsum('bqhe,bkhe->bhqk', query_rows, key_rows, precision=highest) * score_scale)
    attention = low(jax.nn.softmax(scores, axis=-1))
    mixed_rows = jnp.einsum('bhqk,bkhe->bqhe', attention, value_rows, precision=highest)
    mixed_rows = low_back(low(mixed_rows.reshape(seq_count, length, D)))
    middle = hidden + low_back(jnp.einsum('btd,de->bte', mixed_rows, w_out, precision=highest))
    normed_two = low(layer_norm(middle, gain_pair[1], bias_pair[1]))
    lifted = low_back(jnp.einsum('btd,df->btf', normed_two, w_in, precision=highest))
    activated = low(jax.nn.gelu(lifted))
    output = middle + low_back(jnp.einsum('btf,fd->btd', activated, w_down, precision=highest))
    return low_back(low(output))

def micro_objective(table, norm_gain, norm_bias, w_qkv, w_out, w_in, w_down, token_rows, order_rows, stamp_rows):
    visible = order_rows < stamp_rows[:, None]
    shown = jnp.where(visible, token_rows, VOCAB - 1)
    hidden = table[shown] * EMBED_GAIN
    stacked = (low(norm_gain), low(norm_bias), low(w_qkv), low(w_out), low(w_in), low(w_down))

    def layer_step(running, layer_params):
        return (jax.checkpoint(block_forward)(running, *layer_params), None)
    hidden, _ = lax.scan(layer_step, hidden, stacked)
    normalized = low(unit_rows(hidden))
    logits = low_back(jnp.einsum('btd,vd->btv', normalized, low(table), precision=lax.Precision.HIGHEST))
    log_total = jax.nn.logsumexp(logits, axis=-1)
    picked = lax.optimization_barrier(jnp.sum(logits * jax.nn.one_hot(token_rows, VOCAB, dtype=jnp.float32), axis=-1))
    weight_rows = jnp.where(visible, 0.0, 1.0) / (LENGTH - stamp_rows)[:, None].astype(jnp.float32)
    return jnp.sum(weight_rows * (log_total - picked))

def reference(token_ids, order, timesteps, table, norm_gain, norm_bias, w_qkv, w_out, w_in, w_down):
    params = (table, norm_gain, norm_bias, w_qkv, w_out, w_in, w_down)

    def micro_step(running, inputs):
        token_rows, order_rows, stamp_rows = inputs

        def objective(*weights):
            return micro_objective(*weights, token_rows, order_rows, stamp_rows)
        value, pullback = jax.vjp(objective, *params)
        gradients = pullback(jnp.ones((), jnp.float32))
        summed = tuple((before + gradient for before, gradient in zip(running, gradients)))
        return (summed, None)
    initial = tuple((jnp.zeros_like(tensor) for tensor in params))
    grads_all, _ = lax.scan(micro_step, initial, (token_ids, order, timesteps))
    return (grads_all[0], grads_all[1], grads_all[2], grads_all[3], grads_all[4], grads_all[5], grads_all[6])
```

```python
import functools
import math

import jax
import jax.numpy as jnp
from jax import lax
from jax.experimental import pallas as pl
from jax.experimental.pallas import tpu as pltpu
from jax.sharding import PartitionSpec as P

HEADS = 8
EPSILON = 1e-05
EMBED_GAIN = 16.0
FF_CHUNK = 512
MESH = pl.DeviceIdType.MESH


def dot(left, right, left_dim, right_dim):
    return lax.dot_general(
        left, right, (((left_dim,), (right_dim,)), ((), ())), preferred_element_type=jnp.float32
    )


def unit_rows(values):
    average = jnp.mean(values, axis=-1, keepdims=True)
    centered = values - average
    variance = jnp.mean(centered * centered, axis=-1, keepdims=True)
    scale = lax.rsqrt(variance + EPSILON)
    return centered * scale, scale


def unit_back(gradient, unit, scale):
    first = jnp.mean(gradient, axis=-1, keepdims=True)
    second = jnp.mean(gradient * unit, axis=-1, keepdims=True)
    return scale * (gradient - first - unit * second)


def fold_rows(values):
    rows, columns = values.shape
    return jnp.sum(values.reshape(rows // 8, 8, columns), axis=0)


def pipeline_kernel(
    stages,
    token_ref,
    order_ref,
    stamp_ref,
    table_ref,
    gain_ref,
    bias_ref,
    w_qkv_ref,
    w_out_ref,
    w_in_ref,
    w_down_ref,
    d_table_ref,
    d_gain_ref,
    d_bias_ref,
    d_qkv_ref,
    d_out_ref,
    d_in_ref,
    d_down_ref,
    stash_ref,
    h_in,
    g_in,
    h_send,
    g_send,
    packed,
    mixed,
    middle,
    active,
    slope,
    attention_out,
    attention_in,
    work,
    table_parts,
    norm_sums,
    table_sum,
    h_send_sem,
    h_recv_sem,
    g_send_sem,
    g_recv_sem,
    stash_sem,
):
    micro_count, _, length = token_ref.shape
    vocab, width = table_ref.shape
    hidden_units = w_in_ref.shape[1]
    head_size = width // HEADS
    score_scale = 1.0 / math.sqrt(head_size)
    pair_width = 2 * head_size
    stage = lax.axis_index("section")
    last = stages - 1
    bf16, f32 = jnp.bfloat16, jnp.float32

    if stages > 1:
        ahead, behind = lax.rem(stage + 1, stages), lax.rem(stage + stages - 1, stages)
        barrier = pltpu.get_barrier_semaphore()
        for neighbour in (ahead, behind):
            pl.semaphore_signal(
                barrier, inc=1, device_id={"section": neighbour}, device_id_type=MESH
            )
        pl.semaphore_wait(barrier, 2)

    table_rows = table_parts.shape[1]
    work[:table_rows, :] = jnp.zeros((table_rows, width), f32)
    work[:vocab, :] = table_ref[...]
    rest = work[:table_rows, :]
    for part in range(3):
        rounded = rest.astype(bf16)
        table_parts[part] = rounded
        rest = rest - rounded.astype(f32)
    d_qkv_ref[...] = jnp.zeros_like(d_qkv_ref)
    d_out_ref[...] = jnp.zeros_like(d_out_ref)
    d_in_ref[...] = jnp.zeros_like(d_in_ref)
    d_down_ref[...] = jnp.zeros_like(d_down_ref)
    norm_sums[...] = jnp.zeros_like(norm_sums)
    table_sum[...] = jnp.zeros_like(table_sum)

    letters = lax.broadcasted_iota(jnp.int32, (table_rows, length), 0)
    lane = lax.broadcasted_iota(jnp.int32, (length, pair_width), 1)
    lower = lane < head_size

    def shown_rows(micro):
        visible = order_ref[micro] < stamp_ref[micro]
        shown = jnp.where(visible, token_ref[micro], vocab - 1)
        return (letters == shown).astype(bf16)

    def halves(pair):
        zero = jnp.zeros_like(pair)
        return jnp.where(lower, pair, zero), jnp.where(lower, zero, pair)

    def load_hidden(micro):
        @pl.when(stage == 0)
        def _():
            hot = shown_rows(micro)
            total = dot(hot, table_parts[2], 0, 0)
            total = total + dot(hot, table_parts[1], 0, 0)
            total = total + dot(hot, table_parts[0], 0, 0)
            work[...] = total * EMBED_GAIN

        @pl.when(stage > 0)
        def _():
            work[...] = h_in[micro].astype(f32)

    def hidden_copy(micro, target):
        slot = lax.rem(micro, 2)
        return pltpu.make_async_remote_copy(
            src_ref=h_send.at[slot],
            dst_ref=h_in.at[micro],
            send_sem=h_send_sem.at[slot],
            recv_sem=h_recv_sem.at[micro],
            device_id={"section": target},
            device_id_type=MESH,
        )

    def gradient_copy(micro, target):
        slot = lax.rem(micro, 2)
        return pltpu.make_async_remote_copy(
            src_ref=g_send.at[slot],
            dst_ref=g_in.at[micro],
            send_sem=g_send_sem.at[slot],
            recv_sem=g_recv_sem.at[micro],
            device_id={"section": target},
            device_id_type=MESH,
        )

    def forward(micro):
        if stages > 1:
            @pl.when(stage > 0)
            def _():
                hidden_copy(micro, behind).wait_recv()
        load_hidden(micro)
        hidden = work[...]
        unit, _ = unit_rows(hidden)
        normed = (unit * gain_ref[0:1, :] + bias_ref[0:1, :]).astype(bf16)
        packed[micro] = dot(normed, w_qkv_ref[...], 1, 0).astype(bf16)
        for pair in range(HEADS // 2):
            at = pair * pair_width
            query = packed[micro, :, at : at + pair_width] * jnp.asarray(score_scale, bf16)
            key = packed[micro, :, width + at : width + at + pair_width]
            value = packed[micro, :, 2 * width + at : 2 * width + at + pair_width]
            found = []
            for side, part in enumerate(halves(query)):
                scores = dot(part, key, 1, 1)
                largest = jnp.max(scores, axis=-1, keepdims=True)
                powers = jnp.exp(scores - largest)
                total = jnp.sum(powers, axis=-1, keepdims=True)
                attention = (powers * (1.0 / total)).astype(bf16)
                attention_out[2 * pair + side] = attention
                found.append(dot(attention, value, 1, 0))
            mixed[micro, :, at : at + pair_width] = jnp.where(lower, found[0], found[1]).astype(
                bf16
            )
        save = pltpu.make_async_copy(attention_out, stash_ref.at[micro], stash_sem)
        save.start()
        between = hidden + dot(mixed[micro], w_out_ref[...], 1, 0)
        high = between.astype(bf16)
        middle[micro, 0] = high
        middle[micro, 1] = (between - high.astype(f32)).astype(bf16)
        work[...] = between
        unit, _ = unit_rows(between)
        normed_two = (unit * gain_ref[1:2, :] + bias_ref[1:2, :]).astype(bf16)
        for at in range(0, hidden_units, FF_CHUNK):
            lifted = dot(normed_two, w_in_ref[:, at : at + FF_CHUNK], 1, 0)
            square = lifted * lifted
            inner = math.sqrt(2.0 / math.pi) * lifted * (1.0 + 0.044715 * square)
            bend = jnp.tanh(inner)
            half = 0.5 * (1.0 + bend)
            active[micro, :, at : at + FF_CHUNK] = (lifted * half).astype(bf16)
            steep = math.sqrt(2.0 / math.pi) * (1.0 + 3.0 * 0.044715 * square)
            slope[micro, :, at : at + FF_CHUNK] = (
                half + 0.5 * lifted * (1.0 - bend * bend) * steep
            ).astype(bf16)
        if stages > 1:
            @pl.when(jnp.logical_and(micro >= 2, stage < last))
            def _():
                hidden_copy(micro - 2, ahead).wait_send()
        slot = lax.rem(micro, 2)
        h_send[slot] = (work[...] + dot(active[micro], w_down_ref[...], 1, 0)).astype(bf16)
        if stages > 1:
            @pl.when(stage < last)
            def _():
                hidden_copy(micro, ahead).start()
        save.wait()

    def head(micro):
        unit, scale = unit_rows(h_send[lax.rem(micro, 2)].astype(f32))
        rounded = unit.astype(bf16)
        logits = dot(table_parts[0], rounded, 1, 1)
        logits = jnp.where(letters < vocab, logits, -jnp.inf)
        largest = jnp.max(logits, axis=0, keepdims=True)
        powers = jnp.exp(logits - largest)
        total = jnp.sum(powers, axis=0, keepdims=True)
        stamp = stamp_ref[micro]
        weight = jnp.where(
            order_ref[micro] < stamp, 0.0, 1.0 / (length - stamp).astype(f32)
        )
        target = (letters == token_ref[micro]).astype(f32)
        g_logits = (weight * (powers / total - target)).astype(bf16)
        table_sum[...] += dot(g_logits, rounded, 1, 0)
        g_unit = dot(g_logits, table_parts[0], 0, 0)
        g_in[micro] = unit_back(g_unit, unit, scale).astype(bf16)

    def backward(micro):
        @pl.when(stage == last)
        def _():
            head(micro)

        if stages > 1:
            @pl.when(stage < last)
            def _():
                gradient_copy(micro, ahead).wait_recv()
        load = pltpu.make_async_copy(stash_ref.at[micro], attention_in, stash_sem)
        load.start()
        g_out = g_in[micro]
        for at in range(0, hidden_units, FF_CHUNK):
            g_active = dot(g_out, w_down_ref[at : at + FF_CHUNK, :], 1, 1)
            slope[micro, :, at : at + FF_CHUNK] = (
                g_active * slope[micro, :, at : at + FF_CHUNK].astype(f32)
            ).astype(bf16)
        g_normed = dot(slope[micro], w_in_ref[...], 1, 1)
        unit, scale = unit_rows(middle[micro, 0].astype(f32) + middle[micro, 1].astype(f32))
        middle[micro, 0] = (unit * gain_ref[1:2, :] + bias_ref[1:2, :]).astype(bf16)
        norm_sums[1] += fold_rows(g_normed * unit)
        norm_sums[3] += fold_rows(g_normed)
        g_middle = g_out.astype(f32) + unit_back(g_normed * gain_ref[1:2, :], unit, scale)
        g_attended = g_middle.astype(bf16)
        middle[micro, 1] = g_attended
        g_mixed = dot(g_attended, w_out_ref[...], 1, 1).astype(bf16)
        load_hidden(micro)
        load.wait()
        for pair in range(HEADS // 2):
            at = pair * pair_width
            query = packed[micro, :, at : at + pair_width]
            key = packed[micro, :, width + at : width + at + pair_width]
            value = packed[micro, :, 2 * width + at : 2 * width + at + pair_width]
            g_pair = g_mixed[:, at : at + pair_width]
            found = []
            for side, part in enumerate(halves(g_pair)):
                low = attention_in[2 * pair + side]
                attention = low.astype(f32)
                g_attention = dot(part, value, 1, 1)
                inner = jnp.sum(attention * g_attention, axis=-1, keepdims=True)
                g_scores = (attention * (g_attention - inner)).astype(bf16)
                found.append(
                    (
                        dot(g_scores, key, 1, 0),
                        dot(g_scores, query, 0, 0),
                        dot(low, g_pair, 0, 0),
                    )
                )
            for member, factor in enumerate((score_scale, score_scale, None)):
                joined = jnp.where(lower, found[0][member], found[1][member])
                if factor is not None:
                    joined = joined * factor
                packed[
                    micro, :, member * width + at : member * width + at + pair_width
                ] = joined.astype(bf16)
        g_normed = dot(packed[micro], w_qkv_ref[...], 1, 1)
        unit, scale = unit_rows(work[...])
        h_in[micro] = (unit * gain_ref[0:1, :] + bias_ref[0:1, :]).astype(bf16)
        norm_sums[0] += fold_rows(g_normed * unit)
        norm_sums[2] += fold_rows(g_normed)
        g_hidden = g_middle + unit_back(g_normed * gain_ref[0:1, :], unit, scale)

        @pl.when(stage == 0)
        def _():
            hot = shown_rows(micro)
            high = g_hidden.astype(bf16)
            low = (g_hidden - high.astype(f32)).astype(bf16)
            table_sum[...] += EMBED_GAIN * (dot(hot, high, 1, 0) + dot(hot, low, 1, 0))

        if stages > 1:
            @pl.when(stage > 0)
            def _():
                @pl.when(micro >= 2)
                def _():
                    gradient_copy(micro - 2, behind).wait_send()

                g_send[lax.rem(micro, 2)] = g_hidden.astype(bf16)
                gradient_copy(micro, behind).start()

    def weights(micro):
        d_down_ref[...] += dot(active[micro], g_in[micro], 0, 0)
        d_in_ref[...] += dot(middle[micro, 0], slope[micro], 0, 0)
        d_out_ref[...] += dot(mixed[micro], middle[micro, 1], 0, 0)
        d_qkv_ref[...] += dot(h_in[micro], packed[micro], 0, 0)

    steps = max(2 * last + micro_count, last + 2 * micro_count)

    def step(index, carry):
        f_micro = index - stage
        b_micro = index - (2 * last - stage)
        w_micro = index - jnp.maximum(stage + micro_count, 2 * last - stage)

        @pl.when(jnp.logical_and(f_micro >= 0, f_micro < micro_count))
        def _():
            forward(f_micro)

        @pl.when(jnp.logical_and(b_micro >= 0, b_micro < micro_count))
        def _():
            backward(b_micro)

        @pl.when(jnp.logical_and(w_micro >= 0, w_micro < micro_count))
        def _():
            weights(w_micro)

        return carry

    lax.fori_loop(0, steps, step, 0)

    if stages > 1:
        for micro in range(max(micro_count - 2, 0), micro_count):
            @pl.when(stage < last)
            def _():
                hidden_copy(micro, ahead).wait_send()

            @pl.when(stage > 0)
            def _():
                gradient_copy(micro, behind).wait_send()

    d_table_ref[...] = table_sum[...]
    for member in range(2):
        d_gain_ref[member : member + 1, :] = jnp.sum(norm_sums[member], axis=0, keepdims=True)
        d_bias_ref[member : member + 1, :] = jnp.sum(norm_sums[2 + member], axis=0, keepdims=True)


def run_pipeline(stages, token_ids, order, timesteps, table, gathered):
    gain, bias, w_qkv, w_out, w_in, w_down = gathered
    micro_count, _, length = token_ids.shape
    width = table.shape[1]
    hidden_units = w_in.shape[1]
    rows = -(-table.shape[0] // 32) * 32
    bf16, f32 = jnp.bfloat16, jnp.float32
    vmem = pl.BlockSpec(memory_space=pltpu.VMEM)
    outs = (
        jax.ShapeDtypeStruct((rows, width), f32),
        jax.ShapeDtypeStruct((2, width), f32),
        jax.ShapeDtypeStruct((2, width), f32),
        jax.ShapeDtypeStruct(w_qkv.shape, f32),
        jax.ShapeDtypeStruct(w_out.shape, f32),
        jax.ShapeDtypeStruct(w_in.shape, f32),
        jax.ShapeDtypeStruct(w_down.shape, f32),
        jax.ShapeDtypeStruct((micro_count, HEADS, length, length), bf16),
    )
    rows_shape = (micro_count, length, width)
    return pl.pallas_call(
        functools.partial(pipeline_kernel, stages),
        out_shape=outs,
        in_specs=[vmem] * 10,
        out_specs=[vmem] * 7 + [pl.BlockSpec(memory_space=pl.ANY)],
        scratch_shapes=[
            pltpu.VMEM(rows_shape, bf16),
            pltpu.VMEM(rows_shape, bf16),
            pltpu.VMEM((2, length, width), bf16),
            pltpu.VMEM((2, length, width), bf16),
            pltpu.VMEM((micro_count, length, 3 * width), bf16),
            pltpu.VMEM(rows_shape, bf16),
            pltpu.VMEM((micro_count, 2, length, width), bf16),
            pltpu.VMEM((micro_count, length, hidden_units), bf16),
            pltpu.VMEM((micro_count, length, hidden_units), bf16),
            pltpu.VMEM((HEADS, length, length), bf16),
            pltpu.VMEM((HEADS, length, length), bf16),
            pltpu.VMEM((length, width), f32),
            pltpu.VMEM((3, rows, width), bf16),
            pltpu.VMEM((4, 8, width), f32),
            pltpu.VMEM((rows, width), f32),
            pltpu.SemaphoreType.DMA((2,)),
            pltpu.SemaphoreType.DMA((micro_count,)),
            pltpu.SemaphoreType.DMA((2,)),
            pltpu.SemaphoreType.DMA((micro_count,)),
            pltpu.SemaphoreType.DMA,
        ],
        compiler_params=pltpu.CompilerParams(
            vmem_limit_bytes=63 << 20,
            **({"collective_id": 0, "has_side_effects": True} if stages > 1 else {}),
        ),
    )(token_ids, order, timesteps, table, gain, bias, w_qkv, w_out, w_in, w_down)


def body(token_ids, order, timesteps, table, norm_gain, norm_bias, w_qkv, w_out, w_in, w_down):
    stages = lax.axis_size("section")
    vocab = table.shape[0]
    bf16, f32 = jnp.bfloat16, jnp.float32
    gathered = (
        lax.all_gather(norm_gain[0].astype(bf16), "dp", axis=1, tiled=True).astype(f32),
        lax.all_gather(norm_bias[0].astype(bf16), "dp", axis=1, tiled=True).astype(f32),
        lax.all_gather(w_qkv[0].astype(bf16), "dp", axis=0, tiled=True),
        lax.all_gather(w_out[0].astype(bf16), "dp", axis=0, tiled=True),
        lax.all_gather(w_in[0].astype(bf16), "dp", axis=0, tiled=True),
        lax.all_gather(w_down[0].astype(bf16), "dp", axis=0, tiled=True),
    )
    sums = run_pipeline(stages, token_ids, order, timesteps[:, :, None], table, gathered)
    shared = [
        lax.psum_scatter(value.astype(bf16), "dp", scatter_dimension=axis, tiled=True)
        .astype(f32)[None]
        for value, axis in zip(sums[1:7], (1, 1, 0, 0, 0, 0))
    ]
    table_part = lax.psum_scatter(
        sums[0][:vocab].astype(bf16), "section", scatter_dimension=1, tiled=True
    ).astype(f32)
    return (lax.psum(table_part, "dp"), *shared)


def solution(mesh):
    in_specs = (
        P(None, "dp", None),
        P(None, "dp", None),
        P(None, "dp"),
        P(),
        P("section", None, "dp"),
        P("section", None, "dp"),
        P("section", "dp", None),
        P("section", "dp", None),
        P("section", "dp", None),
        P("section", "dp", None),
    )
    out_specs = (
        P(None, "section"),
        P("section", None, "dp"),
        P("section", None, "dp"),
        P("section", "dp", None),
        P("section", "dp", None),
        P("section", "dp", None),
        P("section", "dp", None),
    )
    return jax.shard_map(body, mesh=mesh, in_specs=in_specs, out_specs=out_specs, check_vma=False)
```

```python
import functools
import math

import jax
import jax.numpy as jnp
from jax import lax
from jax.experimental import pallas as pl
from jax.experimental.pallas import tpu as pltpu
from jax.sharding import PartitionSpec as P

HEADS = 8
EPSILON = 1e-05
EMBED_GAIN = 16.0
FF_CHUNK = 512
NORM_ROWS = 8
MESH = pl.DeviceIdType.MESH


def dot(left, right, left_dim, right_dim):
    return lax.dot_general(
        left, right, (((left_dim,), (right_dim,)), ((), ())), preferred_element_type=jnp.float32
    )


def unit_rows(values):
    average = jnp.mean(values, axis=-1, keepdims=True)
    centered = values - average
    variance = jnp.mean(centered * centered, axis=-1, keepdims=True)
    scale = lax.rsqrt(variance + EPSILON)
    return centered * scale, scale


def unit_back(gradient, unit, scale):
    first = jnp.mean(gradient, axis=-1, keepdims=True)
    second = jnp.mean(gradient * unit, axis=-1, keepdims=True)
    return scale * (gradient - first - unit * second)


def fold_rows(values):
    rows, columns = values.shape
    return jnp.sum(values.reshape(rows // 8, 8, columns), axis=0)


def chip_of(place, row, per_plane):
    return row * per_plane + lax.rem(place - lax.rem(row, per_plane) + per_plane, per_plane)


def start_copy(src, dst, send_sem, recv_sem, device, here):
    section, plane = device
    same = jnp.logical_and(section == here[0], plane == here[1])

    @pl.when(same)
    def _():
        pltpu.make_async_copy(src, dst, recv_sem).start()

    @pl.when(jnp.logical_not(same))
    def _():
        remote_copy(src, dst, send_sem, recv_sem, device).start()


def wait_sent(src, dst, send_sem, recv_sem, device, here):
    section, plane = device
    same = jnp.logical_and(section == here[0], plane == here[1])

    @pl.when(jnp.logical_not(same))
    def _():
        remote_copy(src, dst, send_sem, recv_sem, device).wait_send()


def remote_copy(src, dst, send_sem, recv_sem, device):
    return pltpu.make_async_remote_copy(
        src_ref=src,
        dst_ref=dst,
        send_sem=send_sem,
        recv_sem=recv_sem,
        device_id={"section": device[0], "dp": device[1]},
        device_id_type=MESH,
    )


def pipeline_kernel(
    stages,
    planes,
    token_in_ref,
    table_ref,
    norm_shard,
    qkv_shard,
    out_shard,
    in_shard,
    down_shard,
    d_table_ref,
    norm_total,
    qkv_total,
    out_total,
    in_total,
    down_total,
    stash_ref,
    token_ref,
    h_in,
    g_in,
    h_send,
    g_send,
    packed,
    mixed,
    middle,
    active,
    slope,
    attention_out,
    attention_in,
    work,
    table_parts,
    norm_sums,
    table_sum,
    norm_slots,
    norm_full,
    w_qkv_ref,
    w_out_ref,
    w_in_ref,
    w_down_ref,
    gain_ref,
    bias_ref,
    d_norm_ref,
    d_qkv_ref,
    d_out_ref,
    d_in_ref,
    d_down_ref,
    h_send_sem,
    h_recv_sem,
    g_send_sem,
    g_recv_sem,
    stash_sem,
    token_send_sem,
    token_recv_sem,
    load_sem,
    spread_send,
    spread_recv,
    plane_send,
    plane_recv,
    peer_send,
    peer_recv,
    core_send,
    core_recv,
    core_free,
    peer_free,
    total_send,
    total_recv,
):
    micro_count, _, length = token_ref.shape
    vocab, width = table_ref.shape
    hidden_units = w_in_ref.shape[1]
    head_size = width // HEADS
    score_scale = 1.0 / math.sqrt(head_size)
    pair_width = 2 * head_size
    bf16, f32 = jnp.bfloat16, jnp.float32

    per_plane, rows = stages // planes, planes // 2
    section, plane = lax.axis_index("section"), lax.axis_index("dp")
    here = (section, plane)
    chip, core = lax.div(section, 2), lax.rem(section, 2)
    row = lax.div(chip, per_plane)
    place = lax.rem(lax.rem(chip, per_plane) + row, per_plane)
    odd = lax.rem(plane, 2)
    turn = jnp.where(odd == 0, place, per_plane - 1 - place)
    stage = plane * per_plane + turn
    last = stages - 1
    lane_row = lax.rem(row - lax.rem(place, rows) * core + rows, rows)
    lane_index = 2 * lane_row + core

    def next_device():
        step = jnp.where(odd == 0, 1, -1)
        near_place = place + step
        near_row = lax.rem(row + core * step + rows, rows)
        near = 2 * chip_of(near_place + per_plane, near_row, per_plane) + core
        stays = turn < per_plane - 1
        return jnp.where(stays, near, section), jnp.where(stays, plane, plane + 1)

    def previous_device():
        step = jnp.where(odd == 0, -1, 1)
        near_place = place + step
        near_row = lax.rem(row + core * step + rows, rows)
        near = 2 * chip_of(near_place + per_plane, near_row, per_plane) + core
        stays = turn > 0
        return jnp.where(stays, near, section), jnp.where(stays, plane, plane - 1)

    ahead, behind = next_device(), previous_device()
    partner = (section + 1 - 2 * core, plane)

    def layer_device(layer, at_row, at_core):
        at_plane, at_turn = lax.div(layer, per_plane), lax.rem(layer, per_plane)
        at_place = jnp.where(lax.rem(at_plane, 2) == 0, at_turn, per_plane - 1 - at_turn)
        return 2 * chip_of(at_place, at_row, per_plane) + at_core, at_plane

    def layer_here(at_plane):
        at_turn = jnp.where(at_plane % 2 == 0, place, per_plane - 1 - place)
        return at_plane * per_plane + at_turn

    def peer(at_row):
        return layer_device(stage, at_row, core)

    home_plane = lax.div(section, per_plane)
    carries = lax.rem(plane, 2) == core

    barrier = pltpu.get_barrier_semaphore()
    greetings = []

    def greet(device, wanted=True):
        same = jnp.logical_and(device[0] == section, device[1] == plane)
        wanted = jnp.logical_and(wanted, jnp.logical_not(same))
        greetings.append(jnp.where(wanted, 1, 0))

        @pl.when(wanted)
        def _():
            pl.semaphore_signal(
                barrier,
                inc=1,
                device_id={"section": device[0], "dp": device[1]},
                device_id_type=MESH,
            )

    for other in range(planes):
        greet((section, other))
        greet((layer_here(other), plane), carries)
    for at_row in range(rows):
        owner = layer_device(section, at_row, lax.rem(plane, 2))
        greet((owner[0], plane))
        greet(owner)
        greet((stage, 2 * at_row + core))
        greet(peer(at_row))
    greet(partner)
    greet(ahead, stage < last)
    greet(behind, stage > 0)
    pl.semaphore_wait(barrier, sum(greetings))

    matrices = (
        (w_qkv_ref, d_qkv_ref, qkv_shard, qkv_total, packed),
        (w_out_ref, d_out_ref, out_shard, out_total, mixed),
        (w_in_ref, d_in_ref, in_shard, in_total, active),
        (w_down_ref, d_down_ref, down_shard, down_total, middle),
        (norm_full, d_norm_ref, norm_shard, norm_total, norm_slots),
    )
    count = len(matrices)
    norms = count - 1
    heights = [matrix[0].shape[0] // (planes * rows) for matrix in matrices]

    def slot(matrix, index):
        buffer, height = matrices[matrix][4], heights[matrix]
        per_block = buffer.shape[1] // height
        block, inside = index // per_block, index % per_block
        if not isinstance(inside, int):
            inside = pl.multiple_of(inside * height, height)
        else:
            inside = inside * height
        return buffer.at[block, pl.ds(inside, height)]

    def piece(matrix, quarter, at_row):
        height = heights[matrix]
        return pl.ds(pl.multiple_of((quarter * rows + at_row) * height, height), height)

    gives_tokens = jnp.logical_and(place == 0, lane_index == plane)
    takes_tokens = jnp.logical_or(stage == 0, stage == last)

    def token_copy(index, target):
        return (
            token_in_ref,
            token_ref,
            token_send_sem.at[index],
            token_recv_sem,
            (section, target),
        )

    @pl.when(gives_tokens)
    def _():
        for index, target in enumerate((0, planes - 1)):
            start_copy(*token_copy(index, target), here)

    loads = []
    for matrix in range(norms):
        shard, landing = matrices[matrix][2], matrices[matrix][1]
        loads.append(
            pltpu.make_async_copy(
                shard.at[0], landing.at[pl.ds(0, shard.shape[1])], load_sem.at[matrix]
            )
        )
        loads[-1].start()

    def spread_args(matrix, at_row):
        target, _ = layer_device(section, at_row, lax.rem(plane, 2))
        if matrix == norms:
            source = norm_shard.at[pl.ds(at_row * NORM_ROWS, NORM_ROWS)]
        else:
            source = slot(matrix, planes + at_row)
        return (
            source,
            slot(matrix, home_plane),
            spread_send.at[matrix, at_row],
            spread_recv.at[matrix, home_plane],
            (target, plane),
        )

    def plane_args(matrix, to_plane, from_plane):
        return (
            slot(matrix, to_plane),
            matrices[matrix][0].at[piece(matrix, from_plane, row)],
            plane_send.at[matrix, to_plane],
            plane_recv.at[matrix, lax.div(from_plane, 2)],
            (section, to_plane),
        )

    def peer_args(matrix, quarter_pair, from_row, to_row):
        part = matrices[matrix][0].at[piece(matrix, 2 * quarter_pair + core, from_row)]
        return (
            part,
            part,
            peer_send.at[matrix, quarter_pair, to_row],
            peer_recv.at[matrix, quarter_pair, from_row],
            peer(to_row),
        )

    def core_args(matrix, quarter_pair, at_row, from_core):
        part = matrices[matrix][0].at[piece(matrix, 2 * quarter_pair + from_core, at_row)]
        return (
            part,
            part,
            core_send.at[matrix, quarter_pair, at_row],
            core_recv.at[matrix, quarter_pair, at_row],
            partner,
        )

    def spread(matrix):
        if matrix != norms:
            loads[matrix].wait()
            for at_row in range(rows):
                height = heights[matrix]
                source = matrices[matrix][1][at_row * height : (at_row + 1) * height, :]
                slot(matrix, planes + at_row)[...] = source.astype(bf16)
        for at_row in range(rows):
            start_copy(*spread_args(matrix, at_row), here)

    def along_planes(matrix):
        @pl.when(carries)
        def _():
            for to_plane in range(planes):
                remote_copy(
                    slot(matrix, to_plane),
                    slot(matrix, to_plane),
                    spread_send.at[matrix, 0],
                    spread_recv.at[matrix, to_plane],
                    partner,
                ).wait_recv()
                start_copy(*plane_args(matrix, to_plane, plane), here)

    def between_peers(matrix):
        for pair in range(rows):
            remote_copy(*plane_args(matrix, 0, 2 * pair + core)).wait_recv()
            for to_row in range(rows):
                @pl.when(to_row != row)
                def _():
                    remote_copy(*peer_args(matrix, pair, row, to_row)).start()

            remote_copy(*core_args(matrix, pair, row, core)).start()

    def between_cores(matrix):
        for pair in range(rows):
            for from_row in range(rows):
                @pl.when(from_row != row)
                def _():
                    remote_copy(*peer_args(matrix, pair, from_row, from_row)).wait_recv()
                    remote_copy(*core_args(matrix, pair, from_row, core)).start()

    def gathered(matrix):
        for pair in range(rows):
            for at_row in range(rows):
                remote_copy(*core_args(matrix, pair, at_row, 1 - core)).wait_recv()

    def gather_sent(matrix):
        for at_row in range(rows):
            wait_sent(*spread_args(matrix, at_row), here)

        @pl.when(carries)
        def _():
            for to_plane in range(planes):
                wait_sent(*plane_args(matrix, to_plane, plane), here)

        for pair in range(rows):
            for at_row in range(rows):
                @pl.when(at_row != row)
                def _():
                    remote_copy(*peer_args(matrix, pair, row, at_row)).wait_send()

                remote_copy(*core_args(matrix, pair, at_row, core)).wait_send()

    steps_of_gather = (spread, along_planes, between_peers, between_cores, gathered)
    order = (norms, 0, 1, 2, 3)
    for turn_at in range(count + len(steps_of_gather) - 1):
        for depth, action in enumerate(steps_of_gather):
            if 0 <= turn_at - depth < count:
                action(order[turn_at - depth])
    for matrix in range(count):
        gather_sent(matrix)

    @pl.when(takes_tokens)
    def _():
        remote_copy(*token_copy(0, 0)).wait_recv()

    @pl.when(gives_tokens)
    def _():
        for index, target in enumerate((0, planes - 1)):
            wait_sent(*token_copy(index, target), here)

    for kind, ref in enumerate((gain_ref, bias_ref)):
        total = jnp.zeros((NORM_ROWS, width), f32)
        for quarter in range(planes):
            start = (quarter * rows + kind) * NORM_ROWS
            total = total + norm_full[start : start + NORM_ROWS, :]
        ref[...] = total.astype(bf16).astype(f32)

    table_rows = table_parts.shape[1]
    work[:table_rows, :] = jnp.zeros((table_rows, width), f32)
    work[:vocab, :] = table_ref[...]
    rest = work[:table_rows, :]
    for part in range(3):
        rounded = rest.astype(bf16)
        table_parts[part] = rounded
        rest = rest - rounded.astype(f32)
    d_qkv_ref[...] = jnp.zeros_like(d_qkv_ref)
    d_out_ref[...] = jnp.zeros_like(d_out_ref)
    d_in_ref[...] = jnp.zeros_like(d_in_ref)
    d_down_ref[...] = jnp.zeros_like(d_down_ref)
    norm_sums[...] = jnp.zeros_like(norm_sums)
    table_sum[...] = jnp.zeros_like(table_sum)

    letters = lax.broadcasted_iota(jnp.int32, (table_rows, length), 0)
    lane = lax.broadcasted_iota(jnp.int32, (length, pair_width), 1)
    lower = lane < head_size

    def shown_rows(micro):
        rows_of = token_ref[micro]
        visible = rows_of[1:2] < rows_of[2:3]
        shown = jnp.where(visible, rows_of[0:1], vocab - 1)
        return (letters == shown).astype(bf16)

    def halves(pair):
        zero = jnp.zeros_like(pair)
        return jnp.where(lower, pair, zero), jnp.where(lower, zero, pair)

    def load_hidden(micro):
        @pl.when(stage == 0)
        def _():
            hot = shown_rows(micro)
            total = dot(hot, table_parts[2], 0, 0)
            total = total + dot(hot, table_parts[1], 0, 0)
            total = total + dot(hot, table_parts[0], 0, 0)
            work[...] = total * EMBED_GAIN

        @pl.when(stage > 0)
        def _():
            work[...] = h_in[micro].astype(f32)

    def hidden_copy(micro, target):
        slot = lax.rem(micro, 2)
        return pltpu.make_async_remote_copy(
            src_ref=h_send.at[slot],
            dst_ref=h_in.at[micro],
            send_sem=h_send_sem.at[slot],
            recv_sem=h_recv_sem.at[micro],
            device_id={"section": target[0], "dp": target[1]},
            device_id_type=MESH,
        )

    def gradient_copy(micro, target):
        slot = lax.rem(micro, 2)
        return pltpu.make_async_remote_copy(
            src_ref=g_send.at[slot],
            dst_ref=g_in.at[micro],
            send_sem=g_send_sem.at[slot],
            recv_sem=g_recv_sem.at[micro],
            device_id={"section": target[0], "dp": target[1]},
            device_id_type=MESH,
        )

    def forward(micro):
        if stages > 1:
            @pl.when(stage > 0)
            def _():
                hidden_copy(micro, behind).wait_recv()
        load_hidden(micro)
        hidden = work[...]
        unit, _ = unit_rows(hidden)
        normed = (unit * gain_ref[0:1, :] + bias_ref[0:1, :]).astype(bf16)
        packed[micro] = dot(normed, w_qkv_ref[...], 1, 0).astype(bf16)
        for pair in range(HEADS // 2):
            at = pair * pair_width
            query = packed[micro, :, at : at + pair_width] * jnp.asarray(score_scale, bf16)
            key = packed[micro, :, width + at : width + at + pair_width]
            value = packed[micro, :, 2 * width + at : 2 * width + at + pair_width]
            found = []
            for side, part in enumerate(halves(query)):
                scores = dot(part, key, 1, 1)
                largest = jnp.max(scores, axis=-1, keepdims=True)
                powers = jnp.exp(scores - largest)
                total = jnp.sum(powers, axis=-1, keepdims=True)
                attention = (powers * (1.0 / total)).astype(bf16)
                attention_out[2 * pair + side] = attention
                found.append(dot(attention, value, 1, 0))
            mixed[micro, :, at : at + pair_width] = jnp.where(lower, found[0], found[1]).astype(
                bf16
            )
        save = pltpu.make_async_copy(attention_out, stash_ref.at[micro], stash_sem)
        save.start()
        between = hidden + dot(mixed[micro], w_out_ref[...], 1, 0)
        high = between.astype(bf16)
        middle[2 * micro + 0] = high
        middle[2 * micro + 1] = (between - high.astype(f32)).astype(bf16)
        work[...] = between
        unit, _ = unit_rows(between)
        normed_two = (unit * gain_ref[1:2, :] + bias_ref[1:2, :]).astype(bf16)
        for at in range(0, hidden_units, FF_CHUNK):
            lifted = dot(normed_two, w_in_ref[:, at : at + FF_CHUNK], 1, 0)
            square = lifted * lifted
            inner = math.sqrt(2.0 / math.pi) * lifted * (1.0 + 0.044715 * square)
            bend = jnp.tanh(inner)
            half = 0.5 * (1.0 + bend)
            active[micro, :, at : at + FF_CHUNK] = (lifted * half).astype(bf16)
            steep = math.sqrt(2.0 / math.pi) * (1.0 + 3.0 * 0.044715 * square)
            slope[micro, :, at : at + FF_CHUNK] = (
                half + 0.5 * lifted * (1.0 - bend * bend) * steep
            ).astype(bf16)
        if stages > 1:
            @pl.when(jnp.logical_and(micro >= 2, stage < last))
            def _():
                hidden_copy(micro - 2, ahead).wait_send()
        slot = lax.rem(micro, 2)
        h_send[slot] = (work[...] + dot(active[micro], w_down_ref[...], 1, 0)).astype(bf16)
        if stages > 1:
            @pl.when(stage < last)
            def _():
                hidden_copy(micro, ahead).start()
        save.wait()

    def head(micro):
        unit, scale = unit_rows(h_send[lax.rem(micro, 2)].astype(f32))
        rounded = unit.astype(bf16)
        logits = dot(table_parts[0], rounded, 1, 1)
        logits = jnp.where(letters < vocab, logits, -jnp.inf)
        largest = jnp.max(logits, axis=0, keepdims=True)
        powers = jnp.exp(logits - largest)
        total = jnp.sum(powers, axis=0, keepdims=True)
        rows_of = token_ref[micro]
        stamp = rows_of[2:3]
        weight = jnp.where(rows_of[1:2] < stamp, 0.0, 1.0 / (length - stamp).astype(f32))
        target = (letters == rows_of[0:1]).astype(f32)
        g_logits = (weight * (powers / total - target)).astype(bf16)
        table_sum[...] += dot(g_logits, rounded, 1, 0)
        g_unit = dot(g_logits, table_parts[0], 0, 0)
        g_in[micro] = unit_back(g_unit, unit, scale).astype(bf16)

    def backward(micro):
        @pl.when(stage == last)
        def _():
            head(micro)

        if stages > 1:
            @pl.when(stage < last)
            def _():
                gradient_copy(micro, ahead).wait_recv()
        load = pltpu.make_async_copy(stash_ref.at[micro], attention_in, stash_sem)
        load.start()
        g_out = g_in[micro]
        for at in range(0, hidden_units, FF_CHUNK):
            g_active = dot(g_out, w_down_ref[at : at + FF_CHUNK, :], 1, 1)
            slope[micro, :, at : at + FF_CHUNK] = (
                g_active * slope[micro, :, at : at + FF_CHUNK].astype(f32)
            ).astype(bf16)
        g_normed = dot(slope[micro], w_in_ref[...], 1, 1)
        unit, scale = unit_rows(middle[2 * micro + 0].astype(f32) + middle[2 * micro + 1].astype(f32))
        middle[2 * micro + 0] = (unit * gain_ref[1:2, :] + bias_ref[1:2, :]).astype(bf16)
        norm_sums[1] += fold_rows(g_normed * unit)
        norm_sums[3] += fold_rows(g_normed)
        g_middle = g_out.astype(f32) + unit_back(g_normed * gain_ref[1:2, :], unit, scale)
        g_attended = g_middle.astype(bf16)
        middle[2 * micro + 1] = g_attended
        g_mixed = dot(g_attended, w_out_ref[...], 1, 1).astype(bf16)
        load_hidden(micro)
        load.wait()
        for pair in range(HEADS // 2):
            at = pair * pair_width
            query = packed[micro, :, at : at + pair_width]
            key = packed[micro, :, width + at : width + at + pair_width]
            value = packed[micro, :, 2 * width + at : 2 * width + at + pair_width]
            g_pair = g_mixed[:, at : at + pair_width]
            found = []
            for side, part in enumerate(halves(g_pair)):
                low = attention_in[2 * pair + side]
                attention = low.astype(f32)
                g_attention = dot(part, value, 1, 1)
                inner = jnp.sum(attention * g_attention, axis=-1, keepdims=True)
                g_scores = (attention * (g_attention - inner)).astype(bf16)
                found.append(
                    (
                        dot(g_scores, key, 1, 0),
                        dot(g_scores, query, 0, 0),
                        dot(low, g_pair, 0, 0),
                    )
                )
            for member, factor in enumerate((score_scale, score_scale, None)):
                joined = jnp.where(lower, found[0][member], found[1][member])
                if factor is not None:
                    joined = joined * factor
                packed[
                    micro, :, member * width + at : member * width + at + pair_width
                ] = joined.astype(bf16)
        g_normed = dot(packed[micro], w_qkv_ref[...], 1, 1)
        unit, scale = unit_rows(work[...])
        h_in[micro] = (unit * gain_ref[0:1, :] + bias_ref[0:1, :]).astype(bf16)
        norm_sums[0] += fold_rows(g_normed * unit)
        norm_sums[2] += fold_rows(g_normed)
        g_hidden = g_middle + unit_back(g_normed * gain_ref[0:1, :], unit, scale)

        @pl.when(stage == 0)
        def _():
            hot = shown_rows(micro)
            high = g_hidden.astype(bf16)
            low = (g_hidden - high.astype(f32)).astype(bf16)
            table_sum[...] += EMBED_GAIN * (dot(hot, high, 1, 0) + dot(hot, low, 1, 0))

        if stages > 1:
            @pl.when(stage > 0)
            def _():
                @pl.when(micro >= 2)
                def _():
                    gradient_copy(micro - 2, behind).wait_send()

                g_send[lax.rem(micro, 2)] = g_hidden.astype(bf16)
                gradient_copy(micro, behind).start()

    def weights(micro):
        d_down_ref[...] += dot(active[micro], g_in[micro], 0, 0)
        d_in_ref[...] += dot(middle[2 * micro + 0], slope[micro], 0, 0)
        d_out_ref[...] += dot(mixed[micro], middle[2 * micro + 1], 0, 0)
        d_qkv_ref[...] += dot(h_in[micro], packed[micro], 0, 0)

    steps = max(2 * last + micro_count, last + 2 * micro_count)

    def step(index, carry):
        f_micro = index - stage
        b_micro = index - (2 * last - stage)
        w_micro = index - jnp.maximum(stage + micro_count, 2 * last - stage)

        @pl.when(jnp.logical_and(f_micro >= 0, f_micro < micro_count))
        def _():
            forward(f_micro)

        @pl.when(jnp.logical_and(b_micro >= 0, b_micro < micro_count))
        def _():
            backward(b_micro)

        @pl.when(jnp.logical_and(w_micro >= 0, w_micro < micro_count))
        def _():
            weights(w_micro)

        return carry

    lax.fori_loop(0, steps, step, 0)

    if stages > 1:
        for micro in range(max(micro_count - 2, 0), micro_count):
            @pl.when(stage < last)
            def _():
                hidden_copy(micro, ahead).wait_send()

            @pl.when(stage > 0)
            def _():
                gradient_copy(micro, behind).wait_send()

    d_table_ref[...] = table_sum[...]
    for kind in range(2):
        totals = [
            jnp.sum(norm_sums[2 * kind + member], axis=0, keepdims=True) for member in range(2)
        ]
        block = jnp.concatenate(totals + [jnp.zeros((NORM_ROWS - 2, width), f32)], axis=0)
        for quarter in range(planes):
            start = (quarter * rows + kind) * NORM_ROWS
            d_norm_ref[start : start + NORM_ROWS, :] = block

    pl.semaphore_signal(
        core_free, inc=1, device_id={"section": partner[0], "dp": partner[1]}, device_id_type=MESH
    )
    for at_row in range(rows):
        @pl.when(at_row != row)
        def _():
            far = peer(at_row)
            pl.semaphore_signal(
                peer_free, inc=1, device_id={"section": far[0], "dp": far[1]}, device_id_type=MESH
            )

    def core_sum_args(matrix, pair, at_row):
        index = pair * rows + at_row
        return (
            slot(matrix, index),
            slot(matrix, rows * rows + index),
            core_send.at[matrix, pair, at_row],
            core_recv.at[matrix, pair, at_row],
            partner,
        )

    def peer_sum_args(matrix, pair, from_row, to_row):
        return (
            slot(matrix, 2 * rows * rows + pair * rows + to_row),
            slot(matrix, 3 * rows * rows + pair * rows + from_row),
            peer_send.at[matrix, pair, to_row],
            peer_recv.at[matrix, pair, from_row],
            peer(to_row),
        )

    def total_args(matrix, pair):
        height = heights[matrix]
        return (
            slot(matrix, 2 * rows * rows + pair * rows + row),
            matrices[matrix][3].at[pl.ds(pl.multiple_of(row * height, height), height)],
            total_send.at[matrix, pair],
            total_recv.at[matrix, row],
            (stage, 2 * pair + core),
        )

    def give_core(matrix):
        for pair in range(rows):
            for at_row in range(rows):
                args = core_sum_args(matrix, pair, at_row)
                part = matrices[matrix][1][piece(matrix, 2 * pair + 1 - core, at_row), :]
                args[0][...] = part.astype(args[0].dtype)
                remote_copy(*args).start()

    def give_peers(matrix):
        for pair in range(rows):
            for at_row in range(rows):
                remote_copy(*core_sum_args(matrix, pair, at_row)).wait_recv()
                landed = slot(matrix, rows * rows + pair * rows + at_row)
                part = matrices[matrix][1].at[piece(matrix, 2 * pair + core, at_row)]
                total = part[...] + landed[...].astype(f32)

                @pl.when(at_row != row)
                def _():
                    args = peer_sum_args(matrix, pair, row, at_row)
                    args[0][...] = total.astype(args[0].dtype)
                    remote_copy(*args).start()

                @pl.when(at_row == row)
                def _():
                    part[...] = total

    def give_totals(matrix):
        for pair in range(rows):
            part = matrices[matrix][1].at[piece(matrix, 2 * pair + core, row)]
            for from_row in range(rows):
                @pl.when(from_row != row)
                def _():
                    remote_copy(*peer_sum_args(matrix, pair, from_row, from_row)).wait_recv()
                    landed = slot(matrix, 3 * rows * rows + pair * rows + from_row)
                    part[...] += landed[...].astype(f32)

            args = total_args(matrix, pair)
            args[0][...] = part[...].astype(args[0].dtype)
            start_copy(*args, here)

    def finish(matrix):
        height = heights[matrix]
        for from_row in range(rows):
            part = matrices[matrix][3].at[pl.ds(from_row * height, height)]
            remote_copy(
                part, part, total_send.at[matrix, 0], total_recv.at[matrix, from_row], partner
            ).wait_recv()
        for pair in range(rows):
            for at_row in range(rows):
                remote_copy(*core_sum_args(matrix, pair, at_row)).wait_send()

                @pl.when(at_row != row)
                def _():
                    remote_copy(*peer_sum_args(matrix, pair, row, at_row)).wait_send()

            wait_sent(*total_args(matrix, pair), here)

    order = (norms, 3, 2, 0, 1)
    pl.semaphore_wait(core_free, 1)
    for matrix in order:
        give_core(matrix)
    pl.semaphore_wait(peer_free, rows - 1)
    for position in range(count + 1):
        if position < count:
            give_peers(order[position])
        if position > 0:
            give_totals(order[position - 1])
    for matrix in order:
        finish(matrix)


def run_pipeline(stages, planes, tokens, table, norm_shard, w_qkv, w_out, w_in, w_down):
    micro_count, _, length = tokens.shape
    width = table.shape[1]
    hidden_units = w_in.shape[2]
    rows = planes // 2
    table_rows = -(-table.shape[0] // 32) * 32
    bf16, f32 = jnp.bfloat16, jnp.float32
    vmem = pl.BlockSpec(memory_space=pltpu.VMEM)
    anywhere = pl.BlockSpec(memory_space=pl.ANY)
    shards = (w_qkv, w_out, w_in, w_down)
    full = [(shard.shape[1] * planes, shard.shape[2]) for shard in shards]
    norm_full = (planes * norm_shard.shape[0], width)
    outs = (
        jax.ShapeDtypeStruct((table_rows, width), f32),
        jax.ShapeDtypeStruct(norm_shard.shape, f32),
        *(jax.ShapeDtypeStruct(shard.shape[1:], bf16) for shard in shards),
        jax.ShapeDtypeStruct((micro_count, HEADS, length, length), bf16),
    )
    rows_shape = (micro_count, length, width)
    pieces = (5, rows, rows)
    return pl.pallas_call(
        functools.partial(pipeline_kernel, stages, planes),
        out_shape=outs,
        in_specs=[vmem] * 3 + [anywhere] * 4,
        out_specs=[vmem] * 6 + [anywhere],
        scratch_shapes=[
            pltpu.VMEM(tokens.shape, jnp.int32),
            pltpu.VMEM(rows_shape, bf16),
            pltpu.VMEM(rows_shape, bf16),
            pltpu.VMEM((2, length, width), bf16),
            pltpu.VMEM((2, length, width), bf16),
            pltpu.VMEM((micro_count, length, 3 * width), bf16),
            pltpu.VMEM(rows_shape, bf16),
            pltpu.VMEM((2 * micro_count, length, width), bf16),
            pltpu.VMEM((micro_count, length, hidden_units), bf16),
            pltpu.VMEM((micro_count, length, hidden_units), bf16),
            pltpu.VMEM((HEADS, length, length), bf16),
            pltpu.VMEM((HEADS, length, length), bf16),
            pltpu.VMEM((length, width), f32),
            pltpu.VMEM((3, table_rows, width), bf16),
            pltpu.VMEM((4, 8, width), f32),
            pltpu.VMEM((table_rows, width), f32),
            pltpu.VMEM((4 * rows * rows, NORM_ROWS, width), f32),
            pltpu.VMEM(norm_full, f32),
            *(pltpu.VMEM(shape, bf16) for shape in full),
            pltpu.VMEM((NORM_ROWS, width), f32),
            pltpu.VMEM((NORM_ROWS, width), f32),
            pltpu.VMEM(norm_full, f32),
            *(pltpu.VMEM(shape, f32) for shape in full),
            pltpu.SemaphoreType.DMA((2,)),
            pltpu.SemaphoreType.DMA((micro_count,)),
            pltpu.SemaphoreType.DMA((2,)),
            pltpu.SemaphoreType.DMA((micro_count,)),
            pltpu.SemaphoreType.DMA,
            pltpu.SemaphoreType.DMA((2,)),
            pltpu.SemaphoreType.DMA,
            pltpu.SemaphoreType.DMA((4,)),
            pltpu.SemaphoreType.DMA((5, rows)),
            pltpu.SemaphoreType.DMA((5, planes)),
            pltpu.SemaphoreType.DMA((5, planes)),
            pltpu.SemaphoreType.DMA((5, rows)),
            pltpu.SemaphoreType.DMA(pieces),
            pltpu.SemaphoreType.DMA(pieces),
            pltpu.SemaphoreType.DMA(pieces),
            pltpu.SemaphoreType.DMA(pieces),
            pltpu.SemaphoreType.REGULAR,
            pltpu.SemaphoreType.REGULAR,
            pltpu.SemaphoreType.DMA((5, rows)),
            pltpu.SemaphoreType.DMA((5, rows)),
        ],
        compiler_params=pltpu.CompilerParams(
            vmem_limit_bytes=63 << 20, collective_id=0, has_side_effects=True
        ),
    )(tokens, table, norm_shard, w_qkv, w_out, w_in, w_down)


def body(token_ids, order, timesteps, table, norm_gain, norm_bias, w_qkv, w_out, w_in, w_down):
    stages, planes = lax.axis_size("section"), lax.axis_size("dp")
    vocab, width = table.shape
    rows = planes // 2
    stamps = jnp.broadcast_to(timesteps[:, :, None], token_ids.shape)
    tokens = jnp.concatenate([token_ids, order, stamps], axis=1)
    share = norm_gain.shape[2]
    at_column = lax.axis_index("dp") * share
    norm_shard = jnp.zeros((rows * NORM_ROWS, width), jnp.float32)
    for kind, value in enumerate((norm_gain, norm_bias)):
        norm_shard = lax.dynamic_update_slice(
            norm_shard, value[0], (kind * NORM_ROWS, at_column)
        )
    sums = run_pipeline(stages, planes, tokens, table, norm_shard, w_qkv, w_out, w_in, w_down)
    table_total = lax.psum(sums[0][:vocab], ("section", "dp"))
    columns = width // stages
    table_part = lax.dynamic_slice_in_dim(
        table_total, lax.axis_index("section") * columns, columns, 1
    )
    norm_part = lax.dynamic_slice_in_dim(sums[1], at_column, share, 1)
    return (
        table_part,
        norm_part[None, :2],
        norm_part[None, NORM_ROWS : NORM_ROWS + 2],
        *(total.astype(jnp.float32)[None] for total in sums[2:6]),
    )


def solution(mesh):
    in_specs = (
        P(None, "dp", None),
        P(None, "dp", None),
        P(None, "dp"),
        P(),
        P("section", None, "dp"),
        P("section", None, "dp"),
        P("section", "dp", None),
        P("section", "dp", None),
        P("section", "dp", None),
        P("section", "dp", None),
    )
    out_specs = (
        P(None, "section"),
        P("section", None, "dp"),
        P("section", None, "dp"),
        P("section", "dp", None),
        P("section", "dp", None),
        P("section", "dp", None),
        P("section", "dp", None),
    )
    return jax.shard_map(body, mesh=mesh, in_specs=in_specs, out_specs=out_specs, check_vma=False)
```

```python
import functools
import math

import jax
import jax.numpy as jnp
from jax import lax
from jax.experimental import pallas as pl
from jax.experimental.pallas import tpu as pltpu
from jax.sharding import PartitionSpec as P

HEADS = 8
EPSILON = 1e-05
EMBED_GAIN = 16.0
FF_CHUNK = 512
AHEAD = 2
NORM_ROWS = 8
MESH = pl.DeviceIdType.MESH


def dot(left, right, left_dim, right_dim):
    return lax.dot_general(
        left, right, (((left_dim,), (right_dim,)), ((), ())), preferred_element_type=jnp.float32
    )


def unit_rows(values):
    average = jnp.mean(values, axis=-1, keepdims=True)
    centered = values - average
    variance = jnp.mean(centered * centered, axis=-1, keepdims=True)
    scale = lax.rsqrt(variance + EPSILON)
    return centered * scale, scale


def unit_back(gradient, unit, scale):
    first = jnp.mean(gradient, axis=-1, keepdims=True)
    second = jnp.mean(gradient * unit, axis=-1, keepdims=True)
    return scale * (gradient - first - unit * second)


def fold_rows(values):
    rows, columns = values.shape
    return jnp.sum(values.reshape(rows // 8, 8, columns), axis=0)


def chip_of(place, row, per_plane):
    return row * per_plane + lax.rem(place - lax.rem(row, per_plane) + per_plane, per_plane)


def start_copy(src, dst, send_sem, recv_sem, device, here):
    section, plane = device
    same = jnp.logical_and(section == here[0], plane == here[1])

    @pl.when(same)
    def _():
        pltpu.make_async_copy(src, dst, recv_sem).start()

    @pl.when(jnp.logical_not(same))
    def _():
        remote_copy(src, dst, send_sem, recv_sem, device).start()


def wait_sent(src, dst, send_sem, recv_sem, device, here):
    section, plane = device
    same = jnp.logical_and(section == here[0], plane == here[1])

    @pl.when(jnp.logical_not(same))
    def _():
        remote_copy(src, dst, send_sem, recv_sem, device).wait_send()


def remote_copy(src, dst, send_sem, recv_sem, device):
    return pltpu.make_async_remote_copy(
        src_ref=src,
        dst_ref=dst,
        send_sem=send_sem,
        recv_sem=recv_sem,
        device_id={"section": device[0], "dp": device[1]},
        device_id_type=MESH,
    )


def pipeline_kernel(
    stages,
    planes,
    token_in_ref,
    table_ref,
    norm_shard,
    qkv_shard,
    out_shard,
    in_shard,
    down_shard,
    d_table_ref,
    norm_total,
    qkv_total,
    out_total,
    in_total,
    down_total,
    stash_ref,
    token_ref,
    h_in,
    g_in,
    h_send,
    g_send,
    packed,
    mixed,
    middle,
    active,
    slope,
    attention_out,
    attention_in,
    work,
    table_parts,
    norm_sums,
    table_sum,
    norm_slots,
    norm_full,
    w_qkv_ref,
    w_out_ref,
    w_in_ref,
    w_down_ref,
    gain_ref,
    bias_ref,
    d_norm_ref,
    d_qkv_ref,
    d_out_ref,
    d_in_ref,
    d_down_ref,
    h_send_sem,
    h_recv_sem,
    g_send_sem,
    g_recv_sem,
    stash_sem,
    token_send_sem,
    token_recv_sem,
    load_sem,
    spread_send,
    spread_recv,
    plane_send,
    plane_recv,
    peer_send,
    peer_recv,
    core_send,
    core_recv,
    core_free,
    peer_free,
    total_send,
    total_recv,
    table_slots,
    table_send,
    table_recv,
):
    micro_count, _, length = token_ref.shape
    vocab, width = table_ref.shape
    hidden_units = w_in_ref.shape[1]
    head_size = width // HEADS
    score_scale = 1.0 / math.sqrt(head_size)
    root = math.sqrt(2.0 / math.pi)
    pair_width = 2 * head_size
    bf16, f32 = jnp.bfloat16, jnp.float32

    per_plane, rows = stages // planes, planes // 2
    section, plane = lax.axis_index("section"), lax.axis_index("dp")
    here = (section, plane)
    chip, core = lax.div(section, 2), lax.rem(section, 2)
    row = lax.div(chip, per_plane)
    place = lax.rem(lax.rem(chip, per_plane) + row, per_plane)
    odd = lax.rem(plane, 2)
    turn = jnp.where(odd == 0, place, per_plane - 1 - place)
    stage = plane * per_plane + turn
    last = stages - 1
    lane_row = lax.rem(row - lax.rem(place, rows) * core + rows, rows)
    lane_index = 2 * lane_row + core

    def next_device():
        step = jnp.where(odd == 0, 1, -1)
        near_place = place + step
        near_row = lax.rem(row + core * step + rows, rows)
        near = 2 * chip_of(near_place + per_plane, near_row, per_plane) + core
        stays = turn < per_plane - 1
        return jnp.where(stays, near, section), jnp.where(stays, plane, plane + 1)

    def previous_device():
        step = jnp.where(odd == 0, -1, 1)
        near_place = place + step
        near_row = lax.rem(row + core * step + rows, rows)
        near = 2 * chip_of(near_place + per_plane, near_row, per_plane) + core
        stays = turn > 0
        return jnp.where(stays, near, section), jnp.where(stays, plane, plane - 1)

    ahead, behind = next_device(), previous_device()
    partner = (section + 1 - 2 * core, plane)

    def layer_device(layer, at_row, at_core):
        at_plane, at_turn = lax.div(layer, per_plane), lax.rem(layer, per_plane)
        at_place = jnp.where(lax.rem(at_plane, 2) == 0, at_turn, per_plane - 1 - at_turn)
        return 2 * chip_of(at_place, at_row, per_plane) + at_core, at_plane

    def layer_here(at_plane):
        at_turn = jnp.where(at_plane % 2 == 0, place, per_plane - 1 - place)
        return at_plane * per_plane + at_turn

    def peer(at_row):
        return layer_device(stage, at_row, core)

    home_plane = lax.div(section, per_plane)
    carries = lax.rem(plane, 2) == core

    barrier = pltpu.get_barrier_semaphore()
    greetings = []

    def greet(device, wanted=True):
        same = jnp.logical_and(device[0] == section, device[1] == plane)
        wanted = jnp.logical_and(wanted, jnp.logical_not(same))
        greetings.append(jnp.where(wanted, 1, 0))

        @pl.when(wanted)
        def _():
            pl.semaphore_signal(
                barrier,
                inc=1,
                device_id={"section": device[0], "dp": device[1]},
                device_id_type=MESH,
            )

    for other in range(planes):
        greet((section, other))
        greet((layer_here(other), plane), carries)
    for at_row in range(rows):
        owner = layer_device(section, at_row, lax.rem(plane, 2))
        greet((owner[0], plane))
        greet(owner)
        greet((stage, 2 * at_row + core))
        greet(peer(at_row))
    for at_place in range(per_plane):
        greet((2 * chip_of(at_place, row, per_plane) + core, plane))
    greet(partner)
    greet(ahead, stage < last)
    greet(behind, stage > 0)
    pl.semaphore_wait(barrier, sum(greetings))

    matrices = (
        (w_qkv_ref, d_qkv_ref, qkv_shard, qkv_total, packed),
        (w_out_ref, d_out_ref, out_shard, out_total, mixed),
        (w_in_ref, d_in_ref, in_shard, in_total, active),
        (w_down_ref, d_down_ref, down_shard, down_total, middle),
        (norm_full, d_norm_ref, norm_shard, norm_total, norm_slots),
    )
    count = len(matrices)
    norms = count - 1
    heights = [matrix[0].shape[0] // (planes * rows) for matrix in matrices]

    def slot(matrix, index):
        buffer, height = matrices[matrix][4], heights[matrix]
        per_block = buffer.shape[1] // height
        block, inside = index // per_block, index % per_block
        if not isinstance(inside, int):
            inside = pl.multiple_of(inside * height, height)
        else:
            inside = inside * height
        return buffer.at[block, pl.ds(inside, height)]

    def piece(matrix, quarter, at_row):
        height = heights[matrix]
        return pl.ds(pl.multiple_of((quarter * rows + at_row) * height, height), height)

    gives_tokens = jnp.logical_and(place == 0, lane_index == plane)
    takes_tokens = jnp.logical_or(stage == 0, stage == last)

    def token_copy(index, target):
        return (
            token_in_ref,
            token_ref,
            token_send_sem.at[index],
            token_recv_sem,
            (section, target),
        )

    @pl.when(gives_tokens)
    def _():
        for index, target in enumerate((0, planes - 1)):
            start_copy(*token_copy(index, target), here)

    loads = []
    for matrix in range(norms):
        shard, landing = matrices[matrix][2], matrices[matrix][1]
        loads.append(
            pltpu.make_async_copy(
                shard.at[0], landing.at[pl.ds(0, shard.shape[1])], load_sem.at[matrix]
            )
        )
        loads[-1].start()

    def spread_args(matrix, at_row):
        target, _ = layer_device(section, at_row, lax.rem(plane, 2))
        if matrix == norms:
            source = norm_shard.at[pl.ds(at_row * NORM_ROWS, NORM_ROWS)]
        else:
            source = slot(matrix, planes + at_row)
        return (
            source,
            slot(matrix, home_plane),
            spread_send.at[matrix, at_row],
            spread_recv.at[matrix, home_plane],
            (target, plane),
        )

    def plane_args(matrix, to_plane, from_plane):
        return (
            slot(matrix, to_plane),
            matrices[matrix][0].at[piece(matrix, from_plane, row)],
            plane_send.at[matrix, to_plane],
            plane_recv.at[matrix, lax.div(from_plane, 2)],
            (section, to_plane),
        )

    def peer_args(matrix, quarter_pair, from_row, to_row):
        part = matrices[matrix][0].at[piece(matrix, 2 * quarter_pair + core, from_row)]
        return (
            part,
            part,
            peer_send.at[matrix, quarter_pair, to_row],
            peer_recv.at[matrix, quarter_pair, from_row],
            peer(to_row),
        )

    def core_args(matrix, quarter_pair, at_row, from_core):
        part = matrices[matrix][0].at[piece(matrix, 2 * quarter_pair + from_core, at_row)]
        return (
            part,
            part,
            core_send.at[matrix, quarter_pair, at_row],
            core_recv.at[matrix, quarter_pair, at_row],
            partner,
        )

    def spread(matrix):
        if matrix != norms:
            loads[matrix].wait()
            for at_row in range(rows):
                height = heights[matrix]
                source = matrices[matrix][1][at_row * height : (at_row + 1) * height, :]
                slot(matrix, planes + at_row)[...] = source.astype(bf16)
        for at_row in range(rows):
            start_copy(*spread_args(matrix, at_row), here)

    def along_planes(matrix):
        @pl.when(carries)
        def _():
            for to_plane in range(planes):
                remote_copy(
                    slot(matrix, to_plane),
                    slot(matrix, to_plane),
                    spread_send.at[matrix, 0],
                    spread_recv.at[matrix, to_plane],
                    partner,
                ).wait_recv()
                start_copy(*plane_args(matrix, to_plane, plane), here)

    def between_peers(matrix):
        for pair in range(rows):
            remote_copy(*plane_args(matrix, 0, 2 * pair + core)).wait_recv()
            for to_row in range(rows):
                @pl.when(to_row != row)
                def _():
                    remote_copy(*peer_args(matrix, pair, row, to_row)).start()

            remote_copy(*core_args(matrix, pair, row, core)).start()

    def between_cores(matrix):
        for pair in range(rows):
            for from_row in range(rows):
                @pl.when(from_row != row)
                def _():
                    remote_copy(*peer_args(matrix, pair, from_row, from_row)).wait_recv()
                    remote_copy(*core_args(matrix, pair, from_row, core)).start()

    def gathered(matrix):
        for pair in range(rows):
            for at_row in range(rows):
                remote_copy(*core_args(matrix, pair, at_row, 1 - core)).wait_recv()

    def gather_sent(matrix):
        for at_row in range(rows):
            wait_sent(*spread_args(matrix, at_row), here)

        @pl.when(carries)
        def _():
            for to_plane in range(planes):
                wait_sent(*plane_args(matrix, to_plane, plane), here)

        for pair in range(rows):
            for at_row in range(rows):
                @pl.when(at_row != row)
                def _():
                    remote_copy(*peer_args(matrix, pair, row, at_row)).wait_send()

                remote_copy(*core_args(matrix, pair, at_row, core)).wait_send()

    steps_of_gather = (spread, along_planes, between_peers, between_cores, gathered)
    order = (norms, 0, 1, 2, 3)
    for turn_at in range(count + len(steps_of_gather) - 1):
        for depth, action in enumerate(steps_of_gather):
            if 0 <= turn_at - depth < count:
                action(order[turn_at - depth])
    for matrix in range(count):
        gather_sent(matrix)

    @pl.when(takes_tokens)
    def _():
        remote_copy(*token_copy(0, 0)).wait_recv()

    @pl.when(gives_tokens)
    def _():
        for index, target in enumerate((0, planes - 1)):
            wait_sent(*token_copy(index, target), here)

    for kind, ref in enumerate((gain_ref, bias_ref)):
        total = jnp.zeros((NORM_ROWS, width), f32)
        for quarter in range(planes):
            start = (quarter * rows + kind) * NORM_ROWS
            total = total + norm_full[start : start + NORM_ROWS, :]
        ref[...] = total.astype(bf16).astype(f32)

    table_rows = table_parts.shape[1]
    work[:table_rows, :] = jnp.zeros((table_rows, width), f32)
    work[:vocab, :] = table_ref[...]
    rest = work[:table_rows, :]
    for part in range(3):
        rounded = rest.astype(bf16)
        table_parts[part] = rounded
        rest = rest - rounded.astype(f32)
    d_qkv_ref[...] = jnp.zeros_like(d_qkv_ref)
    d_out_ref[...] = jnp.zeros_like(d_out_ref)
    d_in_ref[...] = jnp.zeros_like(d_in_ref)
    d_down_ref[...] = jnp.zeros_like(d_down_ref)
    norm_sums[...] = jnp.zeros_like(norm_sums)
    table_sum[...] = jnp.zeros_like(table_sum)

    letters = lax.broadcasted_iota(jnp.int32, (table_rows, length), 0)
    lane = lax.broadcasted_iota(jnp.int32, (length, pair_width), 1)
    lower = lane < head_size

    def shown_rows(micro):
        rows_of = token_ref[micro]
        visible = rows_of[1:2] < rows_of[2:3]
        shown = jnp.where(visible, rows_of[0:1], vocab - 1)
        return (letters == shown).astype(bf16)

    def stacked(pair):
        zero = jnp.zeros_like(pair)
        return jnp.concatenate(
            [jnp.where(lower, pair, zero), jnp.where(lower, zero, pair)], axis=0
        )

    def load_hidden(micro):
        @pl.when(stage == 0)
        def _():
            hot = shown_rows(micro)
            total = dot(hot, table_parts[2], 0, 0)
            total = total + dot(hot, table_parts[1], 0, 0)
            total = total + dot(hot, table_parts[0], 0, 0)
            work[...] = total * EMBED_GAIN

        @pl.when(stage > 0)
        def _():
            work[...] = h_in[micro].astype(f32)

    def hidden_copy(micro, target):
        slot = lax.rem(micro, 2)
        return pltpu.make_async_remote_copy(
            src_ref=h_send.at[slot],
            dst_ref=h_in.at[micro],
            send_sem=h_send_sem.at[slot],
            recv_sem=h_recv_sem.at[micro],
            device_id={"section": target[0], "dp": target[1]},
            device_id_type=MESH,
        )

    def gradient_copy(micro, target):
        slot = lax.rem(micro, 2)
        return pltpu.make_async_remote_copy(
            src_ref=g_send.at[slot],
            dst_ref=g_in.at[micro],
            send_sem=g_send_sem.at[slot],
            recv_sem=g_recv_sem.at[micro],
            device_id={"section": target[0], "dp": target[1]},
            device_id_type=MESH,
        )

    def forward(micro):
        if stages > 1:
            @pl.when(stage > 0)
            def _():
                hidden_copy(micro, behind).wait_recv()
        load_hidden(micro)
        hidden = work[...]
        unit, _ = unit_rows(hidden)
        normed = (unit * gain_ref[0:1, :] + bias_ref[0:1, :]).astype(bf16)
        packed[micro] = dot(normed, w_qkv_ref[...], 1, 0).astype(bf16)
        pairs = HEADS // 2

        def block(member, pair):
            at = member * width + pair * pair_width
            return packed[micro, :, at : at + pair_width]

        def scores_of(pair):
            query = block(0, pair) * jnp.asarray(score_scale, bf16)
            return dot(stacked(query), block(1, pair), 1, 1)

        waiting = [scores_of(pair) for pair in range(AHEAD)]
        for pair in range(pairs):
            if pair + AHEAD < pairs:
                waiting.append(scores_of(pair + AHEAD))
            scores = waiting[pair]
            largest = jnp.max(scores, axis=-1, keepdims=True)
            powers = jnp.exp(scores - largest)
            total = jnp.sum(powers, axis=-1, keepdims=True)
            attention = (powers * (1.0 / total)).astype(bf16)
            attention_out[2 * pair] = attention[:length]
            attention_out[2 * pair + 1] = attention[length:]
            found = dot(attention, block(2, pair), 1, 0)
            at = pair * pair_width
            mixed[micro, :, at : at + pair_width] = jnp.where(
                lower, found[:length], found[length:]
            ).astype(bf16)
        save = pltpu.make_async_copy(attention_out, stash_ref.at[micro], stash_sem)
        save.start()
        between = hidden + dot(mixed[micro], w_out_ref[...], 1, 0)
        high = between.astype(bf16)
        middle[2 * micro + 0] = high
        middle[2 * micro + 1] = (between - high.astype(f32)).astype(bf16)
        work[...] = between
        unit, _ = unit_rows(between)
        normed_two = (unit * gain_ref[1:2, :] + bias_ref[1:2, :]).astype(bf16)
        for at in range(0, hidden_units, FF_CHUNK):
            lifted = dot(normed_two, w_in_ref[:, at : at + FF_CHUNK], 1, 0)
            bent = (root * 0.044715) * (lifted * lifted)
            half = 0.5 + 0.5 * jnp.tanh(lifted * (bent + root))
            gelu = lifted * half
            active[micro, :, at : at + FF_CHUNK] = gelu.astype(bf16)
            slope[micro, :, at : at + FF_CHUNK] = (
                half + gelu * ((1.0 - half) * (6.0 * bent + 2.0 * root))
            ).astype(bf16)
        if stages > 1:
            @pl.when(jnp.logical_and(micro >= 2, stage < last))
            def _():
                hidden_copy(micro - 2, ahead).wait_send()
        slot = lax.rem(micro, 2)
        h_send[slot] = (work[...] + dot(active[micro], w_down_ref[...], 1, 0)).astype(bf16)
        if stages > 1:
            @pl.when(stage < last)
            def _():
                hidden_copy(micro, ahead).start()
        save.wait()

    def head(micro):
        unit, scale = unit_rows(h_send[lax.rem(micro, 2)].astype(f32))
        rounded = unit.astype(bf16)
        logits = dot(table_parts[0], rounded, 1, 1)
        logits = jnp.where(letters < vocab, logits, -jnp.inf)
        largest = jnp.max(logits, axis=0, keepdims=True)
        powers = jnp.exp(logits - largest)
        total = jnp.sum(powers, axis=0, keepdims=True)
        rows_of = token_ref[micro]
        stamp = rows_of[2:3]
        weight = jnp.where(rows_of[1:2] < stamp, 0.0, 1.0 / (length - stamp).astype(f32))
        target = (letters == rows_of[0:1]).astype(f32)
        g_logits = (weight * (powers / total - target)).astype(bf16)
        table_sum[...] += dot(g_logits, rounded, 1, 0)
        g_unit = dot(g_logits, table_parts[0], 0, 0)
        g_in[micro] = unit_back(g_unit, unit, scale).astype(bf16)

    def backward(micro):
        @pl.when(stage == last)
        def _():
            head(micro)

        if stages > 1:
            @pl.when(stage < last)
            def _():
                gradient_copy(micro, ahead).wait_recv()
        load = pltpu.make_async_copy(stash_ref.at[micro], attention_in, stash_sem)
        load.start()
        g_out = g_in[micro]
        for at in range(0, hidden_units, FF_CHUNK):
            g_active = dot(g_out, w_down_ref[at : at + FF_CHUNK, :], 1, 1)
            slope[micro, :, at : at + FF_CHUNK] = (
                g_active * slope[micro, :, at : at + FF_CHUNK].astype(f32)
            ).astype(bf16)
        g_normed = dot(slope[micro], w_in_ref[...], 1, 1)
        unit, scale = unit_rows(middle[2 * micro + 0].astype(f32) + middle[2 * micro + 1].astype(f32))
        middle[2 * micro + 0] = (unit * gain_ref[1:2, :] + bias_ref[1:2, :]).astype(bf16)
        norm_sums[1] += fold_rows(g_normed * unit)
        norm_sums[3] += fold_rows(g_normed)
        g_middle = g_out.astype(f32) + unit_back(g_normed * gain_ref[1:2, :], unit, scale)
        g_attended = g_middle.astype(bf16)
        middle[2 * micro + 1] = g_attended
        g_mixed = dot(g_attended, w_out_ref[...], 1, 1).astype(bf16)
        load_hidden(micro)
        load.wait()
        pairs = HEADS // 2

        def block(member, pair):
            at = member * width + pair * pair_width
            return packed[micro, :, at : at + pair_width]

        def put(member, pair, value):
            at = member * width + pair * pair_width
            packed[micro, :, at : at + pair_width] = value.astype(bf16)

        def g_attention_of(pair):
            at = pair * pair_width
            g_pair = stacked(g_mixed[:, at : at + pair_width])
            return g_pair, dot(g_pair, block(2, pair), 1, 1)

        waiting = [g_attention_of(pair) for pair in range(AHEAD)]
        for pair in range(pairs):
            if pair + AHEAD < pairs:
                waiting.append(g_attention_of(pair + AHEAD))
            g_pair, g_attention = waiting[pair]
            low = attention_in[2 * pair : 2 * pair + 2].reshape(2 * length, length)
            attention = low.astype(f32)
            inner = jnp.sum(attention * g_attention, axis=-1, keepdims=True)
            g_scores = (attention * (g_attention - inner)).astype(bf16)
            key, query = block(1, pair), stacked(block(0, pair))
            g_values = dot(low, g_pair, 0, 0)
            g_queries = dot(g_scores, key, 1, 0)
            g_keys = dot(g_scores, query, 0, 0)
            put(0, pair, jnp.where(lower, g_queries[:length], g_queries[length:]) * score_scale)
            put(1, pair, g_keys * score_scale)
            put(2, pair, g_values)
        g_normed = dot(packed[micro], w_qkv_ref[...], 1, 1)
        unit, scale = unit_rows(work[...])
        h_in[micro] = (unit * gain_ref[0:1, :] + bias_ref[0:1, :]).astype(bf16)
        norm_sums[0] += fold_rows(g_normed * unit)
        norm_sums[2] += fold_rows(g_normed)
        g_hidden = g_middle + unit_back(g_normed * gain_ref[0:1, :], unit, scale)

        @pl.when(stage == 0)
        def _():
            hot = shown_rows(micro)
            high = g_hidden.astype(bf16)
            low = (g_hidden - high.astype(f32)).astype(bf16)
            table_sum[...] += EMBED_GAIN * (dot(hot, high, 1, 0) + dot(hot, low, 1, 0))

        if stages > 1:
            @pl.when(stage > 0)
            def _():
                @pl.when(micro >= 2)
                def _():
                    gradient_copy(micro - 2, behind).wait_send()

                g_send[lax.rem(micro, 2)] = g_hidden.astype(bf16)
                gradient_copy(micro, behind).start()

    def weights(micro):
        d_down_ref[...] += dot(active[micro], g_in[micro], 0, 0)
        d_in_ref[...] += dot(middle[2 * micro + 0], slope[micro], 0, 0)
        d_out_ref[...] += dot(mixed[micro], middle[2 * micro + 1], 0, 0)
        d_qkv_ref[...] += dot(h_in[micro], packed[micro], 0, 0)

    steps = max(2 * last + micro_count, last + 2 * micro_count)

    def step(index, carry):
        f_micro = index - stage
        b_micro = index - (2 * last - stage)
        w_micro = index - jnp.maximum(stage + micro_count, 2 * last - stage)

        @pl.when(jnp.logical_and(f_micro >= 0, f_micro < micro_count))
        def _():
            forward(f_micro)

        @pl.when(jnp.logical_and(b_micro >= 0, b_micro < micro_count))
        def _():
            backward(b_micro)

        @pl.when(jnp.logical_and(w_micro >= 0, w_micro < micro_count))
        def _():
            weights(w_micro)

        return carry

    lax.fori_loop(0, steps, step, 0)

    if stages > 1:
        for micro in range(max(micro_count - 2, 0), micro_count):
            @pl.when(stage < last)
            def _():
                hidden_copy(micro, ahead).wait_send()

            @pl.when(stage > 0)
            def _():
                gradient_copy(micro, behind).wait_send()

    def table_copy(source, target, send, recv, device):
        return remote_copy(source, target, table_send.at[send], table_recv.at[recv], device)

    def lane_copy():
        return table_copy(table_sum, table_slots.at[0], 0, 0, (section, 0))

    def table_core_copy():
        return table_copy(table_sum, table_slots.at[1], 1, 1, partner)

    def table_peer_copy(from_row, to_row):
        return table_copy(
            table_sum, table_slots.at[2 + from_row], 2 + to_row, 2 + from_row, peer(to_row)
        )

    def table_down_copy(to_plane):
        return table_copy(
            d_table_ref, d_table_ref, 2 + rows + to_plane, 2 + rows, (section, to_plane)
        )

    def table_side_copy(to_place):
        target = 2 * chip_of(to_place, row, per_plane) + core
        return table_copy(
            d_table_ref, d_table_ref, 2 + rows + planes + to_place, 2 + rows, (target, plane)
        )

    @pl.when(stage == last)
    def _():
        lane_copy().start()

    def table_cores():
        @pl.when(stage == 0)
        def _():
            lane_copy().wait_recv()
            table_sum[...] += table_slots[0]
            table_core_copy().start()

    def table_peers():
        @pl.when(stage == 0)
        def _():
            table_core_copy().wait()
            table_sum[...] += table_slots[1]
            for to_row in range(rows):
                @pl.when(to_row != row)
                def _():
                    table_peer_copy(row, to_row).start()

    def table_side():
        for to_place in range(1, per_plane):
            table_side_copy(to_place).start()

    def table_down():
        @pl.when(stage == 0)
        def _():
            total = table_sum[...]
            for from_row in range(rows):
                @pl.when(from_row != row)
                def _():
                    table_peer_copy(from_row, from_row).wait_recv()

                total = total + jnp.where(from_row != row, table_slots[2 + from_row], 0.0)
            d_table_ref[...] = total
            for to_plane in range(1, planes):
                table_down_copy(to_plane).start()
            table_side()

    def table_done():
        @pl.when(place > 0)
        def _():
            table_side_copy(0).wait_recv()

        @pl.when(stage == last)
        def _():
            lane_copy().wait_send()

        @pl.when(stage == 0)
        def _():
            for to_row in range(rows):
                @pl.when(to_row != row)
                def _():
                    table_peer_copy(row, to_row).wait_send()

            for to_plane in range(1, planes):
                table_down_copy(to_plane).wait_send()

        @pl.when(place == 0)
        def _():
            for to_place in range(1, per_plane):
                table_side_copy(to_place).wait_send()

    for kind in range(2):
        totals = [
            jnp.sum(norm_sums[2 * kind + member], axis=0, keepdims=True) for member in range(2)
        ]
        block = jnp.concatenate(totals + [jnp.zeros((NORM_ROWS - 2, width), f32)], axis=0)
        for quarter in range(planes):
            start = (quarter * rows + kind) * NORM_ROWS
            d_norm_ref[start : start + NORM_ROWS, :] = block

    pl.semaphore_signal(
        core_free, inc=1, device_id={"section": partner[0], "dp": partner[1]}, device_id_type=MESH
    )
    for at_row in range(rows):
        @pl.when(at_row != row)
        def _():
            far = peer(at_row)
            pl.semaphore_signal(
                peer_free, inc=1, device_id={"section": far[0], "dp": far[1]}, device_id_type=MESH
            )

    def core_sum_args(matrix, pair, at_row):
        index = pair * rows + at_row
        return (
            slot(matrix, index),
            slot(matrix, rows * rows + index),
            core_send.at[matrix, pair, at_row],
            core_recv.at[matrix, pair, at_row],
            partner,
        )

    def peer_sum_args(matrix, pair, from_row, to_row):
        return (
            slot(matrix, 2 * rows * rows + pair * rows + to_row),
            slot(matrix, 3 * rows * rows + pair * rows + from_row),
            peer_send.at[matrix, pair, to_row],
            peer_recv.at[matrix, pair, from_row],
            peer(to_row),
        )

    def total_args(matrix, pair):
        height = heights[matrix]
        return (
            slot(matrix, 2 * rows * rows + pair * rows + row),
            matrices[matrix][3].at[pl.ds(pl.multiple_of(row * height, height), height)],
            total_send.at[matrix, pair],
            total_recv.at[matrix, row],
            (stage, 2 * pair + core),
        )

    def give_core(matrix):
        for pair in range(rows):
            for at_row in range(rows):
                args = core_sum_args(matrix, pair, at_row)
                part = matrices[matrix][1][piece(matrix, 2 * pair + 1 - core, at_row), :]
                args[0][...] = part.astype(args[0].dtype)
                remote_copy(*args).start()

    def give_peers(matrix):
        for pair in range(rows):
            for at_row in range(rows):
                remote_copy(*core_sum_args(matrix, pair, at_row)).wait_recv()
                landed = slot(matrix, rows * rows + pair * rows + at_row)
                part = matrices[matrix][1].at[piece(matrix, 2 * pair + core, at_row)]
                total = part[...] + landed[...].astype(f32)

                @pl.when(at_row != row)
                def _():
                    args = peer_sum_args(matrix, pair, row, at_row)
                    args[0][...] = total.astype(args[0].dtype)
                    remote_copy(*args).start()

                @pl.when(at_row == row)
                def _():
                    part[...] = total

    def give_totals(matrix):
        for pair in range(rows):
            part = matrices[matrix][1].at[piece(matrix, 2 * pair + core, row)]
            for from_row in range(rows):
                @pl.when(from_row != row)
                def _():
                    remote_copy(*peer_sum_args(matrix, pair, from_row, from_row)).wait_recv()
                    landed = slot(matrix, 3 * rows * rows + pair * rows + from_row)
                    part[...] += landed[...].astype(f32)

            args = total_args(matrix, pair)
            args[0][...] = part[...].astype(args[0].dtype)
            start_copy(*args, here)

    def finish(matrix):
        height = heights[matrix]
        for from_row in range(rows):
            part = matrices[matrix][3].at[pl.ds(from_row * height, height)]
            remote_copy(
                part, part, total_send.at[matrix, 0], total_recv.at[matrix, from_row], partner
            ).wait_recv()
        for pair in range(rows):
            for at_row in range(rows):
                remote_copy(*core_sum_args(matrix, pair, at_row)).wait_send()

                @pl.when(at_row != row)
                def _():
                    remote_copy(*peer_sum_args(matrix, pair, row, at_row)).wait_send()

            wait_sent(*total_args(matrix, pair), here)

    order = (norms, 3, 2, 0, 1)
    table_cores()
    pl.semaphore_wait(core_free, 1)
    for matrix in order:
        give_core(matrix)
    table_peers()
    pl.semaphore_wait(peer_free, rows - 1)
    for position in range(count + 1):
        if position < count:
            give_peers(order[position])
        if position > 0:
            give_totals(order[position - 1])
        if position == 1:
            table_down()
    @pl.when(jnp.logical_and(place == 0, plane > 0))
    def _():
        table_down_copy(0).wait_recv()
        table_side()

    for matrix in order:
        finish(matrix)
    table_done()


def run_pipeline(stages, planes, tokens, table, norm_shard, w_qkv, w_out, w_in, w_down):
    micro_count, _, length = tokens.shape
    width = table.shape[1]
    hidden_units = w_in.shape[2]
    rows = planes // 2
    table_rows = -(-table.shape[0] // 32) * 32
    bf16, f32 = jnp.bfloat16, jnp.float32
    vmem = pl.BlockSpec(memory_space=pltpu.VMEM)
    anywhere = pl.BlockSpec(memory_space=pl.ANY)
    shards = (w_qkv, w_out, w_in, w_down)
    full = [(shard.shape[1] * planes, shard.shape[2]) for shard in shards]
    norm_full = (planes * norm_shard.shape[0], width)
    outs = (
        jax.ShapeDtypeStruct((table_rows, width), f32),
        jax.ShapeDtypeStruct(norm_shard.shape, f32),
        *(jax.ShapeDtypeStruct(shard.shape[1:], bf16) for shard in shards),
        jax.ShapeDtypeStruct((micro_count, HEADS, length, length), bf16),
    )
    rows_shape = (micro_count, length, width)
    pieces = (5, rows, rows)
    return pl.pallas_call(
        functools.partial(pipeline_kernel, stages, planes),
        out_shape=outs,
        in_specs=[vmem] * 3 + [anywhere] * 4,
        out_specs=[vmem] * 6 + [anywhere],
        scratch_shapes=[
            pltpu.VMEM(tokens.shape, jnp.int32),
            pltpu.VMEM(rows_shape, bf16),
            pltpu.VMEM(rows_shape, bf16),
            pltpu.VMEM((2, length, width), bf16),
            pltpu.VMEM((2, length, width), bf16),
            pltpu.VMEM((micro_count, length, 3 * width), bf16),
            pltpu.VMEM(rows_shape, bf16),
            pltpu.VMEM((2 * micro_count, length, width), bf16),
            pltpu.VMEM((micro_count, length, hidden_units), bf16),
            pltpu.VMEM((micro_count, length, hidden_units), bf16),
            pltpu.VMEM((HEADS, length, length), bf16),
            pltpu.VMEM((HEADS, length, length), bf16),
            pltpu.VMEM((length, width), f32),
            pltpu.VMEM((3, table_rows, width), bf16),
            pltpu.VMEM((4, 8, width), f32),
            pltpu.VMEM((table_rows, width), f32),
            pltpu.VMEM((4 * rows * rows, NORM_ROWS, width), f32),
            pltpu.VMEM(norm_full, f32),
            *(pltpu.VMEM(shape, bf16) for shape in full),
            pltpu.VMEM((NORM_ROWS, width), f32),
            pltpu.VMEM((NORM_ROWS, width), f32),
            pltpu.VMEM(norm_full, f32),
            *(pltpu.VMEM(shape, f32) for shape in full),
            pltpu.SemaphoreType.DMA((2,)),
            pltpu.SemaphoreType.DMA((micro_count,)),
            pltpu.SemaphoreType.DMA((2,)),
            pltpu.SemaphoreType.DMA((micro_count,)),
            pltpu.SemaphoreType.DMA,
            pltpu.SemaphoreType.DMA((2,)),
            pltpu.SemaphoreType.DMA,
            pltpu.SemaphoreType.DMA((4,)),
            pltpu.SemaphoreType.DMA((5, rows)),
            pltpu.SemaphoreType.DMA((5, planes)),
            pltpu.SemaphoreType.DMA((5, planes)),
            pltpu.SemaphoreType.DMA((5, rows)),
            pltpu.SemaphoreType.DMA(pieces),
            pltpu.SemaphoreType.DMA(pieces),
            pltpu.SemaphoreType.DMA(pieces),
            pltpu.SemaphoreType.DMA(pieces),
            pltpu.SemaphoreType.REGULAR,
            pltpu.SemaphoreType.REGULAR,
            pltpu.SemaphoreType.DMA((5, rows)),
            pltpu.SemaphoreType.DMA((5, rows)),
            pltpu.VMEM((2 + rows, table_rows, width), f32),
            pltpu.SemaphoreType.DMA((2 + rows + planes + stages // planes,)),
            pltpu.SemaphoreType.DMA((3 + rows,)),
        ],
        compiler_params=pltpu.CompilerParams(
            vmem_limit_bytes=63 << 20, collective_id=0, has_side_effects=True
        ),
    )(tokens, table, norm_shard, w_qkv, w_out, w_in, w_down)


def body(token_ids, order, timesteps, table, norm_gain, norm_bias, w_qkv, w_out, w_in, w_down):
    stages, planes = lax.axis_size("section"), lax.axis_size("dp")
    vocab, width = table.shape
    rows = planes // 2
    stamps = jnp.broadcast_to(timesteps[:, :, None], token_ids.shape)
    tokens = jnp.concatenate([token_ids, order, stamps], axis=1)
    share = norm_gain.shape[2]
    at_column = lax.axis_index("dp") * share
    norm_shard = jnp.zeros((rows * NORM_ROWS, width), jnp.float32)
    for kind, value in enumerate((norm_gain, norm_bias)):
        norm_shard = lax.dynamic_update_slice(
            norm_shard, value[0], (kind * NORM_ROWS, at_column)
        )
    sums = run_pipeline(stages, planes, tokens, table, norm_shard, w_qkv, w_out, w_in, w_down)
    columns = width // stages
    table_part = lax.dynamic_slice(
        sums[0], (0, lax.axis_index("section") * columns), (vocab, columns)
    )
    norm_part = lax.dynamic_slice_in_dim(sums[1], at_column, share, 1)
    return (
        table_part,
        norm_part[None, :2],
        norm_part[None, NORM_ROWS : NORM_ROWS + 2],
        *(total.astype(jnp.float32)[None] for total in sums[2:6]),
    )


def solution(mesh):
    in_specs = (
        P(None, "dp", None),
        P(None, "dp", None),
        P(None, "dp"),
        P(),
        P("section", None, "dp"),
        P("section", None, "dp"),
        P("section", "dp", None),
        P("section", "dp", None),
        P("section", "dp", None),
        P("section", "dp", None),
    )
    out_specs = (
        P(None, "section"),
        P("section", None, "dp"),
        P("section", None, "dp"),
        P("section", "dp", None),
        P("section", "dp", None),
        P("section", "dp", None),
        P("section", "dp", None),
    )
    return jax.shard_map(body, mesh=mesh, in_specs=in_specs, out_specs=out_specs, check_vma=False)
```

```python
import functools
import math

import jax
import jax.numpy as jnp
from jax import lax
from jax.experimental import pallas as pl
from jax.experimental.pallas import tpu as pltpu
from jax.sharding import PartitionSpec as P

HEADS = 8
EPSILON = 1e-05
EMBED_GAIN = 16.0
FF_CHUNK = 512
AHEAD = 2
NORM_ROWS = 8
MESH = pl.DeviceIdType.MESH


def dot(left, right, left_dim, right_dim):
    return lax.dot_general(
        left, right, (((left_dim,), (right_dim,)), ((), ())), preferred_element_type=jnp.float32
    )


def unit_rows(values):
    average = jnp.mean(values, axis=-1, keepdims=True)
    centered = values - average
    variance = jnp.mean(centered * centered, axis=-1, keepdims=True)
    scale = lax.rsqrt(variance + EPSILON)
    return centered * scale, scale


def unit_back(gradient, unit, scale):
    first = jnp.mean(gradient, axis=-1, keepdims=True)
    second = jnp.mean(gradient * unit, axis=-1, keepdims=True)
    return scale * (gradient - first - unit * second)


def fold_rows(values):
    rows, columns = values.shape
    return jnp.sum(values.reshape(rows // 8, 8, columns), axis=0)


def chip_of(place, row, per_plane):
    return row * per_plane + lax.rem(place - lax.rem(row, per_plane) + per_plane, per_plane)


def start_copy(src, dst, send_sem, recv_sem, device, here):
    section, plane = device
    same = jnp.logical_and(section == here[0], plane == here[1])

    @pl.when(same)
    def _():
        pltpu.make_async_copy(src, dst, recv_sem).start()

    @pl.when(jnp.logical_not(same))
    def _():
        remote_copy(src, dst, send_sem, recv_sem, device).start()


def wait_sent(src, dst, send_sem, recv_sem, device, here):
    section, plane = device
    same = jnp.logical_and(section == here[0], plane == here[1])

    @pl.when(jnp.logical_not(same))
    def _():
        remote_copy(src, dst, send_sem, recv_sem, device).wait_send()


def remote_copy(src, dst, send_sem, recv_sem, device):
    return pltpu.make_async_remote_copy(
        src_ref=src,
        dst_ref=dst,
        send_sem=send_sem,
        recv_sem=recv_sem,
        device_id={"section": device[0], "dp": device[1]},
        device_id_type=MESH,
    )


def pipeline_kernel(
    stages,
    planes,
    ids_ref,
    order_ref,
    stamp_ref,
    table_ref,
    gain_shard,
    bias_shard,
    qkv_shard,
    out_shard,
    in_shard,
    down_shard,
    d_table_ref,
    norm_total,
    qkv_total,
    out_total,
    in_total,
    down_total,
    stash_ref,
    token_in_ref,
    norm_shard,
    token_ref,
    h_in,
    g_in,
    h_send,
    g_send,
    packed,
    mixed,
    middle,
    active,
    slope,
    attention_out,
    attention_in,
    work,
    table_parts,
    norm_sums,
    table_sum,
    norm_slots,
    norm_full,
    w_qkv_ref,
    w_out_ref,
    w_in_ref,
    w_down_ref,
    gain_ref,
    bias_ref,
    d_norm_ref,
    d_qkv_ref,
    d_out_ref,
    d_in_ref,
    d_down_ref,
    h_send_sem,
    h_recv_sem,
    g_send_sem,
    g_recv_sem,
    stash_sem,
    token_send_sem,
    token_recv_sem,
    load_sem,
    spread_send,
    spread_recv,
    plane_send,
    plane_recv,
    peer_send,
    peer_recv,
    core_send,
    core_recv,
    core_free,
    peer_free,
    total_send,
    total_recv,
    table_slots,
    table_send,
    table_recv,
):
    micro_count, _, length = token_ref.shape
    vocab, width = table_ref.shape
    hidden_units = w_in_ref.shape[1]
    head_size = width // HEADS
    score_scale = 1.0 / math.sqrt(head_size)
    root = math.sqrt(2.0 / math.pi)
    pair_width = 2 * head_size
    bf16, f32 = jnp.bfloat16, jnp.float32

    per_plane, rows = stages // planes, planes // 2
    section, plane = lax.axis_index("section"), lax.axis_index("dp")
    here = (section, plane)
    chip, core = lax.div(section, 2), lax.rem(section, 2)
    row = lax.div(chip, per_plane)
    place = lax.rem(lax.rem(chip, per_plane) + row, per_plane)
    odd = lax.rem(plane, 2)
    turn = jnp.where(odd == 0, place, per_plane - 1 - place)
    stage = plane * per_plane + turn
    last = stages - 1
    lane_row = lax.rem(row - lax.rem(place, rows) * core + rows, rows)
    lane_index = 2 * lane_row + core

    def next_device():
        step = jnp.where(odd == 0, 1, -1)
        near_place = place + step
        near_row = lax.rem(row + core * step + rows, rows)
        near = 2 * chip_of(near_place + per_plane, near_row, per_plane) + core
        stays = turn < per_plane - 1
        return jnp.where(stays, near, section), jnp.where(stays, plane, plane + 1)

    def previous_device():
        step = jnp.where(odd == 0, -1, 1)
        near_place = place + step
        near_row = lax.rem(row + core * step + rows, rows)
        near = 2 * chip_of(near_place + per_plane, near_row, per_plane) + core
        stays = turn > 0
        return jnp.where(stays, near, section), jnp.where(stays, plane, plane - 1)

    ahead, behind = next_device(), previous_device()
    partner = (section + 1 - 2 * core, plane)

    def layer_device(layer, at_row, at_core):
        at_plane, at_turn = lax.div(layer, per_plane), lax.rem(layer, per_plane)
        at_place = jnp.where(lax.rem(at_plane, 2) == 0, at_turn, per_plane - 1 - at_turn)
        return 2 * chip_of(at_place, at_row, per_plane) + at_core, at_plane

    def layer_here(at_plane):
        at_turn = jnp.where(at_plane % 2 == 0, place, per_plane - 1 - place)
        return at_plane * per_plane + at_turn

    def peer(at_row):
        return layer_device(stage, at_row, core)

    home_plane = lax.div(section, per_plane)
    carries = lax.rem(plane, 2) == core

    for micro in range(micro_count):
        token_in_ref[micro, 0:1, :] = ids_ref[micro]
        token_in_ref[micro, 1:2, :] = order_ref[micro]
        token_in_ref[micro, 2:3, :] = jnp.broadcast_to(stamp_ref[micro : micro + 1, :], (1, length))
    norm_shard[...] = jnp.zeros_like(norm_shard)
    share = gain_shard.shape[2]
    columns = lax.broadcasted_iota(jnp.int32, (2, width), 1)
    mine = jnp.logical_and(columns >= plane * share, columns < (plane + 1) * share)
    for kind, shard in enumerate((gain_shard, bias_shard)):
        spread_out = jnp.concatenate([shard[0]] * planes, axis=1)
        norm_shard[kind * NORM_ROWS : kind * NORM_ROWS + 2, :] = jnp.where(mine, spread_out, 0.0)

    barrier = pltpu.get_barrier_semaphore()
    greetings = []

    def greet(device, wanted=True):
        same = jnp.logical_and(device[0] == section, device[1] == plane)
        wanted = jnp.logical_and(wanted, jnp.logical_not(same))
        greetings.append(jnp.where(wanted, 1, 0))

        @pl.when(wanted)
        def _():
            pl.semaphore_signal(
                barrier,
                inc=1,
                device_id={"section": device[0], "dp": device[1]},
                device_id_type=MESH,
            )

    for other in range(planes):
        greet((section, other))
        greet((layer_here(other), plane), carries)
    for at_row in range(rows):
        owner = layer_device(section, at_row, lax.rem(plane, 2))
        greet((owner[0], plane))
        greet(owner)
        greet((stage, 2 * at_row + core))
        greet(peer(at_row))
    for at_place in range(per_plane):
        greet((2 * chip_of(at_place, row, per_plane) + core, plane))
    greet(partner)
    greet(ahead, stage < last)
    greet(behind, stage > 0)
    pl.semaphore_wait(barrier, sum(greetings))

    matrices = []
    for parts, *members in (
        (2, w_qkv_ref, d_qkv_ref, qkv_shard, qkv_total, packed),
        (1, w_out_ref, d_out_ref, out_shard, out_total, mixed),
        (2, w_in_ref, d_in_ref, in_shard, in_total, active),
        (2, w_down_ref, d_down_ref, down_shard, down_total, middle),
        (1, norm_full, d_norm_ref, norm_shard, norm_total, norm_slots),
    ):
        window = members[0].shape[1] // parts
        for part in range(parts):
            matrices.append((*members, pl.ds(part * window, window)))
    count = len(matrices)
    norms = count - 1
    heights = [matrix[0].shape[0] // (planes * rows) for matrix in matrices]

    def view(matrix, member, rows_of):
        return matrices[matrix][member].at[rows_of, matrices[matrix][5]]

    def slot(matrix, index):
        buffer, height = matrices[matrix][4], heights[matrix]
        per_block = buffer.shape[1] // height
        block, inside = index // per_block, index % per_block
        if not isinstance(inside, int):
            inside = pl.multiple_of(inside * height, height)
        else:
            inside = inside * height
        return buffer.at[block, pl.ds(inside, height), matrices[matrix][5]]

    def piece(matrix, quarter, at_row):
        height = heights[matrix]
        return pl.ds(pl.multiple_of((quarter * rows + at_row) * height, height), height)

    gives_tokens = jnp.logical_and(place == 0, lane_index == plane)
    takes_tokens = jnp.logical_or(stage == 0, stage == last)

    def token_copy(index, target):
        return (
            token_in_ref,
            token_ref,
            token_send_sem.at[index],
            token_recv_sem,
            (section, target),
        )

    @pl.when(gives_tokens)
    def _():
        for index, target in enumerate((0, planes - 1)):
            start_copy(*token_copy(index, target), here)

    loads = []
    for matrix in range(norms):
        shard, window = matrices[matrix][2], matrices[matrix][5]
        loads.append(
            pltpu.make_async_copy(
                shard.at[0, :, window],
                view(matrix, 1, pl.ds(0, shard.shape[1])),
                load_sem.at[matrix],
            )
        )
        loads[-1].start()

    def spread_args(matrix, at_row):
        target, _ = layer_device(section, at_row, lax.rem(plane, 2))
        if matrix == norms:
            source = norm_shard.at[pl.ds(at_row * NORM_ROWS, NORM_ROWS)]
        else:
            source = slot(matrix, planes + at_row)
        return (
            source,
            slot(matrix, home_plane),
            spread_send.at[matrix, at_row],
            spread_recv.at[matrix, home_plane],
            (target, plane),
        )

    def plane_args(matrix, to_plane, from_plane):
        return (
            slot(matrix, to_plane),
            view(matrix, 0, piece(matrix, from_plane, row)),
            plane_send.at[matrix, to_plane],
            plane_recv.at[matrix, lax.div(from_plane, 2)],
            (section, to_plane),
        )

    def peer_args(matrix, quarter_pair, from_row, to_row):
        part = view(matrix, 0, piece(matrix, 2 * quarter_pair + core, from_row))
        return (
            part,
            part,
            peer_send.at[matrix, quarter_pair, to_row],
            peer_recv.at[matrix, quarter_pair, from_row],
            peer(to_row),
        )

    def core_args(matrix, quarter_pair, at_row, from_core):
        part = view(matrix, 0, piece(matrix, 2 * quarter_pair + from_core, at_row))
        return (
            part,
            part,
            core_send.at[matrix, quarter_pair, at_row],
            core_recv.at[matrix, quarter_pair, at_row],
            partner,
        )

    def spread(matrix):
        if matrix != norms:
            loads[matrix].wait()
            for at_row in range(rows):
                height = heights[matrix]
                source = view(matrix, 1, pl.ds(at_row * height, height))
                slot(matrix, planes + at_row)[...] = source[...].astype(bf16)
        for at_row in range(rows):
            start_copy(*spread_args(matrix, at_row), here)

    def along_planes(matrix):
        @pl.when(carries)
        def _():
            for to_plane in range(planes):
                remote_copy(
                    slot(matrix, to_plane),
                    slot(matrix, to_plane),
                    spread_send.at[matrix, 0],
                    spread_recv.at[matrix, to_plane],
                    partner,
                ).wait_recv()
                start_copy(*plane_args(matrix, to_plane, plane), here)

    def between_peers(matrix):
        for pair in range(rows):
            remote_copy(*plane_args(matrix, 0, 2 * pair + core)).wait_recv()
            for to_row in range(rows):
                @pl.when(to_row != row)
                def _():
                    remote_copy(*peer_args(matrix, pair, row, to_row)).start()

            remote_copy(*core_args(matrix, pair, row, core)).start()

    def between_cores(matrix):
        for pair in range(rows):
            for from_row in range(rows):
                @pl.when(from_row != row)
                def _():
                    remote_copy(*peer_args(matrix, pair, from_row, from_row)).wait_recv()
                    remote_copy(*core_args(matrix, pair, from_row, core)).start()

    def gathered(matrix):
        for pair in range(rows):
            for at_row in range(rows):
                remote_copy(*core_args(matrix, pair, at_row, 1 - core)).wait_recv()

    def gather_sent(matrix):
        for at_row in range(rows):
            wait_sent(*spread_args(matrix, at_row), here)

        @pl.when(carries)
        def _():
            for to_plane in range(planes):
                wait_sent(*plane_args(matrix, to_plane, plane), here)

        for pair in range(rows):
            for at_row in range(rows):
                @pl.when(at_row != row)
                def _():
                    remote_copy(*peer_args(matrix, pair, row, at_row)).wait_send()

                remote_copy(*core_args(matrix, pair, at_row, core)).wait_send()

    steps_of_gather = (spread, along_planes, between_peers, between_cores, gathered)
    order = (norms, *range(norms))
    for turn_at in range(count + len(steps_of_gather) - 1):
        for depth, action in enumerate(steps_of_gather):
            if 0 <= turn_at - depth < count:
                action(order[turn_at - depth])
    for matrix in range(count):
        gather_sent(matrix)

    @pl.when(takes_tokens)
    def _():
        remote_copy(*token_copy(0, 0)).wait_recv()

    @pl.when(gives_tokens)
    def _():
        for index, target in enumerate((0, planes - 1)):
            wait_sent(*token_copy(index, target), here)

    for kind, ref in enumerate((gain_ref, bias_ref)):
        total = jnp.zeros((NORM_ROWS, width), f32)
        for quarter in range(planes):
            start = (quarter * rows + kind) * NORM_ROWS
            total = total + norm_full[start : start + NORM_ROWS, :]
        ref[...] = total.astype(bf16).astype(f32)

    table_rows = table_parts.shape[1]
    work[:table_rows, :] = jnp.zeros((table_rows, width), f32)
    work[:vocab, :] = table_ref[...]
    rest = work[:table_rows, :]
    for part in range(3):
        rounded = rest.astype(bf16)
        table_parts[part] = rounded
        rest = rest - rounded.astype(f32)
    d_qkv_ref[...] = jnp.zeros_like(d_qkv_ref)
    d_out_ref[...] = jnp.zeros_like(d_out_ref)
    d_in_ref[...] = jnp.zeros_like(d_in_ref)
    d_down_ref[...] = jnp.zeros_like(d_down_ref)
    norm_sums[...] = jnp.zeros_like(norm_sums)
    table_sum[...] = jnp.zeros_like(table_sum)

    letters = lax.broadcasted_iota(jnp.int32, (table_rows, length), 0)
    lane = lax.broadcasted_iota(jnp.int32, (length, pair_width), 1)
    lower = lane < head_size

    def shown_rows(micro):
        rows_of = token_ref[micro]
        visible = rows_of[1:2] < rows_of[2:3]
        shown = jnp.where(visible, rows_of[0:1], vocab - 1)
        return (letters == shown).astype(bf16)

    def stacked(pair):
        zero = jnp.zeros_like(pair)
        return jnp.concatenate(
            [jnp.where(lower, pair, zero), jnp.where(lower, zero, pair)], axis=0
        )

    def load_hidden(micro):
        @pl.when(stage == 0)
        def _():
            hot = shown_rows(micro)
            total = dot(hot, table_parts[2], 0, 0)
            total = total + dot(hot, table_parts[1], 0, 0)
            total = total + dot(hot, table_parts[0], 0, 0)
            work[...] = total * EMBED_GAIN

        @pl.when(stage > 0)
        def _():
            work[...] = h_in[micro].astype(f32)

    def hidden_copy(micro, target):
        slot = lax.rem(micro, 2)
        return pltpu.make_async_remote_copy(
            src_ref=h_send.at[slot],
            dst_ref=h_in.at[micro],
            send_sem=h_send_sem.at[slot],
            recv_sem=h_recv_sem.at[micro],
            device_id={"section": target[0], "dp": target[1]},
            device_id_type=MESH,
        )

    def gradient_copy(micro, target):
        slot = lax.rem(micro, 2)
        return pltpu.make_async_remote_copy(
            src_ref=g_send.at[slot],
            dst_ref=g_in.at[micro],
            send_sem=g_send_sem.at[slot],
            recv_sem=g_recv_sem.at[micro],
            device_id={"section": target[0], "dp": target[1]},
            device_id_type=MESH,
        )

    def forward(micro):
        if stages > 1:
            @pl.when(stage > 0)
            def _():
                hidden_copy(micro, behind).wait_recv()
        load_hidden(micro)
        hidden = work[...]
        unit, _ = unit_rows(hidden)
        normed = (unit * gain_ref[0:1, :] + bias_ref[0:1, :]).astype(bf16)
        packed[micro] = dot(normed, w_qkv_ref[...], 1, 0).astype(bf16)
        pairs = HEADS // 2

        def block(member, pair):
            at = member * width + pair * pair_width
            return packed[micro, :, at : at + pair_width]

        def scores_of(pair):
            query = block(0, pair) * jnp.asarray(score_scale, bf16)
            return dot(stacked(query), block(1, pair), 1, 1)

        waiting = [scores_of(pair) for pair in range(AHEAD)]
        for pair in range(pairs):
            if pair + AHEAD < pairs:
                waiting.append(scores_of(pair + AHEAD))
            scores = waiting[pair]
            largest = jnp.max(scores, axis=-1, keepdims=True)
            powers = jnp.exp(scores - largest)
            total = jnp.sum(powers, axis=-1, keepdims=True)
            attention = (powers * (1.0 / total)).astype(bf16)
            attention_out[2 * pair] = attention[:length]
            attention_out[2 * pair + 1] = attention[length:]
            found = dot(attention, block(2, pair), 1, 0)
            at = pair * pair_width
            mixed[micro, :, at : at + pair_width] = jnp.where(
                lower, found[:length], found[length:]
            ).astype(bf16)
        save = pltpu.make_async_copy(attention_out, stash_ref.at[micro], stash_sem)
        save.start()
        between = hidden + dot(mixed[micro], w_out_ref[...], 1, 0)
        high = between.astype(bf16)
        middle[2 * micro + 0] = high
        middle[2 * micro + 1] = (between - high.astype(f32)).astype(bf16)
        work[...] = between
        unit, _ = unit_rows(between)
        normed_two = (unit * gain_ref[1:2, :] + bias_ref[1:2, :]).astype(bf16)
        for at in range(0, hidden_units, FF_CHUNK):
            lifted = dot(normed_two, w_in_ref[:, at : at + FF_CHUNK], 1, 0)
            bent = (root * 0.044715) * (lifted * lifted)
            half = 0.5 + 0.5 * jnp.tanh(lifted * (bent + root))
            gelu = lifted * half
            active[micro, :, at : at + FF_CHUNK] = gelu.astype(bf16)
            slope[micro, :, at : at + FF_CHUNK] = (
                half + gelu * ((1.0 - half) * (6.0 * bent + 2.0 * root))
            ).astype(bf16)
        if stages > 1:
            @pl.when(jnp.logical_and(micro >= 2, stage < last))
            def _():
                hidden_copy(micro - 2, ahead).wait_send()
        slot = lax.rem(micro, 2)
        h_send[slot] = (work[...] + dot(active[micro], w_down_ref[...], 1, 0)).astype(bf16)
        if stages > 1:
            @pl.when(stage < last)
            def _():
                hidden_copy(micro, ahead).start()
        save.wait()

    def head(micro):
        unit, scale = unit_rows(h_send[lax.rem(micro, 2)].astype(f32))
        rounded = unit.astype(bf16)
        logits = dot(table_parts[0], rounded, 1, 1)
        logits = jnp.where(letters < vocab, logits, -jnp.inf)
        largest = jnp.max(logits, axis=0, keepdims=True)
        powers = jnp.exp(logits - largest)
        total = jnp.sum(powers, axis=0, keepdims=True)
        rows_of = token_ref[micro]
        stamp = rows_of[2:3]
        weight = jnp.where(rows_of[1:2] < stamp, 0.0, 1.0 / (length - stamp).astype(f32))
        target = (letters == rows_of[0:1]).astype(f32)
        g_logits = (weight * (powers / total - target)).astype(bf16)
        table_sum[...] += dot(g_logits, rounded, 1, 0)
        g_unit = dot(g_logits, table_parts[0], 0, 0)
        g_in[micro] = unit_back(g_unit, unit, scale).astype(bf16)

    def backward(micro):
        @pl.when(stage == last)
        def _():
            head(micro)

        if stages > 1:
            @pl.when(stage < last)
            def _():
                gradient_copy(micro, ahead).wait_recv()
        load = pltpu.make_async_copy(stash_ref.at[micro], attention_in, stash_sem)
        load.start()
        g_out = g_in[micro]
        for at in range(0, hidden_units, FF_CHUNK):
            g_active = dot(g_out, w_down_ref[at : at + FF_CHUNK, :], 1, 1)
            slope[micro, :, at : at + FF_CHUNK] = (
                g_active * slope[micro, :, at : at + FF_CHUNK].astype(f32)
            ).astype(bf16)
        g_normed = dot(slope[micro], w_in_ref[...], 1, 1)
        unit, scale = unit_rows(middle[2 * micro + 0].astype(f32) + middle[2 * micro + 1].astype(f32))
        middle[2 * micro + 0] = (unit * gain_ref[1:2, :] + bias_ref[1:2, :]).astype(bf16)
        norm_sums[1] += fold_rows(g_normed * unit)
        norm_sums[3] += fold_rows(g_normed)
        g_middle = g_out.astype(f32) + unit_back(g_normed * gain_ref[1:2, :], unit, scale)
        g_attended = g_middle.astype(bf16)
        middle[2 * micro + 1] = g_attended
        g_mixed = dot(g_attended, w_out_ref[...], 1, 1).astype(bf16)
        load_hidden(micro)
        load.wait()
        pairs = HEADS // 2

        def block(member, pair):
            at = member * width + pair * pair_width
            return packed[micro, :, at : at + pair_width]

        def put(member, pair, value):
            at = member * width + pair * pair_width
            packed[micro, :, at : at + pair_width] = value.astype(bf16)

        def g_attention_of(pair):
            at = pair * pair_width
            g_pair = stacked(g_mixed[:, at : at + pair_width])
            return g_pair, dot(g_pair, block(2, pair), 1, 1)

        waiting = [g_attention_of(pair) for pair in range(AHEAD)]
        for pair in range(pairs):
            if pair + AHEAD < pairs:
                waiting.append(g_attention_of(pair + AHEAD))
            g_pair, g_attention = waiting[pair]
            low = attention_in[2 * pair : 2 * pair + 2].reshape(2 * length, length)
            attention = low.astype(f32)
            inner = jnp.sum(attention * g_attention, axis=-1, keepdims=True)
            g_scores = (attention * (g_attention - inner)).astype(bf16)
            key, query = block(1, pair), stacked(block(0, pair))
            g_values = dot(low, g_pair, 0, 0)
            g_queries = dot(g_scores, key, 1, 0)
            g_keys = dot(g_scores, query, 0, 0)
            put(0, pair, jnp.where(lower, g_queries[:length], g_queries[length:]) * score_scale)
            put(1, pair, g_keys * score_scale)
            put(2, pair, g_values)
        g_normed = dot(packed[micro], w_qkv_ref[...], 1, 1)
        unit, scale = unit_rows(work[...])
        h_in[micro] = (unit * gain_ref[0:1, :] + bias_ref[0:1, :]).astype(bf16)
        norm_sums[0] += fold_rows(g_normed * unit)
        norm_sums[2] += fold_rows(g_normed)
        g_hidden = g_middle + unit_back(g_normed * gain_ref[0:1, :], unit, scale)

        @pl.when(stage == 0)
        def _():
            hot = shown_rows(micro)
            high = g_hidden.astype(bf16)
            low = (g_hidden - high.astype(f32)).astype(bf16)
            table_sum[...] += EMBED_GAIN * (dot(hot, high, 1, 0) + dot(hot, low, 1, 0))

        if stages > 1:
            @pl.when(stage > 0)
            def _():
                @pl.when(micro >= 2)
                def _():
                    gradient_copy(micro - 2, behind).wait_send()

                g_send[lax.rem(micro, 2)] = g_hidden.astype(bf16)
                gradient_copy(micro, behind).start()

    def weights(micro):
        d_down_ref[...] += dot(active[micro], g_in[micro], 0, 0)
        d_in_ref[...] += dot(middle[2 * micro + 0], slope[micro], 0, 0)
        d_out_ref[...] += dot(mixed[micro], middle[2 * micro + 1], 0, 0)
        d_qkv_ref[...] += dot(h_in[micro], packed[micro], 0, 0)

    steps = max(2 * last + micro_count, last + 2 * micro_count)

    def step(index, carry):
        f_micro = index - stage
        b_micro = index - (2 * last - stage)
        w_micro = index - jnp.maximum(stage + micro_count, 2 * last - stage)

        @pl.when(jnp.logical_and(f_micro >= 0, f_micro < micro_count))
        def _():
            forward(f_micro)

        @pl.when(jnp.logical_and(b_micro >= 0, b_micro < micro_count))
        def _():
            backward(b_micro)

        @pl.when(jnp.logical_and(w_micro >= 0, w_micro < micro_count))
        def _():
            weights(w_micro)

        return carry

    lax.fori_loop(0, steps, step, 0)

    if stages > 1:
        for micro in range(max(micro_count - 2, 0), micro_count):
            @pl.when(stage < last)
            def _():
                hidden_copy(micro, ahead).wait_send()

            @pl.when(stage > 0)
            def _():
                gradient_copy(micro, behind).wait_send()

    def table_copy(source, target, send, recv, device):
        return remote_copy(source, target, table_send.at[send], table_recv.at[recv], device)

    def lane_copy():
        return table_copy(table_sum, table_slots.at[0], 0, 0, (section, 0))

    def table_core_copy():
        return table_copy(table_sum, table_slots.at[1], 1, 1, partner)

    def table_peer_copy(from_row, to_row):
        return table_copy(
            table_sum, table_slots.at[2 + from_row], 2 + to_row, 2 + from_row, peer(to_row)
        )

    def table_down_copy(to_plane):
        return table_copy(
            d_table_ref, d_table_ref, 2 + rows + to_plane, 2 + rows, (section, to_plane)
        )

    def table_side_copy(to_place):
        target = 2 * chip_of(to_place, row, per_plane) + core
        return table_copy(
            d_table_ref, d_table_ref, 2 + rows + planes + to_place, 2 + rows, (target, plane)
        )

    @pl.when(stage == last)
    def _():
        lane_copy().start()

    def table_cores():
        @pl.when(stage == 0)
        def _():
            lane_copy().wait_recv()
            table_sum[...] += table_slots[0]
            table_core_copy().start()

    def table_peers():
        @pl.when(stage == 0)
        def _():
            table_core_copy().wait()
            table_sum[...] += table_slots[1]
            for to_row in range(rows):
                @pl.when(to_row != row)
                def _():
                    table_peer_copy(row, to_row).start()

    def table_side():
        for to_place in range(1, per_plane):
            table_side_copy(to_place).start()

    def table_down():
        @pl.when(stage == 0)
        def _():
            total = table_sum[...]
            for from_row in range(rows):
                @pl.when(from_row != row)
                def _():
                    table_peer_copy(from_row, from_row).wait_recv()

                total = total + jnp.where(from_row != row, table_slots[2 + from_row], 0.0)
            d_table_ref[...] = total
            for to_plane in range(1, planes):
                table_down_copy(to_plane).start()
            table_side()

    def table_done():
        @pl.when(place > 0)
        def _():
            table_side_copy(0).wait_recv()

        @pl.when(stage == last)
        def _():
            lane_copy().wait_send()

        @pl.when(stage == 0)
        def _():
            for to_row in range(rows):
                @pl.when(to_row != row)
                def _():
                    table_peer_copy(row, to_row).wait_send()

            for to_plane in range(1, planes):
                table_down_copy(to_plane).wait_send()

        @pl.when(place == 0)
        def _():
            for to_place in range(1, per_plane):
                table_side_copy(to_place).wait_send()

    for kind in range(2):
        totals = [
            jnp.sum(norm_sums[2 * kind + member], axis=0, keepdims=True) for member in range(2)
        ]
        block = jnp.concatenate(totals + [jnp.zeros((NORM_ROWS - 2, width), f32)], axis=0)
        for quarter in range(planes):
            start = (quarter * rows + kind) * NORM_ROWS
            d_norm_ref[start : start + NORM_ROWS, :] = block

    pl.semaphore_signal(
        core_free, inc=1, device_id={"section": partner[0], "dp": partner[1]}, device_id_type=MESH
    )
    for at_row in range(rows):
        @pl.when(at_row != row)
        def _():
            far = peer(at_row)
            pl.semaphore_signal(
                peer_free, inc=1, device_id={"section": far[0], "dp": far[1]}, device_id_type=MESH
            )

    def core_sum_args(matrix, pair, at_row):
        index = pair * rows + at_row
        return (
            slot(matrix, index),
            slot(matrix, rows * rows + index),
            core_send.at[matrix, pair, at_row],
            core_recv.at[matrix, pair, at_row],
            partner,
        )

    def peer_sum_args(matrix, pair, from_row, to_row):
        return (
            slot(matrix, 2 * rows * rows + pair * rows + to_row),
            slot(matrix, 3 * rows * rows + pair * rows + from_row),
            peer_send.at[matrix, pair, to_row],
            peer_recv.at[matrix, pair, from_row],
            peer(to_row),
        )

    def total_args(matrix, pair):
        height = heights[matrix]
        return (
            slot(matrix, 2 * rows * rows + pair * rows + row),
            view(matrix, 3, pl.ds(pl.multiple_of(row * height, height), height)),
            total_send.at[matrix, pair],
            total_recv.at[matrix, row],
            (stage, 2 * pair + core),
        )

    def give_core(matrix):
        for pair in range(rows):
            for at_row in range(rows):
                args = core_sum_args(matrix, pair, at_row)
                part = view(matrix, 1, piece(matrix, 2 * pair + 1 - core, at_row))
                args[0][...] = part[...].astype(args[0].dtype)
                remote_copy(*args).start()

    def give_peers(matrix):
        for pair in range(rows):
            for at_row in range(rows):
                remote_copy(*core_sum_args(matrix, pair, at_row)).wait_recv()
                landed = slot(matrix, rows * rows + pair * rows + at_row)
                part = view(matrix, 1, piece(matrix, 2 * pair + core, at_row))
                total = part[...] + landed[...].astype(f32)

                @pl.when(at_row != row)
                def _():
                    args = peer_sum_args(matrix, pair, row, at_row)
                    args[0][...] = total.astype(args[0].dtype)
                    remote_copy(*args).start()

                @pl.when(at_row == row)
                def _():
                    part[...] = total

    def give_totals(matrix):
        for pair in range(rows):
            part = view(matrix, 1, piece(matrix, 2 * pair + core, row))
            for from_row in range(rows):
                @pl.when(from_row != row)
                def _():
                    remote_copy(*peer_sum_args(matrix, pair, from_row, from_row)).wait_recv()
                    landed = slot(matrix, 3 * rows * rows + pair * rows + from_row)
                    part[...] += landed[...].astype(f32)

            args = total_args(matrix, pair)
            args[0][...] = part[...].astype(args[0].dtype)
            start_copy(*args, here)

    def finish(matrix):
        height = heights[matrix]
        for from_row in range(rows):
            part = view(matrix, 3, pl.ds(from_row * height, height))
            remote_copy(
                part, part, total_send.at[matrix, 0], total_recv.at[matrix, from_row], partner
            ).wait_recv()
        for pair in range(rows):
            for at_row in range(rows):
                remote_copy(*core_sum_args(matrix, pair, at_row)).wait_send()

                @pl.when(at_row != row)
                def _():
                    remote_copy(*peer_sum_args(matrix, pair, row, at_row)).wait_send()

            wait_sent(*total_args(matrix, pair), here)

    order = tuple(reversed(range(count)))
    table_cores()
    pl.semaphore_wait(core_free, 1)
    for position in range(count + 3):
        if position < count:
            give_core(order[position])
        if position == 1:
            table_peers()
            pl.semaphore_wait(peer_free, rows - 1)
        if 0 <= position - 1 < count:
            give_peers(order[position - 1])
        if 0 <= position - 3 < count:
            give_totals(order[position - 3])
        if position == 4:
            table_down()

    @pl.when(jnp.logical_and(place == 0, plane > 0))
    def _():
        table_down_copy(0).wait_recv()
        table_side()

    for matrix in order:
        finish(matrix)
    table_done()


def run_pipeline(stages, planes, token_ids, order, timesteps, table, gain, bias, *shards):
    w_qkv, w_out, w_in, w_down = shards
    micro_count, _, length = token_ids.shape
    width = table.shape[1]
    hidden_units = w_in.shape[2]
    rows = planes // 2
    table_rows = -(-table.shape[0] // 32) * 32
    bf16, f32 = jnp.bfloat16, jnp.float32
    vmem = pl.BlockSpec(memory_space=pltpu.VMEM)
    anywhere = pl.BlockSpec(memory_space=pl.ANY)
    tokens = (micro_count, 3, length)
    norm_shard = (rows * NORM_ROWS, width)
    full = [(shard.shape[1] * planes, shard.shape[2]) for shard in shards]
    norm_full = (planes * rows * NORM_ROWS, width)
    outs = (
        jax.ShapeDtypeStruct((table_rows, width), f32),
        jax.ShapeDtypeStruct(norm_shard, f32),
        *(jax.ShapeDtypeStruct(shard.shape[1:], bf16) for shard in shards),
        jax.ShapeDtypeStruct((micro_count, HEADS, length, length), bf16),
    )
    rows_shape = (micro_count, length, width)
    units = 8
    pieces = (units, rows, rows)
    return pl.pallas_call(
        functools.partial(pipeline_kernel, stages, planes),
        out_shape=outs,
        in_specs=[vmem] * 6 + [anywhere] * 4,
        out_specs=[vmem] * 6 + [anywhere],
        scratch_shapes=[
            pltpu.VMEM(tokens, jnp.int32),
            pltpu.VMEM(norm_shard, f32),
            pltpu.VMEM(tokens, jnp.int32),
            pltpu.VMEM(rows_shape, bf16),
            pltpu.VMEM(rows_shape, bf16),
            pltpu.VMEM((2, length, width), bf16),
            pltpu.VMEM((2, length, width), bf16),
            pltpu.VMEM((micro_count, length, 3 * width), bf16),
            pltpu.VMEM(rows_shape, bf16),
            pltpu.VMEM((2 * micro_count, length, width), bf16),
            pltpu.VMEM((micro_count, length, hidden_units), bf16),
            pltpu.VMEM((micro_count, length, hidden_units), bf16),
            pltpu.VMEM((HEADS, length, length), bf16),
            pltpu.VMEM((HEADS, length, length), bf16),
            pltpu.VMEM((length, width), f32),
            pltpu.VMEM((3, table_rows, width), bf16),
            pltpu.VMEM((4, 8, width), f32),
            pltpu.VMEM((table_rows, width), f32),
            pltpu.VMEM((4 * rows * rows, NORM_ROWS, width), f32),
            pltpu.VMEM(norm_full, f32),
            *(pltpu.VMEM(shape, bf16) for shape in full),
            pltpu.VMEM((NORM_ROWS, width), f32),
            pltpu.VMEM((NORM_ROWS, width), f32),
            pltpu.VMEM(norm_full, f32),
            *(pltpu.VMEM(shape, f32) for shape in full),
            pltpu.SemaphoreType.DMA((2,)),
            pltpu.SemaphoreType.DMA((micro_count,)),
            pltpu.SemaphoreType.DMA((2,)),
            pltpu.SemaphoreType.DMA((micro_count,)),
            pltpu.SemaphoreType.DMA,
            pltpu.SemaphoreType.DMA((2,)),
            pltpu.SemaphoreType.DMA,
            pltpu.SemaphoreType.DMA((units,)),
            pltpu.SemaphoreType.DMA((units, rows)),
            pltpu.SemaphoreType.DMA((units, planes)),
            pltpu.SemaphoreType.DMA((units, planes)),
            pltpu.SemaphoreType.DMA((units, rows)),
            pltpu.SemaphoreType.DMA(pieces),
            pltpu.SemaphoreType.DMA(pieces),
            pltpu.SemaphoreType.DMA(pieces),
            pltpu.SemaphoreType.DMA(pieces),
            pltpu.SemaphoreType.REGULAR,
            pltpu.SemaphoreType.REGULAR,
            pltpu.SemaphoreType.DMA((units, rows)),
            pltpu.SemaphoreType.DMA((units, rows)),
            pltpu.VMEM((2 + rows, table_rows, width), f32),
            pltpu.SemaphoreType.DMA((2 + rows + planes + stages // planes,)),
            pltpu.SemaphoreType.DMA((3 + rows,)),
        ],
        compiler_params=pltpu.CompilerParams(
            vmem_limit_bytes=63 << 20, collective_id=0, has_side_effects=True
        ),
    )(token_ids, order, timesteps, table, gain, bias, w_qkv, w_out, w_in, w_down)


def finish_kernel(planes, stages, *refs):
    table_ref, norm_ref, *totals = refs[:6]
    table_part, gain_part, bias_part, *results = refs[6:]
    section, plane = lax.axis_index("section"), lax.axis_index("dp")
    for total, result in zip(totals, results):
        result[0] = total[...].astype(jnp.float32)

    @pl.when(pl.program_id(0) == 0)
    def _():
        vocab, columns = table_part.shape
        part = jnp.zeros((vocab, columns), jnp.float32)
        for at in range(stages):
            block = table_ref[:vocab, at * columns : (at + 1) * columns]
            part = jnp.where(section == at, block, part)
        table_part[...] = part
        share = gain_part.shape[2]
        for kind, result in enumerate((gain_part, bias_part)):
            part = jnp.zeros((2, share), jnp.float32)
            for at in range(planes):
                start = kind * NORM_ROWS
                block = norm_ref[start : start + 2, at * share : (at + 1) * share]
                part = jnp.where(plane == at, block, part)
            result[0] = part


def run_finish(stages, planes, vocab, share, sums):
    f32 = jnp.float32
    steps = 4
    whole = [pl.BlockSpec(value.shape, lambda i: (0, 0)) for value in sums[:2]]
    blocks = [
        pl.BlockSpec((value.shape[0] // steps, value.shape[1]), lambda i: (i, 0))
        for value in sums[2:]
    ]
    out_blocks = [
        pl.BlockSpec((1, value.shape[0] // steps, value.shape[1]), lambda i: (0, i, 0))
        for value in sums[2:]
    ]
    columns = sums[0].shape[1] // stages
    return pl.pallas_call(
        functools.partial(finish_kernel, planes, stages),
        grid=(steps,),
        out_shape=(
            jax.ShapeDtypeStruct((vocab, columns), f32),
            jax.ShapeDtypeStruct((1, 2, share), f32),
            jax.ShapeDtypeStruct((1, 2, share), f32),
            *(jax.ShapeDtypeStruct((1, *value.shape), f32) for value in sums[2:]),
        ),
        in_specs=whole + blocks,
        out_specs=[
            pl.BlockSpec((vocab, columns), lambda i: (0, 0)),
            pl.BlockSpec((1, 2, share), lambda i: (0, 0, 0)),
            pl.BlockSpec((1, 2, share), lambda i: (0, 0, 0)),
            *out_blocks,
        ],
    )(*sums)


def body(token_ids, order, timesteps, table, norm_gain, norm_bias, w_qkv, w_out, w_in, w_down):
    stages, planes = lax.axis_size("section"), lax.axis_size("dp")
    sums = run_pipeline(
        stages,
        planes,
        token_ids,
        order,
        timesteps,
        table,
        norm_gain,
        norm_bias,
        w_qkv,
        w_out,
        w_in,
        w_down,
    )
    return tuple(run_finish(stages, planes, table.shape[0], norm_gain.shape[2], sums[:6]))


def solution(mesh):
    in_specs = (
        P(None, "dp", None),
        P(None, "dp", None),
        P(None, "dp"),
        P(),
        P("section", None, "dp"),
        P("section", None, "dp"),
        P("section", "dp", None),
        P("section", "dp", None),
        P("section", "dp", None),
        P("section", "dp", None),
    )
    out_specs = (
        P(None, "section"),
        P("section", None, "dp"),
        P("section", None, "dp"),
        P("section", "dp", None),
        P("section", "dp", None),
        P("section", "dp", None),
        P("section", "dp", None),
    )
    return jax.shard_map(body, mesh=mesh, in_specs=in_specs, out_specs=out_specs, check_vma=False)
```

```python
import functools
import math

import jax
import jax.numpy as jnp
from jax import lax
from jax.experimental import pallas as pl
from jax.experimental.pallas import tpu as pltpu
from jax.sharding import PartitionSpec as P

HEADS = 8
EPSILON = 1e-05
EMBED_GAIN = 16.0
FF_CHUNK = 512
AHEAD = 3
WARM = 3
NORM_ROWS = 8
MESH = pl.DeviceIdType.MESH


def dot(left, right, left_dim, right_dim):
    return lax.dot_general(
        left, right, (((left_dim,), (right_dim,)), ((), ())), preferred_element_type=jnp.float32
    )


def unit_rows(values):
    average = jnp.mean(values, axis=-1, keepdims=True)
    centered = values - average
    variance = jnp.mean(centered * centered, axis=-1, keepdims=True)
    scale = lax.rsqrt(variance + EPSILON)
    return centered * scale, scale


def unit_back(gradient, unit, scale):
    first = jnp.mean(gradient, axis=-1, keepdims=True)
    second = jnp.mean(gradient * unit, axis=-1, keepdims=True)
    return scale * (gradient - first - unit * second)


def fold_rows(values):
    rows, columns = values.shape
    return jnp.sum(values.reshape(rows // 8, 8, columns), axis=0)


def chip_of(place, row, per_plane):
    return row * per_plane + lax.rem(place - lax.rem(row, per_plane) + per_plane, per_plane)


def start_copy(src, dst, send_sem, recv_sem, device, here):
    section, plane = device
    same = jnp.logical_and(section == here[0], plane == here[1])

    @pl.when(same)
    def _():
        pltpu.make_async_copy(src, dst, recv_sem).start()

    @pl.when(jnp.logical_not(same))
    def _():
        remote_copy(src, dst, send_sem, recv_sem, device).start()


def wait_sent(src, dst, send_sem, recv_sem, device, here):
    section, plane = device
    same = jnp.logical_and(section == here[0], plane == here[1])

    @pl.when(jnp.logical_not(same))
    def _():
        remote_copy(src, dst, send_sem, recv_sem, device).wait_send()


def remote_copy(src, dst, send_sem, recv_sem, device):
    return pltpu.make_async_remote_copy(
        src_ref=src,
        dst_ref=dst,
        send_sem=send_sem,
        recv_sem=recv_sem,
        device_id={"section": device[0], "dp": device[1]},
        device_id_type=MESH,
    )


def pipeline_kernel(
    stages,
    planes,
    ids_ref,
    order_ref,
    stamp_ref,
    table_ref,
    gain_shard,
    bias_shard,
    qkv_shard,
    out_shard,
    in_shard,
    down_shard,
    d_table_ref,
    norm_total,
    qkv_total,
    out_total,
    in_total,
    down_total,
    stash_ref,
    token_in_ref,
    norm_shard,
    token_ref,
    h_in,
    g_in,
    h_send,
    g_send,
    packed,
    mixed,
    middle,
    active,
    slope,
    attention_kept,
    work,
    table_parts,
    norm_sums,
    table_sum,
    norm_slots,
    norm_full,
    w_qkv_ref,
    w_out_ref,
    w_in_ref,
    w_down_ref,
    gain_ref,
    bias_ref,
    d_qkv_ref,
    d_out_ref,
    d_in_ref,
    d_down_ref,
    h_send_sem,
    h_recv_sem,
    g_send_sem,
    g_recv_sem,
    stash_sem,
    token_send_sem,
    token_recv_sem,
    load_sem,
    spread_send,
    spread_recv,
    plane_send,
    plane_recv,
    peer_send,
    peer_recv,
    core_send,
    core_recv,
    core_free,
    peer_free,
    total_send,
    total_recv,
    table_slots,
    table_send,
    table_recv,
    more_norm,
    more_qkv,
    more_out,
    more_in,
    more_down,
    direct_recv,
):
    micro_count, _, length = token_ref.shape
    vocab, width = table_ref.shape
    hidden_units = w_in_ref.shape[1]
    head_size = width // HEADS
    score_scale = 1.0 / math.sqrt(head_size)
    root = math.sqrt(2.0 / math.pi)
    pair_width = 2 * head_size
    bf16, f32 = jnp.bfloat16, jnp.float32

    per_plane, rows = stages // planes, planes // 2
    section, plane = lax.axis_index("section"), lax.axis_index("dp")
    here = (section, plane)
    chip, core = lax.div(section, 2), lax.rem(section, 2)
    row = lax.div(chip, per_plane)
    place = lax.rem(lax.rem(chip, per_plane) + row, per_plane)
    odd = lax.rem(plane, 2)
    turn = jnp.where(odd == 0, place, per_plane - 1 - place)
    stage = plane * per_plane + turn
    last = stages - 1
    lane_row = lax.rem(row - lax.rem(place, rows) * core + rows, rows)
    lane_index = 2 * lane_row + core

    def next_device():
        step = jnp.where(odd == 0, 1, -1)
        near_place = place + step
        near_row = lax.rem(row + core * step + rows, rows)
        near = 2 * chip_of(near_place + per_plane, near_row, per_plane) + core
        stays = turn < per_plane - 1
        return jnp.where(stays, near, section), jnp.where(stays, plane, plane + 1)

    def previous_device():
        step = jnp.where(odd == 0, -1, 1)
        near_place = place + step
        near_row = lax.rem(row + core * step + rows, rows)
        near = 2 * chip_of(near_place + per_plane, near_row, per_plane) + core
        stays = turn > 0
        return jnp.where(stays, near, section), jnp.where(stays, plane, plane - 1)

    ahead, behind = next_device(), previous_device()
    partner = (section + 1 - 2 * core, plane)

    def layer_device(layer, at_row, at_core):
        at_plane, at_turn = lax.div(layer, per_plane), lax.rem(layer, per_plane)
        at_place = jnp.where(lax.rem(at_plane, 2) == 0, at_turn, per_plane - 1 - at_turn)
        return 2 * chip_of(at_place, at_row, per_plane) + at_core, at_plane

    def layer_here(at_plane):
        at_turn = jnp.where(at_plane % 2 == 0, place, per_plane - 1 - place)
        return at_plane * per_plane + at_turn

    def peer(at_row):
        return layer_device(stage, at_row, core)

    home_plane = lax.div(section, per_plane)
    carries = lax.rem(plane, 2) == core

    barrier = pltpu.get_barrier_semaphore()
    greetings = []

    def greet(device, wanted=True):
        same = jnp.logical_and(device[0] == section, device[1] == plane)
        wanted = jnp.logical_and(wanted, jnp.logical_not(same))
        greetings.append(jnp.where(wanted, 1, 0))

        @pl.when(wanted)
        def _():
            pl.semaphore_signal(
                barrier,
                inc=1,
                device_id={"section": device[0], "dp": device[1]},
                device_id_type=MESH,
            )

    for other in range(planes):
        greet((section, other))
        greet((layer_here(other), plane), carries)
    for at_row in range(rows):
        owner = layer_device(section, at_row, lax.rem(plane, 2))
        greet((owner[0], plane))
        greet(owner)
        greet((stage, 2 * at_row + core))
        greet(peer(at_row))
    for at_place in range(per_plane):
        greet((2 * chip_of(at_place, row, per_plane) + core, plane))
    greet(partner)
    greet(ahead, stage < last)
    greet(behind, stage > 0)
    matrices = []
    for parts, *members in (
        (2, w_qkv_ref, d_qkv_ref, qkv_shard, qkv_total, packed, more_qkv),
        (1, w_out_ref, d_out_ref, out_shard, out_total, mixed, more_out),
        (2, w_in_ref, d_in_ref, in_shard, in_total, active, more_in),
        (2, w_down_ref, d_down_ref, down_shard, down_total, middle, more_down),
        (1, norm_full, norm_full, norm_shard, norm_total, norm_slots, more_norm),
    ):
        window = members[0].shape[1] // parts
        for part in range(parts):
            matrices.append((*members, pl.ds(part * window, window)))
    count = len(matrices)
    norms = count - 1
    heights = [matrix[0].shape[0] // (planes * rows) for matrix in matrices]

    def view(matrix, member, rows_of):
        return matrices[matrix][member].at[rows_of, matrices[matrix][-1]]

    def slot(matrix, index):
        buffer, height = matrices[matrix][4], heights[matrix]
        per_block = buffer.shape[1] // height
        block, inside = index // per_block, index % per_block
        if not isinstance(inside, int):
            inside = pl.multiple_of(inside * height, height)
        else:
            inside = inside * height
        return buffer.at[block, pl.ds(inside, height), matrices[matrix][-1]]

    def piece(matrix, quarter, at_row):
        height = heights[matrix]
        return pl.ds(pl.multiple_of((quarter * rows + at_row) * height, height), height)

    loads = []
    for matrix in range(norms):
        shard, window = matrices[matrix][2], matrices[matrix][-1]
        loads.append(
            pltpu.make_async_copy(
                shard.at[0, :, window],
                view(matrix, 1, pl.ds(0, shard.shape[1])),
                load_sem.at[matrix],
            )
        )
        loads[-1].start()

    for micro in range(micro_count):
        token_in_ref[micro, 0:1, :] = ids_ref[micro]
        token_in_ref[micro, 1:2, :] = order_ref[micro]
        token_in_ref[micro, 2:3, :] = jnp.full((1, length), stamp_ref[micro, 0], jnp.int32)
    norm_shard[...] = jnp.zeros_like(norm_shard)
    share = gain_shard.shape[2]
    columns = lax.broadcasted_iota(jnp.int32, (2, width), 1)
    mine = jnp.logical_and(columns >= plane * share, columns < (plane + 1) * share)
    for kind, shard in enumerate((gain_shard, bias_shard)):
        spread_out = jnp.concatenate([shard[0]] * planes, axis=1)
        norm_shard[kind * NORM_ROWS : kind * NORM_ROWS + 2, :] = jnp.where(mine, spread_out, 0.0)

    table_rows = table_parts.shape[1]
    work[:table_rows, :] = jnp.zeros((table_rows, width), f32)
    work[:vocab, :] = table_ref[...]
    rest = work[:table_rows, :]
    for part in range(3):
        rounded = rest.astype(bf16)
        table_parts[part] = rounded
        rest = rest - rounded.astype(f32)
    norm_sums[...] = jnp.zeros_like(norm_sums)
    table_sum[...] = jnp.zeros_like(table_sum)
    for matrix in range(norms):
        loads[matrix].wait()
        for at_row in range(rows):
            source = view(matrix, 1, pl.ds(at_row * heights[matrix], heights[matrix]))
            slot(matrix, planes + at_row)[...] = source[...].astype(bf16)
    pl.semaphore_wait(barrier, sum(greetings))

    gives_tokens = jnp.logical_and(place == 0, lane_index == plane)
    takes_tokens = jnp.logical_or(stage == 0, stage == last)

    def token_copy(index, target):
        return (
            token_in_ref,
            token_ref,
            token_send_sem.at[index],
            token_recv_sem,
            (section, target),
        )

    @pl.when(gives_tokens)
    def _():
        for index, target in enumerate((0, planes - 1)):
            start_copy(*token_copy(index, target), here)

    def spread_args(matrix, at_row):
        target, _ = layer_device(section, at_row, lax.rem(plane, 2))
        if matrix == norms:
            source = norm_shard.at[pl.ds(at_row * NORM_ROWS, NORM_ROWS)]
        else:
            source = slot(matrix, planes + at_row)
        return (
            source,
            slot(matrix, home_plane),
            spread_send.at[matrix, at_row],
            spread_recv.at[matrix, home_plane],
            (target, plane),
        )

    def plane_args(matrix, to_plane, from_plane):
        return (
            slot(matrix, to_plane),
            view(matrix, 0, piece(matrix, from_plane, row)),
            plane_send.at[matrix, to_plane],
            plane_recv.at[matrix, lax.div(from_plane, 2)],
            (section, to_plane),
        )

    def peer_args(matrix, quarter_pair, from_row, to_row):
        part = view(matrix, 0, piece(matrix, 2 * quarter_pair + core, from_row))
        return (
            part,
            part,
            peer_send.at[matrix, quarter_pair, to_row],
            peer_recv.at[matrix, quarter_pair, from_row],
            peer(to_row),
        )

    def core_args(matrix, quarter_pair, at_row, from_core):
        part = view(matrix, 0, piece(matrix, 2 * quarter_pair + from_core, at_row))
        return (
            part,
            part,
            core_send.at[matrix, quarter_pair, at_row],
            core_recv.at[matrix, quarter_pair, at_row],
            partner,
        )

    def spread(matrix):
        for at_row in range(rows):
            start_copy(*spread_args(matrix, at_row), here)

    def along_planes(matrix):
        @pl.when(carries)
        def _():
            for to_plane in range(planes):
                remote_copy(
                    slot(matrix, to_plane),
                    slot(matrix, to_plane),
                    spread_send.at[matrix, 0],
                    spread_recv.at[matrix, to_plane],
                    partner,
                ).wait_recv()
                start_copy(*plane_args(matrix, to_plane, plane), here)

    def between_peers(matrix):
        for pair in range(rows):
            remote_copy(*plane_args(matrix, 0, 2 * pair + core)).wait_recv()
            for to_row in range(rows):
                @pl.when(to_row != row)
                def _():
                    remote_copy(*peer_args(matrix, pair, row, to_row)).start()

            remote_copy(*core_args(matrix, pair, row, core)).start()

    def between_cores(matrix):
        for pair in range(rows):
            for from_row in range(rows):
                @pl.when(from_row != row)
                def _():
                    remote_copy(*peer_args(matrix, pair, from_row, from_row)).wait_recv()
                    remote_copy(*core_args(matrix, pair, from_row, core)).start()

    def gathered(matrix):
        for pair in range(rows):
            for at_row in range(rows):
                remote_copy(*core_args(matrix, pair, at_row, 1 - core)).wait_recv()

    def gather_sent(matrix):
        for at_row in range(rows):
            wait_sent(*spread_args(matrix, at_row), here)

        @pl.when(carries)
        def _():
            for to_plane in range(planes):
                wait_sent(*plane_args(matrix, to_plane, plane), here)

        for pair in range(rows):
            for at_row in range(rows):
                @pl.when(at_row != row)
                def _():
                    remote_copy(*peer_args(matrix, pair, row, at_row)).wait_send()

                remote_copy(*core_args(matrix, pair, at_row, core)).wait_send()

    steps_of_gather = (spread, along_planes, between_peers, between_cores, gathered)
    order = (norms, *range(norms))
    for turn_at in range(count + len(steps_of_gather) - 1):
        for depth, action in enumerate(steps_of_gather):
            if 0 <= turn_at - depth < count:
                action(order[turn_at - depth])
        if 1 <= turn_at <= 4:
            sums = (d_qkv_ref, d_out_ref, d_in_ref, d_down_ref)[turn_at - 1]
            sums[...] = jnp.zeros_like(sums)
    for matrix in range(count):
        gather_sent(matrix)

    @pl.when(takes_tokens)
    def _():
        remote_copy(*token_copy(0, 0)).wait_recv()

    @pl.when(gives_tokens)
    def _():
        for index, target in enumerate((0, planes - 1)):
            wait_sent(*token_copy(index, target), here)

    for kind, ref in enumerate((gain_ref, bias_ref)):
        total = jnp.zeros((NORM_ROWS, width), f32)
        for quarter in range(planes):
            start = (quarter * rows + kind) * NORM_ROWS
            total = total + norm_full[start : start + NORM_ROWS, :]
        ref[...] = total.astype(bf16).astype(f32)

    letters = lax.broadcasted_iota(jnp.int32, (table_rows, length), 0)
    lane = lax.broadcasted_iota(jnp.int32, (length, pair_width), 1)
    lower = lane < head_size

    def shown_rows(micro):
        rows_of = token_ref[micro]
        visible = rows_of[1:2] < rows_of[2:3]
        shown = jnp.where(visible, rows_of[0:1], vocab - 1)
        return (letters == shown).astype(bf16)

    def stacked(pair):
        zero = jnp.zeros_like(pair)
        return jnp.concatenate(
            [jnp.where(lower, pair, zero), jnp.where(lower, zero, pair)], axis=0
        )

    def load_hidden(micro):
        @pl.when(stage == 0)
        def _():
            hot = shown_rows(micro)
            total = dot(hot, table_parts[2], 0, 0)
            total = total + dot(hot, table_parts[1], 0, 0)
            total = total + dot(hot, table_parts[0], 0, 0)
            work[...] = total * EMBED_GAIN

        @pl.when(stage > 0)
        def _():
            work[...] = h_in[micro].astype(f32)

    def hidden_copy(micro, target):
        slot = lax.rem(micro, 2)
        return pltpu.make_async_remote_copy(
            src_ref=h_send.at[slot],
            dst_ref=h_in.at[micro],
            send_sem=h_send_sem.at[slot],
            recv_sem=h_recv_sem.at[micro],
            device_id={"section": target[0], "dp": target[1]},
            device_id_type=MESH,
        )

    def gradient_copy(micro, target):
        slot = lax.rem(micro, 2)
        return pltpu.make_async_remote_copy(
            src_ref=g_send.at[slot],
            dst_ref=g_in.at[micro],
            send_sem=g_send_sem.at[slot],
            recv_sem=g_recv_sem.at[micro],
            device_id={"section": target[0], "dp": target[1]},
            device_id_type=MESH,
        )

    def forward(micro):
        if stages > 1:
            @pl.when(stage > 0)
            def _():
                hidden_copy(micro, behind).wait_recv()
        load_hidden(micro)
        hidden = work[...]
        unit, _ = unit_rows(hidden)
        normed = (unit * gain_ref[0:1, :] + bias_ref[0:1, :]).astype(bf16)
        packed[micro] = dot(normed, w_qkv_ref[...], 1, 0).astype(bf16)
        pairs = HEADS // 2

        def block(member, pair):
            at = member * width + pair * pair_width
            return packed[micro, :, at : at + pair_width]

        def scores_of(pair):
            query = block(0, pair) * jnp.asarray(score_scale, bf16)
            return dot(stacked(query), block(1, pair), 1, 1)

        waiting = [scores_of(pair) for pair in range(AHEAD)]
        for pair in range(pairs):
            if pair + AHEAD < pairs:
                waiting.append(scores_of(pair + AHEAD))
            scores = waiting[pair]
            largest = jnp.max(scores, axis=-1, keepdims=True)
            powers = jnp.exp(scores - largest)
            total = jnp.sum(powers, axis=-1, keepdims=True)
            attention = (powers * (1.0 / total)).astype(bf16)
            attention_kept[2 * pair] = attention[:length]
            attention_kept[2 * pair + 1] = attention[length:]
            found = dot(attention, block(2, pair), 1, 0)
            at = pair * pair_width
            mixed[micro, :, at : at + pair_width] = jnp.where(
                lower, found[:length], found[length:]
            ).astype(bf16)
        save = pltpu.make_async_copy(attention_kept, stash_ref.at[micro], stash_sem)
        save.start()
        between = hidden + dot(mixed[micro], w_out_ref[...], 1, 0)
        high = between.astype(bf16)
        middle[2 * micro + 0] = high
        middle[2 * micro + 1] = (between - high.astype(f32)).astype(bf16)
        work[...] = between
        unit, _ = unit_rows(between)
        normed_two = (unit * gain_ref[1:2, :] + bias_ref[1:2, :]).astype(bf16)
        for at in range(0, hidden_units, FF_CHUNK):
            lifted = dot(normed_two, w_in_ref[:, at : at + FF_CHUNK], 1, 0)
            bent = (root * 0.044715) * (lifted * lifted)
            half = 0.5 + 0.5 * jnp.tanh(lifted * (bent + root))
            gelu = lifted * half
            active[micro, :, at : at + FF_CHUNK] = gelu.astype(bf16)
            slope[micro, :, at : at + FF_CHUNK] = (
                half + gelu * ((1.0 - half) * (6.0 * bent + 2.0 * root))
            ).astype(bf16)
        if stages > 1:
            @pl.when(jnp.logical_and(micro >= 2, stage < last))
            def _():
                hidden_copy(micro - 2, ahead).wait_send()
        slot = lax.rem(micro, 2)
        h_send[slot] = (work[...] + dot(active[micro], w_down_ref[...], 1, 0)).astype(bf16)
        if stages > 1:
            @pl.when(stage < last)
            def _():
                hidden_copy(micro, ahead).start()
        save.wait()

    def head(micro):
        unit, scale = unit_rows(h_send[lax.rem(micro, 2)].astype(f32))
        rounded = unit.astype(bf16)
        logits = dot(table_parts[0], rounded, 1, 1)
        logits = jnp.where(letters < vocab, logits, -jnp.inf)
        largest = jnp.max(logits, axis=0, keepdims=True)
        powers = jnp.exp(logits - largest)
        total = jnp.sum(powers, axis=0, keepdims=True)
        rows_of = token_ref[micro]
        stamp = rows_of[2:3]
        weight = jnp.where(rows_of[1:2] < stamp, 0.0, 1.0 / (length - stamp).astype(f32))
        target = (letters == rows_of[0:1]).astype(f32)
        g_logits = (weight * (powers / total - target)).astype(bf16)
        table_sum[...] += dot(g_logits, rounded, 1, 0)
        g_unit = dot(g_logits, table_parts[0], 0, 0)
        g_in[micro] = unit_back(g_unit, unit, scale).astype(bf16)

    def backward(micro):
        @pl.when(stage == last)
        def _():
            head(micro)

        if stages > 1:
            @pl.when(stage < last)
            def _():
                gradient_copy(micro, ahead).wait_recv()
        load = pltpu.make_async_copy(stash_ref.at[micro], attention_kept, stash_sem)
        load.start()
        g_out = g_in[micro]
        for at in range(0, hidden_units, FF_CHUNK):
            g_active = dot(g_out, w_down_ref[at : at + FF_CHUNK, :], 1, 1)
            slope[micro, :, at : at + FF_CHUNK] = (
                g_active * slope[micro, :, at : at + FF_CHUNK].astype(f32)
            ).astype(bf16)
        g_normed = dot(slope[micro], w_in_ref[...], 1, 1)
        unit, scale = unit_rows(middle[2 * micro + 0].astype(f32) + middle[2 * micro + 1].astype(f32))
        middle[2 * micro + 0] = (unit * gain_ref[1:2, :] + bias_ref[1:2, :]).astype(bf16)
        norm_sums[1] += fold_rows(g_normed * unit)
        norm_sums[3] += fold_rows(g_normed)
        g_middle = g_out.astype(f32) + unit_back(g_normed * gain_ref[1:2, :], unit, scale)
        g_attended = g_middle.astype(bf16)
        middle[2 * micro + 1] = g_attended
        g_mixed = dot(g_attended, w_out_ref[...], 1, 1).astype(bf16)
        load_hidden(micro)
        load.wait()
        pairs = HEADS // 2

        def block(member, pair):
            at = member * width + pair * pair_width
            return packed[micro, :, at : at + pair_width]

        def put(member, pair, value):
            at = member * width + pair * pair_width
            packed[micro, :, at : at + pair_width] = value.astype(bf16)

        def g_attention_of(pair):
            at = pair * pair_width
            g_pair = stacked(g_mixed[:, at : at + pair_width])
            return g_pair, dot(g_pair, block(2, pair), 1, 1)

        waiting = [g_attention_of(pair) for pair in range(AHEAD)]
        for pair in range(pairs):
            if pair + AHEAD < pairs:
                waiting.append(g_attention_of(pair + AHEAD))
            g_pair, g_attention = waiting[pair]
            low = attention_kept[2 * pair : 2 * pair + 2].reshape(2 * length, length)
            attention = low.astype(f32)
            inner = jnp.sum(attention * g_attention, axis=-1, keepdims=True)
            g_scores = (attention * (g_attention - inner)).astype(bf16)
            key, query = block(1, pair), stacked(block(0, pair))
            g_values = dot(low, g_pair, 0, 0)
            g_queries = dot(g_scores, key, 1, 0)
            g_keys = dot(g_scores, query, 0, 0)
            put(0, pair, jnp.where(lower, g_queries[:length], g_queries[length:]) * score_scale)
            put(1, pair, g_keys * score_scale)
            put(2, pair, g_values)
        g_normed = dot(packed[micro], w_qkv_ref[...], 1, 1)
        unit, scale = unit_rows(work[...])
        h_in[micro] = (unit * gain_ref[0:1, :] + bias_ref[0:1, :]).astype(bf16)
        norm_sums[0] += fold_rows(g_normed * unit)
        norm_sums[2] += fold_rows(g_normed)
        g_hidden = g_middle + unit_back(g_normed * gain_ref[0:1, :], unit, scale)

        @pl.when(stage == 0)
        def _():
            hot = shown_rows(micro)
            high = g_hidden.astype(bf16)
            low = (g_hidden - high.astype(f32)).astype(bf16)
            table_sum[...] += EMBED_GAIN * (dot(hot, high, 1, 0) + dot(hot, low, 1, 0))

        if stages > 1:
            @pl.when(stage > 0)
            def _():
                @pl.when(micro >= 2)
                def _():
                    gradient_copy(micro - 2, behind).wait_send()

                g_send[lax.rem(micro, 2)] = g_hidden.astype(bf16)
                gradient_copy(micro, behind).start()

    def weights(micro):
        d_down_ref[...] += dot(active[micro], g_in[micro], 0, 0)
        d_in_ref[...] += dot(middle[2 * micro + 0], slope[micro], 0, 0)
        d_out_ref[...] += dot(mixed[micro], middle[2 * micro + 1], 0, 0)
        d_qkv_ref[...] += dot(h_in[micro], packed[micro], 0, 0)

    warm = jnp.minimum(WARM * (last - stage), micro_count - 1)
    steps = 2 * micro_count

    def step(index, carry):
        b_micro = index - warm
        w_micro = index - micro_count

        @pl.when(index < micro_count)
        def _():
            forward(index)

        @pl.when(w_micro >= 0)
        def _():
            weights(w_micro)

        @pl.when(jnp.logical_and(b_micro >= 0, b_micro < micro_count))
        def _():
            backward(b_micro)

        return carry

    lax.fori_loop(0, steps, step, 0)

    if stages > 1:
        for micro in range(max(micro_count - 2, 0), micro_count):
            @pl.when(stage < last)
            def _():
                hidden_copy(micro, ahead).wait_send()

            @pl.when(stage > 0)
            def _():
                gradient_copy(micro, behind).wait_send()

    def table_copy(source, target, send, recv, device):
        return remote_copy(source, target, table_send.at[send], table_recv.at[recv], device)

    def lane_copy():
        return table_copy(table_sum, table_slots.at[0], 0, 0, (section, 0))

    def table_core_copy():
        return table_copy(table_sum, table_slots.at[1], 1, 1, partner)

    def table_peer_copy(from_row, to_row):
        return table_copy(
            table_sum, table_slots.at[2 + from_row], 2 + to_row, 2 + from_row, peer(to_row)
        )

    def table_down_copy(to_plane):
        return table_copy(
            d_table_ref, d_table_ref, 2 + rows + to_plane, 2 + rows, (section, to_plane)
        )

    def table_side_copy(to_place):
        target = 2 * chip_of(to_place, row, per_plane) + core
        return table_copy(
            d_table_ref, d_table_ref, 2 + rows + planes + to_place, 2 + rows, (target, plane)
        )

    @pl.when(stage == last)
    def _():
        lane_copy().start()

    def table_cores():
        @pl.when(stage == 0)
        def _():
            lane_copy().wait_recv()
            table_sum[...] += table_slots[0]
            table_core_copy().start()

    def table_peers():
        @pl.when(stage == 0)
        def _():
            table_core_copy().wait()
            table_sum[...] += table_slots[1]
            for to_row in range(rows):
                @pl.when(to_row != row)
                def _():
                    table_peer_copy(row, to_row).start()

    def table_side():
        for to_place in range(1, per_plane):
            table_side_copy(to_place).start()

    def table_down():
        @pl.when(stage == 0)
        def _():
            total = table_sum[...]
            for from_row in range(rows):
                @pl.when(from_row != row)
                def _():
                    table_peer_copy(from_row, from_row).wait_recv()

                total = total + jnp.where(from_row != row, table_slots[2 + from_row], 0.0)
            d_table_ref[...] = total
            for to_plane in range(1, planes):
                table_down_copy(to_plane).start()
            table_side()

    def table_done():
        @pl.when(place > 0)
        def _():
            table_side_copy(0).wait_recv()

        @pl.when(stage == last)
        def _():
            lane_copy().wait_send()

        @pl.when(stage == 0)
        def _():
            for to_row in range(rows):
                @pl.when(to_row != row)
                def _():
                    table_peer_copy(row, to_row).wait_send()

            for to_plane in range(1, planes):
                table_down_copy(to_plane).wait_send()

        @pl.when(place == 0)
        def _():
            for to_place in range(1, per_plane):
                table_side_copy(to_place).wait_send()

    for kind in range(2):
        totals = [
            jnp.sum(norm_sums[2 * kind + member], axis=0, keepdims=True) for member in range(2)
        ]
        block = jnp.concatenate(totals + [jnp.zeros((NORM_ROWS - 2, width), f32)], axis=0)
        for quarter in range(planes):
            start = (quarter * rows + kind) * NORM_ROWS
            norm_full[start : start + NORM_ROWS, :] = block

    pl.semaphore_signal(
        core_free, inc=1, device_id={"section": partner[0], "dp": partner[1]}, device_id_type=MESH
    )
    for at_row in range(rows):
        @pl.when(at_row != row)
        def _():
            far = peer(at_row)
            pl.semaphore_signal(
                peer_free, inc=1, device_id={"section": far[0], "dp": far[1]}, device_id_type=MESH
            )

    def direct_quarter(at_plane):
        return jnp.where(at_plane < planes - 1, at_plane + 1, at_plane - 1)

    def is_direct(pair):
        return 2 * pair + core == direct_quarter(plane)

    owns_direct = plane == direct_quarter(home_plane)

    def direct_landing(matrix, from_row, at_row):
        rows_of = pl.ds(at_row * heights[matrix], heights[matrix])
        if from_row == 0:
            return view(matrix, 3, rows_of)
        return matrices[matrix][5].at[from_row - 1, rows_of, matrices[matrix][-1]]

    def direct_args(matrix, pair, from_row, at_row):
        return (
            slot(matrix, 2 * rows * rows + pair * rows + at_row),
            direct_landing(matrix, from_row, at_row),
            peer_send.at[matrix, pair, at_row],
            direct_recv.at[matrix, from_row, at_row],
            (stage, 2 * pair + core),
        )

    def send_direct(matrix, pair, at_row):
        for from_row in range(rows):
            @pl.when(from_row == row)
            def _():
                remote_copy(*direct_args(matrix, pair, from_row, at_row)).start()

    def core_sum_args(matrix, pair, at_row):
        index = pair * rows + at_row
        return (
            slot(matrix, index),
            slot(matrix, rows * rows + index),
            core_send.at[matrix, pair, at_row],
            core_recv.at[matrix, pair, at_row],
            partner,
        )

    def peer_sum_args(matrix, pair, from_row, to_row):
        return (
            slot(matrix, 2 * rows * rows + pair * rows + to_row),
            slot(matrix, 3 * rows * rows + pair * rows + from_row),
            peer_send.at[matrix, pair, to_row],
            peer_recv.at[matrix, pair, from_row],
            peer(to_row),
        )

    def total_args(matrix, pair):
        height = heights[matrix]
        return (
            slot(matrix, 2 * rows * rows + pair * rows + row),
            view(matrix, 3, pl.ds(pl.multiple_of(row * height, height), height)),
            total_send.at[matrix, pair],
            total_recv.at[matrix, row],
            (stage, 2 * pair + core),
        )

    def give_core(matrix):
        for pair in range(rows):
            for at_row in range(rows):
                args = core_sum_args(matrix, pair, at_row)
                part = view(matrix, 1, piece(matrix, 2 * pair + 1 - core, at_row))
                args[0][...] = part[...].astype(args[0].dtype)
                remote_copy(*args).start()

    def give_peers(matrix):
        for pair in range(rows):
            for at_row in range(rows):
                remote_copy(*core_sum_args(matrix, pair, at_row)).wait_recv()
                landed = slot(matrix, rows * rows + pair * rows + at_row)
                part = view(matrix, 1, piece(matrix, 2 * pair + core, at_row))
                total = part[...] + landed[...].astype(f32)
                direct = is_direct(pair)

                @pl.when(direct)
                def _():
                    staged = slot(matrix, 2 * rows * rows + pair * rows + at_row)
                    staged[...] = total.astype(staged.dtype)
                    send_direct(matrix, pair, at_row)

                @pl.when(jnp.logical_and(jnp.logical_not(direct), at_row != row))
                def _():
                    args = peer_sum_args(matrix, pair, row, at_row)
                    args[0][...] = total.astype(args[0].dtype)
                    remote_copy(*args).start()

                @pl.when(jnp.logical_and(jnp.logical_not(direct), at_row == row))
                def _():
                    part[...] = total

    def give_total(matrix, pair):
        part = view(matrix, 1, piece(matrix, 2 * pair + core, row))
        for from_row in range(rows):
            @pl.when(from_row != row)
            def _():
                remote_copy(*peer_sum_args(matrix, pair, from_row, from_row)).wait_recv()
                landed = slot(matrix, 3 * rows * rows + pair * rows + from_row)
                part[...] += landed[...].astype(f32)

        args = total_args(matrix, pair)
        args[0][...] = part[...].astype(args[0].dtype)
        start_copy(*args, here)

    def give_totals(matrix):
        for pair in range(rows):
            @pl.when(jnp.logical_not(is_direct(pair)))
            def _():
                give_total(matrix, pair)

    def sent(matrix, pair):
        for at_row in range(rows):
            @pl.when(at_row != row)
            def _():
                remote_copy(*peer_sum_args(matrix, pair, row, at_row)).wait_send()

        wait_sent(*total_args(matrix, pair), here)

    def finish(matrix):
        height = heights[matrix]

        @pl.when(owns_direct)
        def _():
            for at_row in range(rows):
                for from_row in range(rows):
                    remote_copy(*direct_args(matrix, 0, from_row, at_row)).wait_recv()
                total = direct_landing(matrix, 0, at_row)
                value = total[...].astype(f32)
                for from_row in range(1, rows):
                    value = value + direct_landing(matrix, from_row, at_row)[...].astype(f32)
                total[...] = value.astype(total.dtype)

        @pl.when(jnp.logical_not(owns_direct))
        def _():
            for from_row in range(rows):
                part = view(matrix, 3, pl.ds(from_row * height, height))
                remote_copy(
                    part, part, total_send.at[matrix, 0], total_recv.at[matrix, from_row], partner
                ).wait_recv()

        for pair in range(rows):
            for at_row in range(rows):
                remote_copy(*core_sum_args(matrix, pair, at_row)).wait_send()

            @pl.when(is_direct(pair))
            def _():
                for at_row in range(rows):
                    remote_copy(*direct_args(matrix, pair, 0, at_row)).wait_send()

            @pl.when(jnp.logical_not(is_direct(pair)))
            def _():
                sent(matrix, pair)

    order = tuple(reversed(range(count)))
    table_cores()
    pl.semaphore_wait(core_free, 1)
    for position in range(count + 3):
        if position < count:
            give_core(order[position])
        if position == 1:
            table_peers()
            pl.semaphore_wait(peer_free, rows - 1)
        if 0 <= position - 1 < count:
            give_peers(order[position - 1])
        if 0 <= position - 3 < count:
            give_totals(order[position - 3])
        if position == 4:
            table_down()

    @pl.when(jnp.logical_and(place == 0, plane > 0))
    def _():
        table_down_copy(0).wait_recv()
        table_side()

    for matrix in order:
        finish(matrix)
    table_done()


def run_pipeline(stages, planes, token_ids, order, timesteps, table, gain, bias, *shards):
    w_qkv, w_out, w_in, w_down = shards
    micro_count, _, length = token_ids.shape
    width = table.shape[1]
    hidden_units = w_in.shape[2]
    rows = planes // 2
    table_rows = -(-table.shape[0] // 32) * 32
    bf16, f32 = jnp.bfloat16, jnp.float32
    vmem = pl.BlockSpec(memory_space=pltpu.VMEM)
    anywhere = pl.BlockSpec(memory_space=pl.ANY)
    scalars = pl.BlockSpec(memory_space=pltpu.SMEM)
    tokens = (micro_count, 3, length)
    norm_shard = (rows * NORM_ROWS, width)
    full = [(shard.shape[1] * planes, shard.shape[2]) for shard in shards]
    norm_full = (planes * rows * NORM_ROWS, width)
    outs = (
        jax.ShapeDtypeStruct((table_rows, width), f32),
        jax.ShapeDtypeStruct(norm_shard, f32),
        *(jax.ShapeDtypeStruct(shard.shape[1:], bf16) for shard in shards),
        jax.ShapeDtypeStruct((micro_count, HEADS, length, length), bf16),
    )
    rows_shape = (micro_count, length, width)
    units = 8
    pieces = (units, rows, rows)
    return pl.pallas_call(
        functools.partial(pipeline_kernel, stages, planes),
        out_shape=outs,
        in_specs=[vmem] * 2 + [scalars] + [vmem] * 3 + [anywhere] * 4,
        out_specs=[vmem] * 6 + [anywhere],
        scratch_shapes=[
            pltpu.VMEM(tokens, jnp.int32),
            pltpu.VMEM(norm_shard, f32),
            pltpu.VMEM(tokens, jnp.int32),
            pltpu.VMEM(rows_shape, bf16),
            pltpu.VMEM(rows_shape, bf16),
            pltpu.VMEM((2, length, width), bf16),
            pltpu.VMEM((2, length, width), bf16),
            pltpu.VMEM((micro_count, length, 3 * width), bf16),
            pltpu.VMEM(rows_shape, bf16),
            pltpu.VMEM((2 * micro_count, length, width), bf16),
            pltpu.VMEM((micro_count, length, hidden_units), bf16),
            pltpu.VMEM((micro_count, length, hidden_units), bf16),
            pltpu.VMEM((HEADS, length, length), bf16),
            pltpu.VMEM((length, width), f32),
            pltpu.VMEM((3, table_rows, width), bf16),
            pltpu.VMEM((4, 8, width), f32),
            pltpu.VMEM((table_rows, width), f32),
            pltpu.VMEM((4 * rows * rows, NORM_ROWS, width), f32),
            pltpu.VMEM(norm_full, f32),
            *(pltpu.VMEM(shape, bf16) for shape in full),
            pltpu.VMEM((NORM_ROWS, width), f32),
            pltpu.VMEM((NORM_ROWS, width), f32),
            *(pltpu.VMEM(shape, f32) for shape in full),
            pltpu.SemaphoreType.DMA((2,)),
            pltpu.SemaphoreType.DMA((micro_count,)),
            pltpu.SemaphoreType.DMA((2,)),
            pltpu.SemaphoreType.DMA((micro_count,)),
            pltpu.SemaphoreType.DMA,
            pltpu.SemaphoreType.DMA((2,)),
            pltpu.SemaphoreType.DMA,
            pltpu.SemaphoreType.DMA((units,)),
            pltpu.SemaphoreType.DMA((units, rows)),
            pltpu.SemaphoreType.DMA((units, planes)),
            pltpu.SemaphoreType.DMA((units, planes)),
            pltpu.SemaphoreType.DMA((units, rows)),
            pltpu.SemaphoreType.DMA(pieces),
            pltpu.SemaphoreType.DMA(pieces),
            pltpu.SemaphoreType.DMA(pieces),
            pltpu.SemaphoreType.DMA(pieces),
            pltpu.SemaphoreType.REGULAR,
            pltpu.SemaphoreType.REGULAR,
            pltpu.SemaphoreType.DMA((units, rows)),
            pltpu.SemaphoreType.DMA((units, rows)),
            pltpu.VMEM((2 + rows, table_rows, width), f32),
            pltpu.SemaphoreType.DMA((2 + rows + planes + stages // planes,)),
            pltpu.SemaphoreType.DMA((3 + rows,)),
            pltpu.VMEM((rows - 1, *norm_shard), f32),
            *(pltpu.VMEM((rows - 1, *shard.shape[1:]), bf16) for shard in shards),
            pltpu.SemaphoreType.DMA(pieces),
        ],
        compiler_params=pltpu.CompilerParams(
            vmem_limit_bytes=(64 << 20) - (192 << 10), collective_id=0, has_side_effects=True
        ),
    )(token_ids, order, timesteps, table, gain, bias, w_qkv, w_out, w_in, w_down)


def finish_kernel(planes, stages, *refs):
    table_ref, norm_ref, *totals = refs[:6]
    table_part, gain_part, bias_part, *results = refs[6:]
    section, plane = lax.axis_index("section"), lax.axis_index("dp")
    for total, result in zip(totals, results):
        result[0] = total[...].astype(jnp.float32)

    @pl.when(pl.program_id(0) == 0)
    def _():
        vocab, columns = table_part.shape
        part = jnp.zeros((vocab, columns), jnp.float32)
        for at in range(stages):
            block = table_ref[:vocab, at * columns : (at + 1) * columns]
            part = jnp.where(section == at, block, part)
        table_part[...] = part
        share = gain_part.shape[2]
        for kind, result in enumerate((gain_part, bias_part)):
            part = jnp.zeros((2, share), jnp.float32)
            for at in range(planes):
                start = kind * NORM_ROWS
                block = norm_ref[start : start + 2, at * share : (at + 1) * share]
                part = jnp.where(plane == at, block, part)
            result[0] = part


def run_finish(stages, planes, vocab, share, sums):
    f32 = jnp.float32
    steps = 4
    whole = [pl.BlockSpec(value.shape, lambda i: (0, 0)) for value in sums[:2]]
    blocks = [
        pl.BlockSpec((value.shape[0] // steps, value.shape[1]), lambda i: (i, 0))
        for value in sums[2:]
    ]
    out_blocks = [
        pl.BlockSpec((1, value.shape[0] // steps, value.shape[1]), lambda i: (0, i, 0))
        for value in sums[2:]
    ]
    columns = sums[0].shape[1] // stages
    return pl.pallas_call(
        functools.partial(finish_kernel, planes, stages),
        grid=(steps,),
        out_shape=(
            jax.ShapeDtypeStruct((vocab, columns), f32),
            jax.ShapeDtypeStruct((1, 2, share), f32),
            jax.ShapeDtypeStruct((1, 2, share), f32),
            *(jax.ShapeDtypeStruct((1, *value.shape), f32) for value in sums[2:]),
        ),
        in_specs=whole + blocks,
        out_specs=[
            pl.BlockSpec((vocab, columns), lambda i: (0, 0)),
            pl.BlockSpec((1, 2, share), lambda i: (0, 0, 0)),
            pl.BlockSpec((1, 2, share), lambda i: (0, 0, 0)),
            *out_blocks,
        ],
    )(*sums)


def body(token_ids, order, timesteps, table, norm_gain, norm_bias, w_qkv, w_out, w_in, w_down):
    stages, planes = lax.axis_size("section"), lax.axis_size("dp")
    sums = run_pipeline(
        stages,
        planes,
        token_ids,
        order,
        timesteps,
        table,
        norm_gain,
        norm_bias,
        w_qkv,
        w_out,
        w_in,
        w_down,
    )
    return tuple(run_finish(stages, planes, table.shape[0], norm_gain.shape[2], sums[:6]))


def solution(mesh):
    in_specs = (
        P(None, "dp", None),
        P(None, "dp", None),
        P(None, "dp"),
        P(),
        P("section", None, "dp"),
        P("section", None, "dp"),
        P("section", "dp", None),
        P("section", "dp", None),
        P("section", "dp", None),
        P("section", "dp", None),
    )
    out_specs = (
        P(None, "section"),
        P("section", None, "dp"),
        P("section", None, "dp"),
        P("section", "dp", None),
        P("section", "dp", None),
        P("section", "dp", None),
        P("section", "dp", None),
    )
    return jax.shard_map(body, mesh=mesh, in_specs=in_specs, out_specs=out_specs, check_vma=False)
```

```python
import functools
import math

import jax
import jax.numpy as jnp
from jax import lax
from jax.experimental import pallas as pl
from jax.experimental.pallas import tpu as pltpu
from jax.sharding import PartitionSpec as P

HEADS = 8
EPSILON = 1e-05
EMBED_GAIN = 16.0
FF_CHUNK = 512
AHEAD = 3
WARM = 3
NORM_ROWS = 8
MESH = pl.DeviceIdType.MESH


def dot(left, right, left_dim, right_dim):
    return lax.dot_general(
        left, right, (((left_dim,), (right_dim,)), ((), ())), preferred_element_type=jnp.float32
    )


def unit_rows(values):
    average = jnp.mean(values, axis=-1, keepdims=True)
    centered = values - average
    variance = jnp.mean(centered * centered, axis=-1, keepdims=True)
    scale = lax.rsqrt(variance + EPSILON)
    return centered * scale, scale


def unit_back(gradient, unit, scale):
    first = jnp.mean(gradient, axis=-1, keepdims=True)
    second = jnp.mean(gradient * unit, axis=-1, keepdims=True)
    return scale * (gradient - first - unit * second)


def fold_rows(values):
    rows, columns = values.shape
    return jnp.sum(values.reshape(rows // 8, 8, columns), axis=0)


def chip_of(place, row, per_plane):
    return row * per_plane + lax.rem(place - lax.rem(row, per_plane) + per_plane, per_plane)


def start_copy(src, dst, send_sem, recv_sem, device, here):
    section, plane = device
    same = jnp.logical_and(section == here[0], plane == here[1])

    @pl.when(same)
    def _():
        pltpu.make_async_copy(src, dst, recv_sem).start()

    @pl.when(jnp.logical_not(same))
    def _():
        remote_copy(src, dst, send_sem, recv_sem, device).start()


def wait_sent(src, dst, send_sem, recv_sem, device, here):
    section, plane = device
    same = jnp.logical_and(section == here[0], plane == here[1])

    @pl.when(jnp.logical_not(same))
    def _():
        remote_copy(src, dst, send_sem, recv_sem, device).wait_send()


def remote_copy(src, dst, send_sem, recv_sem, device):
    return pltpu.make_async_remote_copy(
        src_ref=src,
        dst_ref=dst,
        send_sem=send_sem,
        recv_sem=recv_sem,
        device_id={"section": device[0], "dp": device[1]},
        device_id_type=MESH,
    )


def pipeline_kernel(
    stages,
    planes,
    ids_ref,
    order_ref,
    stamp_ref,
    table_ref,
    gain_shard,
    bias_shard,
    qkv_shard,
    out_shard,
    in_shard,
    down_shard,
    d_table_ref,
    norm_total,
    qkv_total,
    out_total,
    in_total,
    down_total,
    stash_ref,
    token_in_ref,
    norm_shard,
    token_ref,
    h_in,
    g_in,
    h_send,
    g_send,
    packed,
    mixed,
    middle,
    active,
    slope,
    attention_kept,
    work,
    table_parts,
    norm_sums,
    table_sum,
    norm_slots,
    norm_full,
    w_qkv_ref,
    w_out_ref,
    w_in_ref,
    w_down_ref,
    gain_ref,
    bias_ref,
    d_qkv_ref,
    d_out_ref,
    d_in_ref,
    d_down_ref,
    h_send_sem,
    h_recv_sem,
    g_send_sem,
    g_recv_sem,
    stash_sem,
    token_send_sem,
    token_recv_sem,
    load_sem,
    spread_send,
    spread_recv,
    plane_send,
    plane_recv,
    peer_send,
    peer_recv,
    core_send,
    core_recv,
    core_free,
    peer_free,
    total_send,
    total_recv,
    table_slots,
    table_send,
    table_recv,
    more_norm,
    more_qkv,
    more_out,
    more_in,
    more_down,
    direct_recv,
):
    micro_count, _, length = token_ref.shape
    vocab, width = table_ref.shape
    hidden_units = w_in_ref.shape[1]
    head_size = width // HEADS
    score_scale = 1.0 / math.sqrt(head_size)
    root = math.sqrt(2.0 / math.pi)
    pair_width = 2 * head_size
    bf16, f32 = jnp.bfloat16, jnp.float32

    per_plane, rows = stages // planes, planes // 2
    section, plane = lax.axis_index("section"), lax.axis_index("dp")
    here = (section, plane)
    chip, core = lax.div(section, 2), lax.rem(section, 2)
    row = lax.div(chip, per_plane)
    place = lax.rem(lax.rem(chip, per_plane) + row, per_plane)
    odd = lax.rem(plane, 2)
    turn = jnp.where(odd == 0, place, per_plane - 1 - place)
    stage = plane * per_plane + turn
    last = stages - 1
    lane_row = lax.rem(row - lax.rem(place, rows) * core + rows, rows)
    lane_index = 2 * lane_row + core

    def next_device():
        step = jnp.where(odd == 0, 1, -1)
        near_place = place + step
        near_row = lax.rem(row + core * step + rows, rows)
        near = 2 * chip_of(near_place + per_plane, near_row, per_plane) + core
        stays = turn < per_plane - 1
        return jnp.where(stays, near, section), jnp.where(stays, plane, plane + 1)

    def previous_device():
        step = jnp.where(odd == 0, -1, 1)
        near_place = place + step
        near_row = lax.rem(row + core * step + rows, rows)
        near = 2 * chip_of(near_place + per_plane, near_row, per_plane) + core
        stays = turn > 0
        return jnp.where(stays, near, section), jnp.where(stays, plane, plane - 1)

    ahead, behind = next_device(), previous_device()
    partner = (section + 1 - 2 * core, plane)

    def layer_device(layer, at_row, at_core):
        at_plane, at_turn = lax.div(layer, per_plane), lax.rem(layer, per_plane)
        at_place = jnp.where(lax.rem(at_plane, 2) == 0, at_turn, per_plane - 1 - at_turn)
        return 2 * chip_of(at_place, at_row, per_plane) + at_core, at_plane

    def layer_here(at_plane):
        at_turn = jnp.where(at_plane % 2 == 0, place, per_plane - 1 - place)
        return at_plane * per_plane + at_turn

    def peer(at_row):
        return layer_device(stage, at_row, core)

    home_plane = lax.div(section, per_plane)
    carries = lax.rem(plane, 2) == core

    barrier = pltpu.get_barrier_semaphore()
    greetings = []

    def greet(device, wanted=True):
        same = jnp.logical_and(device[0] == section, device[1] == plane)
        wanted = jnp.logical_and(wanted, jnp.logical_not(same))
        greetings.append(jnp.where(wanted, 1, 0))

        @pl.when(wanted)
        def _():
            pl.semaphore_signal(
                barrier,
                inc=1,
                device_id={"section": device[0], "dp": device[1]},
                device_id_type=MESH,
            )

    for other in range(planes):
        greet((section, other))
        greet((layer_here(other), plane), carries)
    for at_row in range(rows):
        owner = layer_device(section, at_row, lax.rem(plane, 2))
        greet((owner[0], plane))
        greet(owner)
        greet((stage, 2 * at_row + core))
        greet(peer(at_row))
    for at_place in range(per_plane):
        greet((2 * chip_of(at_place, row, per_plane) + core, plane))
    greet(partner)
    greet(ahead, stage < last)
    greet(behind, stage > 0)
    matrices = []
    for parts, *members in (
        (2, w_qkv_ref, d_qkv_ref, qkv_shard, qkv_total, packed, more_qkv),
        (1, w_out_ref, d_out_ref, out_shard, out_total, mixed, more_out),
        (2, w_in_ref, d_in_ref, in_shard, in_total, active, more_in),
        (2, w_down_ref, d_down_ref, down_shard, down_total, middle, more_down),
        (1, norm_full, norm_full, norm_shard, norm_total, norm_slots, more_norm),
    ):
        window = members[0].shape[1] // parts
        for part in range(parts):
            matrices.append((*members, pl.ds(part * window, window)))
    count = len(matrices)
    norms = count - 1
    heights = [matrix[0].shape[0] // (planes * rows) for matrix in matrices]

    def view(matrix, member, rows_of):
        return matrices[matrix][member].at[rows_of, matrices[matrix][-1]]

    def slot(matrix, index):
        buffer, height = matrices[matrix][4], heights[matrix]
        per_block = buffer.shape[1] // height
        block, inside = index // per_block, index % per_block
        if not isinstance(inside, int):
            inside = pl.multiple_of(inside * height, height)
        else:
            inside = inside * height
        return buffer.at[block, pl.ds(inside, height), matrices[matrix][-1]]

    def transit(matrix, index):
        return slot(matrix, 2 * (matrices[matrix][4].shape[1] // heights[matrix]) + index)

    def piece(matrix, quarter, at_row):
        height = heights[matrix]
        return pl.ds(pl.multiple_of((quarter * rows + at_row) * height, height), height)

    loads = []
    for matrix in range(norms):
        shard, window = matrices[matrix][2], matrices[matrix][-1]
        loads.append(
            pltpu.make_async_copy(
                shard.at[0, :, window],
                view(matrix, 1, pl.ds(0, shard.shape[1])),
                load_sem.at[matrix],
            )
        )
        loads[-1].start()

    for micro in range(micro_count):
        token_in_ref[micro, 0:1, :] = ids_ref[micro]
        token_in_ref[micro, 1:2, :] = order_ref[micro]
        token_in_ref[micro, 2:3, :] = jnp.full((1, length), stamp_ref[micro], jnp.int32)
    norm_shard[...] = jnp.zeros_like(norm_shard)
    share = gain_shard.shape[2]
    columns = lax.broadcasted_iota(jnp.int32, (2, width), 1)
    mine = jnp.logical_and(columns >= plane * share, columns < (plane + 1) * share)
    for kind, shard in enumerate((gain_shard, bias_shard)):
        spread_out = jnp.concatenate([shard[0]] * planes, axis=1)
        norm_shard[kind * NORM_ROWS : kind * NORM_ROWS + 2, :] = jnp.where(mine, spread_out, 0.0)

    table_rows = table_parts.shape[1]
    work[:table_rows, :] = jnp.zeros((table_rows, width), f32)
    work[:vocab, :] = table_ref[...]
    rest = work[:table_rows, :]
    for part in range(3):
        rounded = rest.astype(bf16)
        table_parts[part] = rounded
        rest = rest - rounded.astype(f32)
    norm_sums[...] = jnp.zeros_like(norm_sums)
    table_sum[...] = jnp.zeros_like(table_sum)
    for matrix in range(norms):
        loads[matrix].wait()
        for at_row in range(rows):
            source = view(matrix, 1, pl.ds(at_row * heights[matrix], heights[matrix]))
            transit(matrix, planes + at_row)[...] = source[...].astype(bf16)
    pl.semaphore_wait(barrier, sum(greetings))

    gives_tokens = jnp.logical_and(place == 0, lane_index == plane)
    takes_tokens = jnp.logical_or(stage == 0, stage == last)

    def token_copy(index, target):
        return (
            token_in_ref,
            token_ref,
            token_send_sem.at[index],
            token_recv_sem,
            (section, target),
        )

    @pl.when(gives_tokens)
    def _():
        for index, target in enumerate((0, planes - 1)):
            start_copy(*token_copy(index, target), here)

    def spread_args(matrix, at_row):
        target, _ = layer_device(section, at_row, lax.rem(plane, 2))
        if matrix == norms:
            source = norm_shard.at[pl.ds(at_row * NORM_ROWS, NORM_ROWS)]
        else:
            source = transit(matrix, planes + at_row)
        return (
            source,
            transit(matrix, home_plane),
            spread_send.at[matrix, at_row],
            spread_recv.at[matrix, home_plane],
            (target, plane),
        )

    def plane_args(matrix, to_plane, from_plane):
        return (
            transit(matrix, to_plane),
            view(matrix, 0, piece(matrix, from_plane, row)),
            plane_send.at[matrix, to_plane],
            plane_recv.at[matrix, lax.div(from_plane, 2)],
            (section, to_plane),
        )

    def peer_args(matrix, quarter_pair, from_row, to_row):
        part = view(matrix, 0, piece(matrix, 2 * quarter_pair + core, from_row))
        return (
            part,
            part,
            peer_send.at[matrix, quarter_pair, to_row],
            peer_recv.at[matrix, quarter_pair, from_row],
            peer(to_row),
        )

    def core_args(matrix, quarter_pair, at_row, from_core):
        part = view(matrix, 0, piece(matrix, 2 * quarter_pair + from_core, at_row))
        return (
            part,
            part,
            core_send.at[matrix, quarter_pair, at_row],
            core_recv.at[matrix, quarter_pair, at_row],
            partner,
        )

    def spread(matrix):
        for at_row in range(rows):
            start_copy(*spread_args(matrix, at_row), here)

    def along_planes(matrix):
        @pl.when(carries)
        def _():
            for to_plane in range(planes):
                landed = transit(matrix, to_plane)
                remote_copy(
                    landed,
                    landed,
                    spread_send.at[matrix, 0],
                    spread_recv.at[matrix, to_plane],
                    partner,
                ).wait_recv()
                start_copy(*plane_args(matrix, to_plane, plane), here)

    def between_peers(matrix):
        for pair in range(rows):
            remote_copy(*plane_args(matrix, 0, 2 * pair + core)).wait_recv()
            for to_row in range(rows):
                @pl.when(to_row != row)
                def _():
                    remote_copy(*peer_args(matrix, pair, row, to_row)).start()

            remote_copy(*core_args(matrix, pair, row, core)).start()

    def between_cores(matrix):
        for pair in range(rows):
            for from_row in range(rows):
                @pl.when(from_row != row)
                def _():
                    remote_copy(*peer_args(matrix, pair, from_row, from_row)).wait_recv()
                    remote_copy(*core_args(matrix, pair, from_row, core)).start()

    def gathered(matrix):
        for pair in range(rows):
            for at_row in range(rows):
                remote_copy(*core_args(matrix, pair, at_row, 1 - core)).wait_recv()

    def gather_sent(matrix):
        for at_row in range(rows):
            wait_sent(*spread_args(matrix, at_row), here)

        @pl.when(carries)
        def _():
            for to_plane in range(planes):
                wait_sent(*plane_args(matrix, to_plane, plane), here)

        for pair in range(rows):
            for at_row in range(rows):
                @pl.when(at_row != row)
                def _():
                    remote_copy(*peer_args(matrix, pair, row, at_row)).wait_send()

                remote_copy(*core_args(matrix, pair, at_row, core)).wait_send()

    letters = lax.broadcasted_iota(jnp.int32, (table_rows, length), 0)
    lane = lax.broadcasted_iota(jnp.int32, (length, pair_width), 1)
    lower = lane < head_size

    def shown_rows(micro):
        rows_of = token_ref[micro]
        visible = rows_of[1:2] < rows_of[2:3]
        shown = jnp.where(visible, rows_of[0:1], vocab - 1)
        return (letters == shown).astype(bf16)

    def stacked(pair):
        zero = jnp.zeros_like(pair)
        return jnp.concatenate(
            [jnp.where(lower, pair, zero), jnp.where(lower, zero, pair)], axis=0
        )

    def load_hidden(micro):
        @pl.when(stage == 0)
        def _():
            hot = shown_rows(micro)
            total = dot(hot, table_parts[2], 0, 0)
            total = total + dot(hot, table_parts[1], 0, 0)
            total = total + dot(hot, table_parts[0], 0, 0)
            work[...] = total * EMBED_GAIN

        @pl.when(stage > 0)
        def _():
            work[...] = h_in[micro].astype(f32)

    def hidden_copy(micro, target):
        slot = lax.rem(micro, 2)
        return pltpu.make_async_remote_copy(
            src_ref=h_send.at[slot],
            dst_ref=h_in.at[micro],
            send_sem=h_send_sem.at[slot],
            recv_sem=h_recv_sem.at[micro],
            device_id={"section": target[0], "dp": target[1]},
            device_id_type=MESH,
        )

    def gradient_copy(micro, target):
        slot = lax.rem(micro, 2)
        return pltpu.make_async_remote_copy(
            src_ref=g_send.at[slot],
            dst_ref=g_in.at[micro],
            send_sem=g_send_sem.at[slot],
            recv_sem=g_recv_sem.at[micro],
            device_id={"section": target[0], "dp": target[1]},
            device_id_type=MESH,
        )

    def forward_attention(micro):
        load_hidden(micro)
        hidden = work[...]
        unit, _ = unit_rows(hidden)
        normed = (unit * gain_ref[0:1, :] + bias_ref[0:1, :]).astype(bf16)
        packed[micro] = dot(normed, w_qkv_ref[...], 1, 0).astype(bf16)
        pairs = HEADS // 2

        def block(member, pair):
            at = member * width + pair * pair_width
            return packed[micro, :, at : at + pair_width]

        def scores_of(pair):
            query = block(0, pair) * jnp.asarray(score_scale, bf16)
            return dot(stacked(query), block(1, pair), 1, 1)

        waiting = [scores_of(pair) for pair in range(AHEAD)]
        for pair in range(pairs):
            if pair + AHEAD < pairs:
                waiting.append(scores_of(pair + AHEAD))
            scores = waiting[pair]
            largest = jnp.max(scores, axis=-1, keepdims=True)
            powers = jnp.exp(scores - largest)
            total = jnp.sum(powers, axis=-1, keepdims=True)
            attention = (powers * (1.0 / total)).astype(bf16)
            attention_kept[2 * pair] = attention[:length]
            attention_kept[2 * pair + 1] = attention[length:]
            found = dot(attention, block(2, pair), 1, 0)
            at = pair * pair_width
            mixed[micro, :, at : at + pair_width] = jnp.where(
                lower, found[:length], found[length:]
            ).astype(bf16)
        pltpu.make_async_copy(attention_kept, stash_ref.at[micro], stash_sem).start()
        between = hidden + dot(mixed[micro], w_out_ref[...], 1, 0)
        high = between.astype(bf16)
        middle[2 * micro + 0] = high
        middle[2 * micro + 1] = (between - high.astype(f32)).astype(bf16)
        work[...] = between
        unit, _ = unit_rows(between)
        return (unit * gain_ref[1:2, :] + bias_ref[1:2, :]).astype(bf16)

    def forward_lift(micro, normed_two):
        for at in range(0, hidden_units, FF_CHUNK):
            lifted = dot(normed_two, w_in_ref[:, at : at + FF_CHUNK], 1, 0)
            bent = (root * 0.044715) * (lifted * lifted)
            half = 0.5 + 0.5 * jnp.tanh(lifted * (bent + root))
            gelu = lifted * half
            active[micro, :, at : at + FF_CHUNK] = gelu.astype(bf16)
            slope[micro, :, at : at + FF_CHUNK] = (
                half + gelu * ((1.0 - half) * (6.0 * bent + 2.0 * root))
            ).astype(bf16)
    def forward_end(micro):
        if stages > 1:
            @pl.when(jnp.logical_and(micro >= 2, stage < last))
            def _():
                hidden_copy(micro - 2, ahead).wait_send()
        slot = lax.rem(micro, 2)
        h_send[slot] = (work[...] + dot(active[micro], w_down_ref[...], 1, 0)).astype(bf16)
        if stages > 1:
            @pl.when(stage < last)
            def _():
                hidden_copy(micro, ahead).start()
        pltpu.make_async_copy(attention_kept, stash_ref.at[micro], stash_sem).wait()

    def forward(micro):
        if stages > 1:
            @pl.when(stage > 0)
            def _():
                hidden_copy(micro, behind).wait_recv()

        forward_lift(micro, forward_attention(micro))
        forward_end(micro)

    def set_norms():
        for kind, ref in enumerate((gain_ref, bias_ref)):
            total = jnp.zeros((NORM_ROWS, width), f32)
            for quarter in range(planes):
                start = (quarter * rows + kind) * NORM_ROWS
                total = total + norm_full[start : start + NORM_ROWS, :]
            ref[...] = total.astype(bf16).astype(f32)

    out_unit, in_unit = 2, 4
    steps_of_gather = (spread, along_planes, between_peers, between_cores, gathered)
    order = (norms, *range(norms))
    for turn_at in range(count + len(steps_of_gather) - 1):
        for depth, action in enumerate(steps_of_gather):
            if 0 <= turn_at - depth < count:
                action(order[turn_at - depth])
        done = turn_at - len(steps_of_gather) + 1
        if done == 0:
            set_norms()
        if done == order.index(out_unit):
            @pl.when(takes_tokens)
            def _():
                remote_copy(*token_copy(0, 0)).wait_recv()

            @pl.when(stage == 0)
            def _():
                g_send[0] = forward_attention(0)

        if done == order.index(in_unit):
            @pl.when(stage == 0)
            def _():
                forward_lift(0, g_send[0])

        if 1 <= turn_at <= 4:
            sums = (d_qkv_ref, d_out_ref, d_in_ref, d_down_ref)[turn_at - 1]
            sums[...] = jnp.zeros_like(sums)
    @pl.when(stage == 0)
    def _():
        forward_end(0)

    for matrix in range(count):
        gather_sent(matrix)

    @pl.when(gives_tokens)
    def _():
        for index, target in enumerate((0, planes - 1)):
            wait_sent(*token_copy(index, target), here)


    def head(micro):
        unit, scale = unit_rows(h_send[lax.rem(micro, 2)].astype(f32))
        rounded = unit.astype(bf16)
        logits = dot(table_parts[0], rounded, 1, 1)
        logits = jnp.where(letters < vocab, logits, -jnp.inf)
        largest = jnp.max(logits, axis=0, keepdims=True)
        powers = jnp.exp(logits - largest)
        total = jnp.sum(powers, axis=0, keepdims=True)
        rows_of = token_ref[micro]
        stamp = rows_of[2:3]
        weight = jnp.where(rows_of[1:2] < stamp, 0.0, 1.0 / (length - stamp).astype(f32))
        target = (letters == rows_of[0:1]).astype(f32)
        g_logits = (weight * (powers / total - target)).astype(bf16)
        table_sum[...] += dot(g_logits, rounded, 1, 0)
        g_unit = dot(g_logits, table_parts[0], 0, 0)
        g_in[micro] = unit_back(g_unit, unit, scale).astype(bf16)

    def backward(micro):
        @pl.when(stage == last)
        def _():
            head(micro)

        if stages > 1:
            @pl.when(stage < last)
            def _():
                gradient_copy(micro, ahead).wait_recv()
        load = pltpu.make_async_copy(stash_ref.at[micro], attention_kept, stash_sem)
        load.start()
        g_out = g_in[micro]
        for at in range(0, hidden_units, FF_CHUNK):
            g_active = dot(g_out, w_down_ref[at : at + FF_CHUNK, :], 1, 1)
            slope[micro, :, at : at + FF_CHUNK] = (
                g_active * slope[micro, :, at : at + FF_CHUNK].astype(f32)
            ).astype(bf16)
        g_normed = dot(slope[micro], w_in_ref[...], 1, 1)
        unit, scale = unit_rows(middle[2 * micro + 0].astype(f32) + middle[2 * micro + 1].astype(f32))
        middle[2 * micro + 0] = (unit * gain_ref[1:2, :] + bias_ref[1:2, :]).astype(bf16)
        norm_sums[1] += fold_rows(g_normed * unit)
        norm_sums[3] += fold_rows(g_normed)
        g_middle = g_out.astype(f32) + unit_back(g_normed * gain_ref[1:2, :], unit, scale)
        g_attended = g_middle.astype(bf16)
        middle[2 * micro + 1] = g_attended
        g_mixed = dot(g_attended, w_out_ref[...], 1, 1).astype(bf16)
        load_hidden(micro)
        load.wait()
        pairs = HEADS // 2

        def block(member, pair):
            at = member * width + pair * pair_width
            return packed[micro, :, at : at + pair_width]

        def put(member, pair, value):
            at = member * width + pair * pair_width
            packed[micro, :, at : at + pair_width] = value.astype(bf16)

        def g_attention_of(pair):
            at = pair * pair_width
            g_pair = stacked(g_mixed[:, at : at + pair_width])
            return g_pair, dot(g_pair, block(2, pair), 1, 1)

        waiting = [g_attention_of(pair) for pair in range(AHEAD)]
        for pair in range(pairs):
            if pair + AHEAD < pairs:
                waiting.append(g_attention_of(pair + AHEAD))
            g_pair, g_attention = waiting[pair]
            low = attention_kept[2 * pair : 2 * pair + 2].reshape(2 * length, length)
            attention = low.astype(f32)
            inner = jnp.sum(attention * g_attention, axis=-1, keepdims=True)
            g_scores = (attention * (g_attention - inner)).astype(bf16)
            key, query = block(1, pair), stacked(block(0, pair))
            g_values = dot(low, g_pair, 0, 0)
            g_queries = dot(g_scores, key, 1, 0)
            g_keys = dot(g_scores, query, 0, 0)
            put(0, pair, jnp.where(lower, g_queries[:length], g_queries[length:]) * score_scale)
            put(1, pair, g_keys * score_scale)
            put(2, pair, g_values)
        g_normed = dot(packed[micro], w_qkv_ref[...], 1, 1)
        unit, scale = unit_rows(work[...])
        h_in[micro] = (unit * gain_ref[0:1, :] + bias_ref[0:1, :]).astype(bf16)
        norm_sums[0] += fold_rows(g_normed * unit)
        norm_sums[2] += fold_rows(g_normed)
        g_hidden = g_middle + unit_back(g_normed * gain_ref[0:1, :], unit, scale)

        @pl.when(stage == 0)
        def _():
            hot = shown_rows(micro)
            high = g_hidden.astype(bf16)
            low = (g_hidden - high.astype(f32)).astype(bf16)
            table_sum[...] += EMBED_GAIN * (dot(hot, high, 1, 0) + dot(hot, low, 1, 0))

        if stages > 1:
            @pl.when(stage > 0)
            def _():
                @pl.when(micro >= 2)
                def _():
                    gradient_copy(micro - 2, behind).wait_send()

                g_send[lax.rem(micro, 2)] = g_hidden.astype(bf16)
                gradient_copy(micro, behind).start()

    def weights(micro):
        d_down_ref[...] += dot(active[micro], g_in[micro], 0, 0)
        d_in_ref[...] += dot(middle[2 * micro + 0], slope[micro], 0, 0)
        d_out_ref[...] += dot(mixed[micro], middle[2 * micro + 1], 0, 0)
        d_qkv_ref[...] += dot(h_in[micro], packed[micro], 0, 0)

    warm = jnp.minimum(WARM * (last - stage), micro_count - 1)
    steps = 2 * micro_count

    def step(index, carry):
        b_micro = index - warm
        w_micro = index - micro_count

        @pl.when(jnp.logical_and(index < micro_count, jnp.logical_or(stage > 0, index > 0)))
        def _():
            forward(index)

        @pl.when(w_micro >= 0)
        def _():
            weights(w_micro)

        @pl.when(jnp.logical_and(b_micro >= 0, b_micro < micro_count))
        def _():
            backward(b_micro)

        return carry

    lax.fori_loop(0, steps, step, 0)

    if stages > 1:
        for micro in range(max(micro_count - 2, 0), micro_count):
            @pl.when(stage < last)
            def _():
                hidden_copy(micro, ahead).wait_send()

            @pl.when(stage > 0)
            def _():
                gradient_copy(micro, behind).wait_send()

    def table_copy(source, target, send, recv, device):
        return remote_copy(source, target, table_send.at[send], table_recv.at[recv], device)

    def lane_copy():
        return table_copy(table_sum, table_slots.at[0], 0, 0, (section, 0))

    def table_core_copy():
        return table_copy(table_sum, table_slots.at[1], 1, 1, partner)

    def table_peer_copy(from_row, to_row):
        return table_copy(
            table_sum, table_slots.at[2 + from_row], 2 + to_row, 2 + from_row, peer(to_row)
        )

    def table_down_copy(to_plane):
        return table_copy(
            d_table_ref, d_table_ref, 2 + rows + to_plane, 2 + rows, (section, to_plane)
        )

    def table_side_copy(to_place):
        target = 2 * chip_of(to_place, row, per_plane) + core
        return table_copy(
            d_table_ref, d_table_ref, 2 + rows + planes + to_place, 2 + rows, (target, plane)
        )

    @pl.when(stage == last)
    def _():
        lane_copy().start()

    def table_cores():
        @pl.when(stage == 0)
        def _():
            lane_copy().wait_recv()
            table_sum[...] += table_slots[0]
            table_core_copy().start()

    def table_peers():
        @pl.when(stage == 0)
        def _():
            table_core_copy().wait()
            table_sum[...] += table_slots[1]
            for to_row in range(rows):
                @pl.when(to_row != row)
                def _():
                    table_peer_copy(row, to_row).start()

    def table_side():
        for to_place in range(1, per_plane):
            table_side_copy(to_place).start()

    def table_down():
        @pl.when(stage == 0)
        def _():
            total = table_sum[...]
            for from_row in range(rows):
                @pl.when(from_row != row)
                def _():
                    table_peer_copy(from_row, from_row).wait_recv()

                total = total + jnp.where(from_row != row, table_slots[2 + from_row], 0.0)
            d_table_ref[...] = total
            for to_plane in range(1, planes):
                table_down_copy(to_plane).start()
            table_side()

    def table_done():
        @pl.when(place > 0)
        def _():
            table_side_copy(0).wait_recv()

        @pl.when(stage == last)
        def _():
            lane_copy().wait_send()

        @pl.when(stage == 0)
        def _():
            for to_row in range(rows):
                @pl.when(to_row != row)
                def _():
                    table_peer_copy(row, to_row).wait_send()

            for to_plane in range(1, planes):
                table_down_copy(to_plane).wait_send()

        @pl.when(place == 0)
        def _():
            for to_place in range(1, per_plane):
                table_side_copy(to_place).wait_send()

    for kind in range(2):
        totals = [
            jnp.sum(norm_sums[2 * kind + member], axis=0, keepdims=True) for member in range(2)
        ]
        block = jnp.concatenate(totals + [jnp.zeros((NORM_ROWS - 2, width), f32)], axis=0)
        for quarter in range(planes):
            start = (quarter * rows + kind) * NORM_ROWS
            norm_full[start : start + NORM_ROWS, :] = block

    pl.semaphore_signal(
        core_free, inc=1, device_id={"section": partner[0], "dp": partner[1]}, device_id_type=MESH
    )
    for at_row in range(rows):
        @pl.when(at_row != row)
        def _():
            far = peer(at_row)
            pl.semaphore_signal(
                peer_free, inc=1, device_id={"section": far[0], "dp": far[1]}, device_id_type=MESH
            )

    def direct_quarter(at_plane):
        return jnp.where(at_plane < planes - 1, at_plane + 1, at_plane - 1)

    def is_direct(pair):
        return 2 * pair + core == direct_quarter(plane)

    owns_direct = plane == direct_quarter(home_plane)

    def direct_landing(matrix, from_row, at_row):
        rows_of = pl.ds(at_row * heights[matrix], heights[matrix])
        if from_row == 0:
            return view(matrix, 3, rows_of)
        return matrices[matrix][5].at[from_row - 1, rows_of, matrices[matrix][-1]]

    def direct_args(matrix, pair, from_row, at_row):
        return (
            slot(matrix, 2 * rows * rows + pair * rows + at_row),
            direct_landing(matrix, from_row, at_row),
            peer_send.at[matrix, pair, at_row],
            direct_recv.at[matrix, from_row, at_row],
            (stage, 2 * pair + core),
        )

    def send_direct(matrix, pair, at_row):
        for from_row in range(rows):
            @pl.when(from_row == row)
            def _():
                remote_copy(*direct_args(matrix, pair, from_row, at_row)).start()

    def core_sum_args(matrix, pair, at_row):
        index = pair * rows + at_row
        return (
            slot(matrix, index),
            slot(matrix, rows * rows + index),
            core_send.at[matrix, pair, at_row],
            core_recv.at[matrix, pair, at_row],
            partner,
        )

    def peer_sum_args(matrix, pair, from_row, to_row):
        return (
            slot(matrix, 2 * rows * rows + pair * rows + to_row),
            slot(matrix, 3 * rows * rows + pair * rows + from_row),
            peer_send.at[matrix, pair, to_row],
            peer_recv.at[matrix, pair, from_row],
            peer(to_row),
        )

    def total_args(matrix, pair):
        height = heights[matrix]
        return (
            slot(matrix, 2 * rows * rows + pair * rows + row),
            view(matrix, 3, pl.ds(pl.multiple_of(row * height, height), height)),
            total_send.at[matrix, pair],
            total_recv.at[matrix, row],
            (stage, 2 * pair + core),
        )

    def give_core(matrix):
        for pair in range(rows):
            for at_row in range(rows):
                args = core_sum_args(matrix, pair, at_row)
                part = view(matrix, 1, piece(matrix, 2 * pair + 1 - core, at_row))
                args[0][...] = part[...].astype(args[0].dtype)
                remote_copy(*args).start()

    def give_peers(matrix):
        for pair in range(rows):
            for at_row in range(rows):
                remote_copy(*core_sum_args(matrix, pair, at_row)).wait_recv()
                landed = slot(matrix, rows * rows + pair * rows + at_row)
                part = view(matrix, 1, piece(matrix, 2 * pair + core, at_row))
                total = part[...] + landed[...].astype(f32)
                direct = is_direct(pair)

                @pl.when(direct)
                def _():
                    staged = slot(matrix, 2 * rows * rows + pair * rows + at_row)
                    staged[...] = total.astype(staged.dtype)
                    send_direct(matrix, pair, at_row)

                @pl.when(jnp.logical_and(jnp.logical_not(direct), at_row != row))
                def _():
                    args = peer_sum_args(matrix, pair, row, at_row)
                    args[0][...] = total.astype(args[0].dtype)
                    remote_copy(*args).start()

                @pl.when(jnp.logical_and(jnp.logical_not(direct), at_row == row))
                def _():
                    part[...] = total

    def give_total(matrix, pair):
        part = view(matrix, 1, piece(matrix, 2 * pair + core, row))
        for from_row in range(rows):
            @pl.when(from_row != row)
            def _():
                remote_copy(*peer_sum_args(matrix, pair, from_row, from_row)).wait_recv()
                landed = slot(matrix, 3 * rows * rows + pair * rows + from_row)
                part[...] += landed[...].astype(f32)

        args = total_args(matrix, pair)
        args[0][...] = part[...].astype(args[0].dtype)
        start_copy(*args, here)

    def give_totals(matrix):
        for pair in range(rows):
            @pl.when(jnp.logical_not(is_direct(pair)))
            def _():
                give_total(matrix, pair)

    def sent(matrix, pair):
        for at_row in range(rows):
            @pl.when(at_row != row)
            def _():
                remote_copy(*peer_sum_args(matrix, pair, row, at_row)).wait_send()

        wait_sent(*total_args(matrix, pair), here)

    def finish(matrix):
        height = heights[matrix]

        @pl.when(owns_direct)
        def _():
            for at_row in range(rows):
                for from_row in range(rows):
                    remote_copy(*direct_args(matrix, 0, from_row, at_row)).wait_recv()
                total = direct_landing(matrix, 0, at_row)
                value = total[...].astype(f32)
                for from_row in range(1, rows):
                    value = value + direct_landing(matrix, from_row, at_row)[...].astype(f32)
                total[...] = value.astype(total.dtype)

        @pl.when(jnp.logical_not(owns_direct))
        def _():
            for from_row in range(rows):
                part = view(matrix, 3, pl.ds(from_row * height, height))
                remote_copy(
                    part, part, total_send.at[matrix, 0], total_recv.at[matrix, from_row], partner
                ).wait_recv()

        for pair in range(rows):
            for at_row in range(rows):
                remote_copy(*core_sum_args(matrix, pair, at_row)).wait_send()

            @pl.when(is_direct(pair))
            def _():
                for at_row in range(rows):
                    remote_copy(*direct_args(matrix, pair, 0, at_row)).wait_send()

            @pl.when(jnp.logical_not(is_direct(pair)))
            def _():
                sent(matrix, pair)

    order = tuple(reversed(range(count)))
    table_cores()
    pl.semaphore_wait(core_free, 1)
    for position in range(count + 3):
        if position < count:
            give_core(order[position])
        if position == 1:
            table_peers()
            pl.semaphore_wait(peer_free, rows - 1)
        if 0 <= position - 1 < count:
            give_peers(order[position - 1])
        if 0 <= position - 3 < count:
            give_totals(order[position - 3])
        if position == 4:
            table_down()

    @pl.when(jnp.logical_and(place == 0, plane > 0))
    def _():
        table_down_copy(0).wait_recv()
        table_side()

    for matrix in order:
        finish(matrix)
    table_done()


def run_pipeline(stages, planes, token_ids, order, timesteps, table, gain, bias, *shards):
    w_qkv, w_out, w_in, w_down = shards
    micro_count, _, length = token_ids.shape
    width = table.shape[1]
    hidden_units = w_in.shape[2]
    rows = planes // 2
    table_rows = -(-table.shape[0] // 32) * 32
    bf16, f32 = jnp.bfloat16, jnp.float32
    vmem = pl.BlockSpec(memory_space=pltpu.VMEM)
    anywhere = pl.BlockSpec(memory_space=pl.ANY)
    scalars = pl.BlockSpec(memory_space=pltpu.SMEM)
    tokens = (micro_count, 3, length)
    norm_shard = (rows * NORM_ROWS, width)
    full = [(shard.shape[1] * planes, shard.shape[2]) for shard in shards]
    norm_full = (planes * rows * NORM_ROWS, width)
    outs = (
        jax.ShapeDtypeStruct((table_rows, width), f32),
        jax.ShapeDtypeStruct(norm_shard, f32),
        *(jax.ShapeDtypeStruct(shard.shape[1:], bf16) for shard in shards),
        jax.ShapeDtypeStruct((micro_count, HEADS, length, length), bf16),
    )
    rows_shape = (micro_count, length, width)
    units = 8
    pieces = (units, rows, rows)
    return pl.pallas_call(
        functools.partial(pipeline_kernel, stages, planes),
        out_shape=outs,
        in_specs=[vmem] * 2 + [scalars] + [vmem] * 3 + [anywhere] * 4,
        out_specs=[vmem] * 6 + [anywhere],
        scratch_shapes=[
            pltpu.VMEM(tokens, jnp.int32),
            pltpu.VMEM(norm_shard, f32),
            pltpu.VMEM(tokens, jnp.int32),
            pltpu.VMEM(rows_shape, bf16),
            pltpu.VMEM(rows_shape, bf16),
            pltpu.VMEM((2, length, width), bf16),
            pltpu.VMEM((2, length, width), bf16),
            pltpu.VMEM((micro_count, length, 3 * width), bf16),
            pltpu.VMEM(rows_shape, bf16),
            pltpu.VMEM((2 * micro_count, length, width), bf16),
            pltpu.VMEM((micro_count, length, hidden_units), bf16),
            pltpu.VMEM((micro_count, length, hidden_units), bf16),
            pltpu.VMEM((HEADS, length, length), bf16),
            pltpu.VMEM((length, width), f32),
            pltpu.VMEM((3, table_rows, width), bf16),
            pltpu.VMEM((4, 8, width), f32),
            pltpu.VMEM((table_rows, width), f32),
            pltpu.VMEM((4 * rows * rows, NORM_ROWS, width), f32),
            pltpu.VMEM(norm_full, f32),
            *(pltpu.VMEM(shape, bf16) for shape in full),
            pltpu.VMEM((NORM_ROWS, width), f32),
            pltpu.VMEM((NORM_ROWS, width), f32),
            *(pltpu.VMEM(shape, f32) for shape in full),
            pltpu.SemaphoreType.DMA((2,)),
            pltpu.SemaphoreType.DMA((micro_count,)),
            pltpu.SemaphoreType.DMA((2,)),
            pltpu.SemaphoreType.DMA((micro_count,)),
            pltpu.SemaphoreType.DMA,
            pltpu.SemaphoreType.DMA((2,)),
            pltpu.SemaphoreType.DMA,
            pltpu.SemaphoreType.DMA((units,)),
            pltpu.SemaphoreType.DMA((units, rows)),
            pltpu.SemaphoreType.DMA((units, planes)),
            pltpu.SemaphoreType.DMA((units, planes)),
            pltpu.SemaphoreType.DMA((units, rows)),
            pltpu.SemaphoreType.DMA(pieces),
            pltpu.SemaphoreType.DMA(pieces),
            pltpu.SemaphoreType.DMA(pieces),
            pltpu.SemaphoreType.DMA(pieces),
            pltpu.SemaphoreType.REGULAR,
            pltpu.SemaphoreType.REGULAR,
            pltpu.SemaphoreType.DMA((units, rows)),
            pltpu.SemaphoreType.DMA((units, rows)),
            pltpu.VMEM((2 + rows, table_rows, width), f32),
            pltpu.SemaphoreType.DMA((2 + rows + planes + stages // planes,)),
            pltpu.SemaphoreType.DMA((3 + rows,)),
            pltpu.VMEM((rows - 1, *norm_shard), f32),
            *(pltpu.VMEM((rows - 1, *shard.shape[1:]), bf16) for shard in shards),
            pltpu.SemaphoreType.DMA(pieces),
        ],
        compiler_params=pltpu.CompilerParams(
            vmem_limit_bytes=(64 << 20) - (192 << 10), collective_id=0, has_side_effects=True
        ),
    )(token_ids, order, timesteps, table, gain, bias, w_qkv, w_out, w_in, w_down)


def finish_kernel(planes, stages, *refs):
    table_ref, norm_ref, *totals = refs[:6]
    table_part, gain_part, bias_part, *results = refs[6:]
    section, plane = lax.axis_index("section"), lax.axis_index("dp")
    for total, result in zip(totals, results):
        result[0] = total[...].astype(jnp.float32)

    @pl.when(pl.program_id(0) == 0)
    def _():
        vocab, columns = table_part.shape
        part = jnp.zeros((vocab, columns), jnp.float32)
        for at in range(stages):
            block = table_ref[:vocab, at * columns : (at + 1) * columns]
            part = jnp.where(section == at, block, part)
        table_part[...] = part
        share = gain_part.shape[2]
        for kind, result in enumerate((gain_part, bias_part)):
            part = jnp.zeros((2, share), jnp.float32)
            for at in range(planes):
                start = kind * NORM_ROWS
                block = norm_ref[start : start + 2, at * share : (at + 1) * share]
                part = jnp.where(plane == at, block, part)
            result[0] = part


def run_finish(stages, planes, vocab, share, sums):
    f32 = jnp.float32
    steps = 2
    whole = [pl.BlockSpec(value.shape, lambda i: (0, 0)) for value in sums[:2]]
    blocks = [
        pl.BlockSpec((value.shape[0] // steps, value.shape[1]), lambda i: (i, 0))
        for value in sums[2:]
    ]
    out_blocks = [
        pl.BlockSpec((1, value.shape[0] // steps, value.shape[1]), lambda i: (0, i, 0))
        for value in sums[2:]
    ]
    columns = sums[0].shape[1] // stages
    return pl.pallas_call(
        functools.partial(finish_kernel, planes, stages),
        grid=(steps,),
        out_shape=(
            jax.ShapeDtypeStruct((vocab, columns), f32),
            jax.ShapeDtypeStruct((1, 2, share), f32),
            jax.ShapeDtypeStruct((1, 2, share), f32),
            *(jax.ShapeDtypeStruct((1, *value.shape), f32) for value in sums[2:]),
        ),
        in_specs=whole + blocks,
        out_specs=[
            pl.BlockSpec((vocab, columns), lambda i: (0, 0)),
            pl.BlockSpec((1, 2, share), lambda i: (0, 0, 0)),
            pl.BlockSpec((1, 2, share), lambda i: (0, 0, 0)),
            *out_blocks,
        ],
    )(*sums)


def body(token_ids, order, timesteps, table, norm_gain, norm_bias, w_qkv, w_out, w_in, w_down):
    stages, planes = lax.axis_size("section"), lax.axis_size("dp")
    sums = run_pipeline(
        stages,
        planes,
        token_ids,
        order,
        timesteps[:, 0],
        table,
        norm_gain,
        norm_bias,
        w_qkv,
        w_out,
        w_in,
        w_down,
    )
    return tuple(run_finish(stages, planes, table.shape[0], norm_gain.shape[2], sums[:6]))


def solution(mesh):
    in_specs = (
        P(None, "dp", None),
        P(None, "dp", None),
        P(None, "dp"),
        P(),
        P("section", None, "dp"),
        P("section", None, "dp"),
        P("section", "dp", None),
        P("section", "dp", None),
        P("section", "dp", None),
        P("section", "dp", None),
    )
    out_specs = (
        P(None, "section"),
        P("section", None, "dp"),
        P("section", None, "dp"),
        P("section", "dp", None),
        P("section", "dp", None),
        P("section", "dp", None),
        P("section", "dp", None),
    )
    return jax.shard_map(body, mesh=mesh, in_specs=in_specs, out_specs=out_specs, check_vma=False)
```

```python
import functools
import math

import jax
import jax.numpy as jnp
from jax import lax
from jax.experimental import pallas as pl
from jax.experimental.pallas import tpu as pltpu
from jax.sharding import PartitionSpec as P

HEADS = 8
EPSILON = 1e-05
EMBED_GAIN = 16.0
FF_CHUNK = 512
AHEAD = 3
WARM = 3
NORM_ROWS = 8
MESH = pl.DeviceIdType.MESH


def dot(left, right, left_dim, right_dim):
    return lax.dot_general(
        left, right, (((left_dim,), (right_dim,)), ((), ())), preferred_element_type=jnp.float32
    )


def unit_rows(values):
    average = jnp.mean(values, axis=-1, keepdims=True)
    centered = values - average
    variance = jnp.mean(centered * centered, axis=-1, keepdims=True)
    scale = lax.rsqrt(variance + EPSILON)
    return centered * scale, scale


def unit_back(gradient, unit, scale):
    first = jnp.mean(gradient, axis=-1, keepdims=True)
    second = jnp.mean(gradient * unit, axis=-1, keepdims=True)
    return scale * (gradient - first - unit * second)


def fold_rows(values):
    rows, columns = values.shape
    return jnp.sum(values.reshape(rows // 8, 8, columns), axis=0)


def chip_of(place, row, per_plane):
    return row * per_plane + lax.rem(place - lax.rem(row, per_plane) + per_plane, per_plane)


def start_copy(src, dst, send_sem, recv_sem, device, here):
    section, plane = device
    same = jnp.logical_and(section == here[0], plane == here[1])

    @pl.when(same)
    def _():
        pltpu.make_async_copy(src, dst, recv_sem).start()

    @pl.when(jnp.logical_not(same))
    def _():
        remote_copy(src, dst, send_sem, recv_sem, device).start()


def wait_sent(src, dst, send_sem, recv_sem, device, here):
    section, plane = device
    same = jnp.logical_and(section == here[0], plane == here[1])

    @pl.when(jnp.logical_not(same))
    def _():
        remote_copy(src, dst, send_sem, recv_sem, device).wait_send()


def remote_copy(src, dst, send_sem, recv_sem, device):
    return pltpu.make_async_remote_copy(
        src_ref=src,
        dst_ref=dst,
        send_sem=send_sem,
        recv_sem=recv_sem,
        device_id={"section": device[0], "dp": device[1]},
        device_id_type=MESH,
    )


def pipeline_kernel(
    stages,
    planes,
    ids_ref,
    order_ref,
    stamp_ref,
    table_ref,
    gain_shard,
    bias_shard,
    qkv_shard,
    out_shard,
    in_shard,
    down_shard,
    d_table_ref,
    norm_total,
    qkv_total,
    out_total,
    in_total,
    down_total,
    stash_ref,
    token_in_ref,
    norm_shard,
    token_ref,
    h_in,
    g_in,
    h_send,
    g_send,
    packed,
    mixed,
    middle,
    active,
    slope,
    attention_kept,
    work,
    table_parts,
    norm_sums,
    table_sum,
    norm_slots,
    norm_full,
    w_qkv_ref,
    w_out_ref,
    w_in_ref,
    w_down_ref,
    gain_ref,
    bias_ref,
    d_qkv_ref,
    d_out_ref,
    d_in_ref,
    d_down_ref,
    h_send_sem,
    h_recv_sem,
    g_send_sem,
    g_recv_sem,
    stash_sem,
    token_send_sem,
    token_recv_sem,
    load_sem,
    spread_send,
    spread_recv,
    plane_send,
    plane_recv,
    peer_send,
    peer_recv,
    core_send,
    core_recv,
    core_free,
    peer_free,
    total_send,
    total_recv,
    table_slots,
    table_send,
    table_recv,
    more_norm,
    more_qkv,
    more_out,
    more_in,
    more_down,
    direct_recv,
):
    micro_count, _, length = token_ref.shape
    vocab, width = table_ref.shape
    hidden_units = w_in_ref.shape[1]
    head_size = width // HEADS
    score_scale = 1.0 / math.sqrt(head_size)
    root = math.sqrt(2.0 / math.pi)
    pair_width = 2 * head_size
    bf16, f32 = jnp.bfloat16, jnp.float32

    per_plane, rows = stages // planes, planes // 2
    section, plane = lax.axis_index("section"), lax.axis_index("dp")
    here = (section, plane)
    chip, core = lax.div(section, 2), lax.rem(section, 2)
    row = lax.div(chip, per_plane)
    place = lax.rem(lax.rem(chip, per_plane) + row, per_plane)
    odd = lax.rem(plane, 2)
    turn = jnp.where(odd == 0, place, per_plane - 1 - place)
    stage = plane * per_plane + turn
    last = stages - 1
    lane_row = lax.rem(row - lax.rem(place, rows) * core + rows, rows)
    lane_index = 2 * lane_row + core

    def next_device():
        step = jnp.where(odd == 0, 1, -1)
        near_place = place + step
        near_row = lax.rem(row + core * step + rows, rows)
        near = 2 * chip_of(near_place + per_plane, near_row, per_plane) + core
        stays = turn < per_plane - 1
        return jnp.where(stays, near, section), jnp.where(stays, plane, plane + 1)

    def previous_device():
        step = jnp.where(odd == 0, -1, 1)
        near_place = place + step
        near_row = lax.rem(row + core * step + rows, rows)
        near = 2 * chip_of(near_place + per_plane, near_row, per_plane) + core
        stays = turn > 0
        return jnp.where(stays, near, section), jnp.where(stays, plane, plane - 1)

    ahead, behind = next_device(), previous_device()
    partner = (section + 1 - 2 * core, plane)

    def layer_device(layer, at_row, at_core):
        at_plane, at_turn = lax.div(layer, per_plane), lax.rem(layer, per_plane)
        at_place = jnp.where(lax.rem(at_plane, 2) == 0, at_turn, per_plane - 1 - at_turn)
        return 2 * chip_of(at_place, at_row, per_plane) + at_core, at_plane

    def layer_here(at_plane):
        at_turn = jnp.where(at_plane % 2 == 0, place, per_plane - 1 - place)
        return at_plane * per_plane + at_turn

    def peer(at_row):
        return layer_device(stage, at_row, core)

    home_plane = lax.div(section, per_plane)
    carries = lax.rem(plane, 2) == core

    barrier = pltpu.get_barrier_semaphore()
    greetings = []

    def greet(device, wanted=True):
        same = jnp.logical_and(device[0] == section, device[1] == plane)
        wanted = jnp.logical_and(wanted, jnp.logical_not(same))
        greetings.append(jnp.where(wanted, 1, 0))

        @pl.when(wanted)
        def _():
            pl.semaphore_signal(
                barrier,
                inc=1,
                device_id={"section": device[0], "dp": device[1]},
                device_id_type=MESH,
            )

    for other in range(planes):
        greet((section, other))
        greet((layer_here(other), plane), carries)
    for at_row in range(rows):
        owner = layer_device(section, at_row, lax.rem(plane, 2))
        greet((owner[0], plane))
        greet(owner)
        greet((stage, 2 * at_row + core))
        greet(peer(at_row))
    for at_place in range(per_plane):
        greet((2 * chip_of(at_place, row, per_plane) + core, plane))
    greet(partner)
    greet(ahead, stage < last)
    greet(behind, stage > 0)
    matrices = []
    for parts, *members in (
        (2, w_qkv_ref, d_qkv_ref, qkv_shard, qkv_total, packed, more_qkv),
        (1, w_out_ref, d_out_ref, out_shard, out_total, mixed, more_out),
        (2, w_in_ref, d_in_ref, in_shard, in_total, active, more_in),
        (2, w_down_ref, d_down_ref, down_shard, down_total, middle, more_down),
        (1, norm_full, norm_full, norm_shard, norm_total, norm_slots, more_norm),
    ):
        window = members[0].shape[1] // parts
        for part in range(parts):
            matrices.append((*members, pl.ds(part * window, window)))
    count = len(matrices)
    norms = count - 1
    heights = [matrix[0].shape[0] // (planes * rows) for matrix in matrices]

    def view(matrix, member, rows_of):
        return matrices[matrix][member].at[rows_of, matrices[matrix][-1]]

    def slot(matrix, index):
        buffer, height = matrices[matrix][4], heights[matrix]
        per_block = buffer.shape[1] // height
        block, inside = index // per_block, index % per_block
        if not isinstance(inside, int):
            inside = pl.multiple_of(inside * height, height)
        else:
            inside = inside * height
        return buffer.at[block, pl.ds(inside, height), matrices[matrix][-1]]

    def transit(matrix, index):
        return slot(matrix, 2 * (matrices[matrix][4].shape[1] // heights[matrix]) + index)

    def piece(matrix, quarter, at_row):
        height = heights[matrix]
        return pl.ds(pl.multiple_of((quarter * rows + at_row) * height, height), height)

    loads = []
    for matrix in range(norms):
        shard, window = matrices[matrix][2], matrices[matrix][-1]
        loads.append(
            pltpu.make_async_copy(
                shard.at[0, :, window],
                view(matrix, 1, pl.ds(0, shard.shape[1])),
                load_sem.at[matrix],
            )
        )
        loads[-1].start()

    for micro in range(micro_count):
        token_in_ref[micro, 0:1, :] = ids_ref[micro]
        token_in_ref[micro, 1:2, :] = order_ref[micro]
        token_in_ref[micro, 2:3, :] = jnp.full((1, length), stamp_ref[micro], jnp.int32)
    norm_shard[...] = jnp.zeros_like(norm_shard)
    share = gain_shard.shape[2]
    columns = lax.broadcasted_iota(jnp.int32, (2, width), 1)
    mine = jnp.logical_and(columns >= plane * share, columns < (plane + 1) * share)
    for kind, shard in enumerate((gain_shard, bias_shard)):
        spread_out = jnp.concatenate([shard[0]] * planes, axis=1)
        norm_shard[kind * NORM_ROWS : kind * NORM_ROWS + 2, :] = jnp.where(mine, spread_out, 0.0)

    table_rows = table_parts.shape[1]
    work[:table_rows, :] = jnp.zeros((table_rows, width), f32)
    work[:vocab, :] = table_ref[...]
    rest = work[:table_rows, :]
    for part in range(3):
        rounded = rest.astype(bf16)
        table_parts[part] = rounded
        rest = rest - rounded.astype(f32)
    norm_sums[...] = jnp.zeros_like(norm_sums)
    table_sum[...] = jnp.zeros_like(table_sum)
    def rounded(matrix):
        loads[matrix].wait()
        for at_row in range(rows):
            source = view(matrix, 1, pl.ds(at_row * heights[matrix], heights[matrix]))
            transit(matrix, planes + at_row)[...] = source[...].astype(bf16)

    rounded(0)
    pl.semaphore_wait(barrier, sum(greetings))

    gives_tokens = jnp.logical_and(place == 0, lane_index == plane)
    takes_tokens = jnp.logical_or(stage == 0, stage == last)

    def token_copy(index, target):
        return (
            token_in_ref,
            token_ref,
            token_send_sem.at[index],
            token_recv_sem,
            (section, target),
        )

    @pl.when(gives_tokens)
    def _():
        for index, target in enumerate((0, planes - 1)):
            start_copy(*token_copy(index, target), here)

    def spread_args(matrix, at_row):
        target, _ = layer_device(section, at_row, lax.rem(plane, 2))
        if matrix == norms:
            source = norm_shard.at[pl.ds(at_row * NORM_ROWS, NORM_ROWS)]
        else:
            source = transit(matrix, planes + at_row)
        return (
            source,
            transit(matrix, home_plane),
            spread_send.at[matrix, at_row],
            spread_recv.at[matrix, home_plane],
            (target, plane),
        )

    def plane_args(matrix, to_plane, from_plane):
        return (
            transit(matrix, to_plane),
            view(matrix, 0, piece(matrix, from_plane, row)),
            plane_send.at[matrix, to_plane],
            plane_recv.at[matrix, lax.div(from_plane, 2)],
            (section, to_plane),
        )

    def peer_args(matrix, quarter_pair, from_row, to_row):
        part = view(matrix, 0, piece(matrix, 2 * quarter_pair + core, from_row))
        return (
            part,
            part,
            peer_send.at[matrix, quarter_pair, to_row],
            peer_recv.at[matrix, quarter_pair, from_row],
            peer(to_row),
        )

    def core_args(matrix, quarter_pair, at_row, from_core):
        part = view(matrix, 0, piece(matrix, 2 * quarter_pair + from_core, at_row))
        return (
            part,
            part,
            core_send.at[matrix, quarter_pair, at_row],
            core_recv.at[matrix, quarter_pair, at_row],
            partner,
        )

    def spread(matrix):
        if matrix not in (0, norms):
            rounded(matrix)
        for at_row in range(rows):
            start_copy(*spread_args(matrix, at_row), here)

    def along_planes(matrix):
        @pl.when(carries)
        def _():
            for to_plane in range(planes):
                landed = transit(matrix, to_plane)
                remote_copy(
                    landed,
                    landed,
                    spread_send.at[matrix, 0],
                    spread_recv.at[matrix, to_plane],
                    partner,
                ).wait_recv()
                start_copy(*plane_args(matrix, to_plane, plane), here)

    def between_peers(matrix):
        for pair in range(rows):
            remote_copy(*plane_args(matrix, 0, 2 * pair + core)).wait_recv()
            for to_row in range(rows):
                @pl.when(to_row != row)
                def _():
                    remote_copy(*peer_args(matrix, pair, row, to_row)).start()

            remote_copy(*core_args(matrix, pair, row, core)).start()

    def between_cores(matrix):
        for pair in range(rows):
            for from_row in range(rows):
                @pl.when(from_row != row)
                def _():
                    remote_copy(*peer_args(matrix, pair, from_row, from_row)).wait_recv()
                    remote_copy(*core_args(matrix, pair, from_row, core)).start()

    def gathered(matrix):
        for pair in range(rows):
            for at_row in range(rows):
                remote_copy(*core_args(matrix, pair, at_row, 1 - core)).wait_recv()

    def gather_sent(matrix):
        for at_row in range(rows):
            wait_sent(*spread_args(matrix, at_row), here)

        @pl.when(carries)
        def _():
            for to_plane in range(planes):
                wait_sent(*plane_args(matrix, to_plane, plane), here)

        for pair in range(rows):
            for at_row in range(rows):
                @pl.when(at_row != row)
                def _():
                    remote_copy(*peer_args(matrix, pair, row, at_row)).wait_send()

                remote_copy(*core_args(matrix, pair, at_row, core)).wait_send()

    letters = lax.broadcasted_iota(jnp.int32, (table_rows, length), 0)
    lane = lax.broadcasted_iota(jnp.int32, (length, pair_width), 1)
    lower = lane < head_size

    def shown_rows(micro):
        rows_of = token_ref[micro]
        visible = rows_of[1:2] < rows_of[2:3]
        shown = jnp.where(visible, rows_of[0:1], vocab - 1)
        return (letters == shown).astype(bf16)

    def stacked(pair):
        zero = jnp.zeros_like(pair)
        return jnp.concatenate(
            [jnp.where(lower, pair, zero), jnp.where(lower, zero, pair)], axis=0
        )

    def load_hidden(micro):
        @pl.when(stage == 0)
        def _():
            hot = shown_rows(micro)
            total = dot(hot, table_parts[2], 0, 0)
            total = total + dot(hot, table_parts[1], 0, 0)
            total = total + dot(hot, table_parts[0], 0, 0)
            work[...] = total * EMBED_GAIN

        @pl.when(stage > 0)
        def _():
            work[...] = h_in[micro].astype(f32)

    def hidden_copy(micro, target):
        slot = lax.rem(micro, 2)
        return pltpu.make_async_remote_copy(
            src_ref=h_send.at[slot],
            dst_ref=h_in.at[micro],
            send_sem=h_send_sem.at[slot],
            recv_sem=h_recv_sem.at[micro],
            device_id={"section": target[0], "dp": target[1]},
            device_id_type=MESH,
        )

    def gradient_copy(micro, target):
        slot = lax.rem(micro, 2)
        return pltpu.make_async_remote_copy(
            src_ref=g_send.at[slot],
            dst_ref=g_in.at[micro],
            send_sem=g_send_sem.at[slot],
            recv_sem=g_recv_sem.at[micro],
            device_id={"section": target[0], "dp": target[1]},
            device_id_type=MESH,
        )

    def forward_attention(micro):
        load_hidden(micro)
        hidden = work[...]
        unit, _ = unit_rows(hidden)
        normed = (unit * gain_ref[0:1, :] + bias_ref[0:1, :]).astype(bf16)
        packed[micro] = dot(normed, w_qkv_ref[...], 1, 0).astype(bf16)
        pairs = HEADS // 2

        def block(member, pair):
            at = member * width + pair * pair_width
            return packed[micro, :, at : at + pair_width]

        def scores_of(pair):
            query = block(0, pair) * jnp.asarray(score_scale, bf16)
            return dot(stacked(query), block(1, pair), 1, 1)

        waiting = [scores_of(pair) for pair in range(AHEAD)]
        for pair in range(pairs):
            if pair + AHEAD < pairs:
                waiting.append(scores_of(pair + AHEAD))
            scores = waiting[pair]
            largest = jnp.max(scores, axis=-1, keepdims=True)
            powers = jnp.exp(scores - largest)
            total = jnp.sum(powers, axis=-1, keepdims=True)
            attention = (powers * (1.0 / total)).astype(bf16)
            attention_kept[2 * pair] = attention[:length]
            attention_kept[2 * pair + 1] = attention[length:]
            found = dot(attention, block(2, pair), 1, 0)
            at = pair * pair_width
            mixed[micro, :, at : at + pair_width] = jnp.where(
                lower, found[:length], found[length:]
            ).astype(bf16)
        pltpu.make_async_copy(attention_kept, stash_ref.at[micro], stash_sem).start()
        between = hidden + dot(mixed[micro], w_out_ref[...], 1, 0)
        high = between.astype(bf16)
        middle[2 * micro + 0] = high
        middle[2 * micro + 1] = (between - high.astype(f32)).astype(bf16)
        work[...] = between
        unit, _ = unit_rows(between)
        return (unit * gain_ref[1:2, :] + bias_ref[1:2, :]).astype(bf16)

    def forward_lift(micro, normed_two):
        for at in range(0, hidden_units, FF_CHUNK):
            lifted = dot(normed_two, w_in_ref[:, at : at + FF_CHUNK], 1, 0)
            bent = (root * 0.044715) * (lifted * lifted)
            half = 0.5 + 0.5 * jnp.tanh(lifted * (bent + root))
            gelu = lifted * half
            active[micro, :, at : at + FF_CHUNK] = gelu.astype(bf16)
            slope[micro, :, at : at + FF_CHUNK] = (
                half + gelu * ((1.0 - half) * (6.0 * bent + 2.0 * root))
            ).astype(bf16)
    def forward_end(micro):
        if stages > 1:
            @pl.when(jnp.logical_and(micro >= 2, stage < last))
            def _():
                hidden_copy(micro - 2, ahead).wait_send()
        slot = lax.rem(micro, 2)
        h_send[slot] = (work[...] + dot(active[micro], w_down_ref[...], 1, 0)).astype(bf16)
        if stages > 1:
            @pl.when(stage < last)
            def _():
                hidden_copy(micro, ahead).start()
        pltpu.make_async_copy(attention_kept, stash_ref.at[micro], stash_sem).wait()

    def forward(micro):
        if stages > 1:
            @pl.when(stage > 0)
            def _():
                hidden_copy(micro, behind).wait_recv()

        forward_lift(micro, forward_attention(micro))
        forward_end(micro)

    def set_norms():
        for kind, ref in enumerate((gain_ref, bias_ref)):
            total = jnp.zeros((NORM_ROWS, width), f32)
            for quarter in range(planes):
                start = (quarter * rows + kind) * NORM_ROWS
                total = total + norm_full[start : start + NORM_ROWS, :]
            ref[...] = total.astype(bf16).astype(f32)

    out_unit, in_unit = 2, 4
    steps_of_gather = (spread, along_planes, between_peers, between_cores, gathered)
    order = (norms, *range(norms))
    for turn_at in range(count + len(steps_of_gather) - 1):
        for depth, action in enumerate(steps_of_gather):
            if 0 <= turn_at - depth < count:
                action(order[turn_at - depth])
        done = turn_at - len(steps_of_gather) + 1
        if done == 0:
            set_norms()
        if done == order.index(out_unit):
            @pl.when(takes_tokens)
            def _():
                remote_copy(*token_copy(0, 0)).wait_recv()

            @pl.when(stage == 0)
            def _():
                g_send[0] = forward_attention(0)

        if done == order.index(in_unit):
            @pl.when(stage == 0)
            def _():
                forward_lift(0, g_send[0])

        if 7 <= turn_at <= 10:
            sums = (d_qkv_ref, d_out_ref, d_in_ref, d_down_ref)[turn_at - 7]
            sums[...] = jnp.zeros_like(sums)
    @pl.when(stage == 0)
    def _():
        forward_end(0)

    for matrix in range(count):
        gather_sent(matrix)

    @pl.when(gives_tokens)
    def _():
        for index, target in enumerate((0, planes - 1)):
            wait_sent(*token_copy(index, target), here)


    def head(micro):
        unit, scale = unit_rows(h_send[lax.rem(micro, 2)].astype(f32))
        rounded = unit.astype(bf16)
        logits = dot(table_parts[0], rounded, 1, 1)
        logits = jnp.where(letters < vocab, logits, -jnp.inf)
        largest = jnp.max(logits, axis=0, keepdims=True)
        powers = jnp.exp(logits - largest)
        total = jnp.sum(powers, axis=0, keepdims=True)
        rows_of = token_ref[micro]
        stamp = rows_of[2:3]
        weight = jnp.where(rows_of[1:2] < stamp, 0.0, 1.0 / (length - stamp).astype(f32))
        target = (letters == rows_of[0:1]).astype(f32)
        g_logits = (weight * (powers / total - target)).astype(bf16)
        table_sum[...] += dot(g_logits, rounded, 1, 0)
        g_unit = dot(g_logits, table_parts[0], 0, 0)
        g_in[micro] = unit_back(g_unit, unit, scale).astype(bf16)

    def backward(micro):
        @pl.when(stage == last)
        def _():
            head(micro)

        if stages > 1:
            @pl.when(stage < last)
            def _():
                gradient_copy(micro, ahead).wait_recv()
        load = pltpu.make_async_copy(stash_ref.at[micro], attention_kept, stash_sem)
        load.start()
        g_out = g_in[micro]
        for at in range(0, hidden_units, FF_CHUNK):
            g_active = dot(g_out, w_down_ref[at : at + FF_CHUNK, :], 1, 1)
            slope[micro, :, at : at + FF_CHUNK] = (
                g_active * slope[micro, :, at : at + FF_CHUNK].astype(f32)
            ).astype(bf16)
        g_normed = dot(slope[micro], w_in_ref[...], 1, 1)
        unit, scale = unit_rows(middle[2 * micro + 0].astype(f32) + middle[2 * micro + 1].astype(f32))
        middle[2 * micro + 0] = (unit * gain_ref[1:2, :] + bias_ref[1:2, :]).astype(bf16)
        norm_sums[1] += fold_rows(g_normed * unit)
        norm_sums[3] += fold_rows(g_normed)
        g_middle = g_out.astype(f32) + unit_back(g_normed * gain_ref[1:2, :], unit, scale)
        g_attended = g_middle.astype(bf16)
        middle[2 * micro + 1] = g_attended
        g_mixed = dot(g_attended, w_out_ref[...], 1, 1).astype(bf16)
        load_hidden(micro)
        load.wait()
        pairs = HEADS // 2

        def block(member, pair):
            at = member * width + pair * pair_width
            return packed[micro, :, at : at + pair_width]

        def put(member, pair, value):
            at = member * width + pair * pair_width
            packed[micro, :, at : at + pair_width] = value.astype(bf16)

        def g_attention_of(pair):
            at = pair * pair_width
            g_pair = stacked(g_mixed[:, at : at + pair_width])
            return g_pair, dot(g_pair, block(2, pair), 1, 1)

        waiting = [g_attention_of(pair) for pair in range(AHEAD)]
        for pair in range(pairs):
            if pair + AHEAD < pairs:
                waiting.append(g_attention_of(pair + AHEAD))
            g_pair, g_attention = waiting[pair]
            low = attention_kept[2 * pair : 2 * pair + 2].reshape(2 * length, length)
            attention = low.astype(f32)
            inner = jnp.sum(attention * g_attention, axis=-1, keepdims=True)
            g_scores = (attention * (g_attention - inner)).astype(bf16)
            key, query = block(1, pair), stacked(block(0, pair))
            g_values = dot(low, g_pair, 0, 0)
            g_queries = dot(g_scores, key, 1, 0)
            g_keys = dot(g_scores, query, 0, 0)
            put(0, pair, jnp.where(lower, g_queries[:length], g_queries[length:]) * score_scale)
            put(1, pair, g_keys * score_scale)
            put(2, pair, g_values)
        g_normed = dot(packed[micro], w_qkv_ref[...], 1, 1)
        unit, scale = unit_rows(work[...])
        h_in[micro] = (unit * gain_ref[0:1, :] + bias_ref[0:1, :]).astype(bf16)
        norm_sums[0] += fold_rows(g_normed * unit)
        norm_sums[2] += fold_rows(g_normed)
        g_hidden = g_middle + unit_back(g_normed * gain_ref[0:1, :], unit, scale)

        @pl.when(stage == 0)
        def _():
            hot = shown_rows(micro)
            high = g_hidden.astype(bf16)
            low = (g_hidden - high.astype(f32)).astype(bf16)
            table_sum[...] += EMBED_GAIN * (dot(hot, high, 1, 0) + dot(hot, low, 1, 0))

        if stages > 1:
            @pl.when(stage > 0)
            def _():
                @pl.when(micro >= 2)
                def _():
                    gradient_copy(micro - 2, behind).wait_send()

                g_send[lax.rem(micro, 2)] = g_hidden.astype(bf16)
                gradient_copy(micro, behind).start()

    def weights(micro):
        d_down_ref[...] += dot(active[micro], g_in[micro], 0, 0)
        d_in_ref[...] += dot(middle[2 * micro + 0], slope[micro], 0, 0)
        d_out_ref[...] += dot(mixed[micro], middle[2 * micro + 1], 0, 0)
        d_qkv_ref[...] += dot(h_in[micro], packed[micro], 0, 0)

    warm = jnp.minimum(WARM * (last - stage), micro_count - 1)
    steps = 2 * micro_count

    def step(index, carry):
        b_micro = index - warm
        w_micro = index - micro_count

        @pl.when(jnp.logical_and(index < micro_count, jnp.logical_or(stage > 0, index > 0)))
        def _():
            forward(index)

        @pl.when(w_micro >= 0)
        def _():
            weights(w_micro)

        @pl.when(jnp.logical_and(b_micro >= 0, b_micro < micro_count))
        def _():
            backward(b_micro)

        return carry

    lax.fori_loop(0, steps, step, 0)

    if stages > 1:
        for micro in range(max(micro_count - 2, 0), micro_count):
            @pl.when(stage < last)
            def _():
                hidden_copy(micro, ahead).wait_send()

            @pl.when(stage > 0)
            def _():
                gradient_copy(micro, behind).wait_send()

    def table_copy(source, target, send, recv, device):
        return remote_copy(source, target, table_send.at[send], table_recv.at[recv], device)

    def lane_copy():
        return table_copy(table_sum, table_slots.at[0], 0, 0, (section, 0))

    def table_core_copy():
        return table_copy(table_sum, table_slots.at[1], 1, 1, partner)

    def table_peer_copy(from_row, to_row):
        return table_copy(
            table_sum, table_slots.at[2 + from_row], 2 + to_row, 2 + from_row, peer(to_row)
        )

    def table_down_copy(to_plane):
        return table_copy(
            d_table_ref, d_table_ref, 2 + rows + to_plane, 2 + rows, (section, to_plane)
        )

    def table_side_copy(to_place):
        target = 2 * chip_of(to_place, row, per_plane) + core
        return table_copy(
            d_table_ref, d_table_ref, 2 + rows + planes + to_place, 2 + rows, (target, plane)
        )

    @pl.when(stage == last)
    def _():
        lane_copy().start()

    def table_cores():
        @pl.when(stage == 0)
        def _():
            lane_copy().wait_recv()
            table_sum[...] += table_slots[0]
            table_core_copy().start()

    def table_peers():
        @pl.when(stage == 0)
        def _():
            table_core_copy().wait()
            table_sum[...] += table_slots[1]
            for to_row in range(rows):
                @pl.when(to_row != row)
                def _():
                    table_peer_copy(row, to_row).start()

    def table_side():
        for to_place in range(1, per_plane):
            table_side_copy(to_place).start()

    def table_down():
        @pl.when(stage == 0)
        def _():
            total = table_sum[...]
            for from_row in range(rows):
                @pl.when(from_row != row)
                def _():
                    table_peer_copy(from_row, from_row).wait_recv()

                total = total + jnp.where(from_row != row, table_slots[2 + from_row], 0.0)
            d_table_ref[...] = total
            for to_plane in range(1, planes):
                table_down_copy(to_plane).start()
            table_side()

    def table_done():
        @pl.when(place > 0)
        def _():
            table_side_copy(0).wait_recv()

        @pl.when(stage == last)
        def _():
            lane_copy().wait_send()

        @pl.when(stage == 0)
        def _():
            for to_row in range(rows):
                @pl.when(to_row != row)
                def _():
                    table_peer_copy(row, to_row).wait_send()

            for to_plane in range(1, planes):
                table_down_copy(to_plane).wait_send()

        @pl.when(place == 0)
        def _():
            for to_place in range(1, per_plane):
                table_side_copy(to_place).wait_send()

    for kind in range(2):
        totals = [
            jnp.sum(norm_sums[2 * kind + member], axis=0, keepdims=True) for member in range(2)
        ]
        block = jnp.concatenate(totals + [jnp.zeros((NORM_ROWS - 2, width), f32)], axis=0)
        for quarter in range(planes):
            start = (quarter * rows + kind) * NORM_ROWS
            norm_full[start : start + NORM_ROWS, :] = block

    pl.semaphore_signal(
        core_free, inc=1, device_id={"section": partner[0], "dp": partner[1]}, device_id_type=MESH
    )
    for at_row in range(rows):
        @pl.when(at_row != row)
        def _():
            far = peer(at_row)
            pl.semaphore_signal(
                peer_free, inc=1, device_id={"section": far[0], "dp": far[1]}, device_id_type=MESH
            )

    def direct_quarter(at_plane):
        return jnp.where(at_plane < planes - 1, at_plane + 1, at_plane - 1)

    def is_direct(pair):
        return 2 * pair + core == direct_quarter(plane)

    owns_direct = plane == direct_quarter(home_plane)

    def direct_landing(matrix, from_row, at_row):
        rows_of = pl.ds(at_row * heights[matrix], heights[matrix])
        if from_row == 0:
            return view(matrix, 3, rows_of)
        return matrices[matrix][5].at[from_row - 1, rows_of, matrices[matrix][-1]]

    def direct_args(matrix, pair, from_row, at_row):
        return (
            slot(matrix, 2 * rows * rows + pair * rows + at_row),
            direct_landing(matrix, from_row, at_row),
            peer_send.at[matrix, pair, at_row],
            direct_recv.at[matrix, from_row, at_row],
            (stage, 2 * pair + core),
        )

    def send_direct(matrix, pair, at_row):
        for from_row in range(rows):
            @pl.when(from_row == row)
            def _():
                remote_copy(*direct_args(matrix, pair, from_row, at_row)).start()

    def core_sum_args(matrix, pair, at_row):
        index = pair * rows + at_row
        return (
            slot(matrix, index),
            slot(matrix, rows * rows + index),
            core_send.at[matrix, pair, at_row],
            core_recv.at[matrix, pair, at_row],
            partner,
        )

    def peer_sum_args(matrix, pair, from_row, to_row):
        return (
            slot(matrix, 2 * rows * rows + pair * rows + to_row),
            slot(matrix, 3 * rows * rows + pair * rows + from_row),
            peer_send.at[matrix, pair, to_row],
            peer_recv.at[matrix, pair, from_row],
            peer(to_row),
        )

    def total_args(matrix, pair):
        height = heights[matrix]
        return (
            slot(matrix, 2 * rows * rows + pair * rows + row),
            view(matrix, 3, pl.ds(pl.multiple_of(row * height, height), height)),
            total_send.at[matrix, pair],
            total_recv.at[matrix, row],
            (stage, 2 * pair + core),
        )

    def give_core(matrix):
        for pair in range(rows):
            for at_row in range(rows):
                args = core_sum_args(matrix, pair, at_row)
                part = view(matrix, 1, piece(matrix, 2 * pair + 1 - core, at_row))
                args[0][...] = part[...].astype(args[0].dtype)
                remote_copy(*args).start()

    def give_peers(matrix):
        for pair in range(rows):
            for at_row in range(rows):
                remote_copy(*core_sum_args(matrix, pair, at_row)).wait_recv()
                landed = slot(matrix, rows * rows + pair * rows + at_row)
                part = view(matrix, 1, piece(matrix, 2 * pair + core, at_row))
                total = part[...] + landed[...].astype(f32)
                direct = is_direct(pair)

                @pl.when(direct)
                def _():
                    staged = slot(matrix, 2 * rows * rows + pair * rows + at_row)
                    staged[...] = total.astype(staged.dtype)
                    send_direct(matrix, pair, at_row)

                @pl.when(jnp.logical_and(jnp.logical_not(direct), at_row != row))
                def _():
                    args = peer_sum_args(matrix, pair, row, at_row)
                    args[0][...] = total.astype(args[0].dtype)
                    remote_copy(*args).start()

                @pl.when(jnp.logical_and(jnp.logical_not(direct), at_row == row))
                def _():
                    part[...] = total

    def give_total(matrix, pair):
        part = view(matrix, 1, piece(matrix, 2 * pair + core, row))
        for from_row in range(rows):
            @pl.when(from_row != row)
            def _():
                remote_copy(*peer_sum_args(matrix, pair, from_row, from_row)).wait_recv()
                landed = slot(matrix, 3 * rows * rows + pair * rows + from_row)
                part[...] += landed[...].astype(f32)

        args = total_args(matrix, pair)
        args[0][...] = part[...].astype(args[0].dtype)
        start_copy(*args, here)

    def give_totals(matrix):
        for pair in range(rows):
            @pl.when(jnp.logical_not(is_direct(pair)))
            def _():
                give_total(matrix, pair)

    def sent(matrix, pair):
        for at_row in range(rows):
            @pl.when(at_row != row)
            def _():
                remote_copy(*peer_sum_args(matrix, pair, row, at_row)).wait_send()

        wait_sent(*total_args(matrix, pair), here)

    def finish(matrix):
        height = heights[matrix]

        @pl.when(owns_direct)
        def _():
            for at_row in range(rows):
                for from_row in range(rows):
                    remote_copy(*direct_args(matrix, 0, from_row, at_row)).wait_recv()
                total = direct_landing(matrix, 0, at_row)
                value = total[...].astype(f32)
                for from_row in range(1, rows):
                    value = value + direct_landing(matrix, from_row, at_row)[...].astype(f32)
                total[...] = value.astype(total.dtype)

        @pl.when(jnp.logical_not(owns_direct))
        def _():
            for from_row in range(rows):
                part = view(matrix, 3, pl.ds(from_row * height, height))
                remote_copy(
                    part, part, total_send.at[matrix, 0], total_recv.at[matrix, from_row], partner
                ).wait_recv()

        for pair in range(rows):
            for at_row in range(rows):
                remote_copy(*core_sum_args(matrix, pair, at_row)).wait_send()

            @pl.when(is_direct(pair))
            def _():
                for at_row in range(rows):
                    remote_copy(*direct_args(matrix, pair, 0, at_row)).wait_send()

            @pl.when(jnp.logical_not(is_direct(pair)))
            def _():
                sent(matrix, pair)

    order = tuple(reversed(range(count)))
    table_cores()
    pl.semaphore_wait(core_free, 1)
    for position in range(count + 4):
        if position < count:
            give_core(order[position])
        if position == 1:
            table_peers()
            pl.semaphore_wait(peer_free, rows - 1)
        if 0 <= position - 1 < count:
            give_peers(order[position - 1])
        if 0 <= position - 4 < count:
            give_totals(order[position - 4])
        if position == 4:
            table_down()

    @pl.when(jnp.logical_and(place == 0, plane > 0))
    def _():
        table_down_copy(0).wait_recv()
        table_side()

    for matrix in order:
        finish(matrix)
    table_done()


def run_pipeline(stages, planes, token_ids, order, timesteps, table, gain, bias, *shards):
    w_qkv, w_out, w_in, w_down = shards
    micro_count, _, length = token_ids.shape
    width = table.shape[1]
    hidden_units = w_in.shape[2]
    rows = planes // 2
    table_rows = -(-table.shape[0] // 32) * 32
    bf16, f32 = jnp.bfloat16, jnp.float32
    vmem = pl.BlockSpec(memory_space=pltpu.VMEM)
    anywhere = pl.BlockSpec(memory_space=pl.ANY)
    scalars = pl.BlockSpec(memory_space=pltpu.SMEM)
    tokens = (micro_count, 3, length)
    norm_shard = (rows * NORM_ROWS, width)
    full = [(shard.shape[1] * planes, shard.shape[2]) for shard in shards]
    norm_full = (planes * rows * NORM_ROWS, width)
    outs = (
        jax.ShapeDtypeStruct((table_rows, width), f32),
        jax.ShapeDtypeStruct(norm_shard, f32),
        *(jax.ShapeDtypeStruct(shard.shape[1:], bf16) for shard in shards),
        jax.ShapeDtypeStruct((micro_count, HEADS, length, length), bf16),
    )
    rows_shape = (micro_count, length, width)
    units = 8
    pieces = (units, rows, rows)
    return pl.pallas_call(
        functools.partial(pipeline_kernel, stages, planes),
        out_shape=outs,
        in_specs=[vmem] * 2 + [scalars] + [vmem] * 3 + [anywhere] * 4,
        out_specs=[vmem] * 6 + [anywhere],
        scratch_shapes=[
            pltpu.VMEM(tokens, jnp.int32),
            pltpu.VMEM(norm_shard, f32),
            pltpu.VMEM(tokens, jnp.int32),
            pltpu.VMEM(rows_shape, bf16),
            pltpu.VMEM(rows_shape, bf16),
            pltpu.VMEM((2, length, width), bf16),
            pltpu.VMEM((2, length, width), bf16),
            pltpu.VMEM((micro_count, length, 3 * width), bf16),
            pltpu.VMEM(rows_shape, bf16),
            pltpu.VMEM((2 * micro_count, length, width), bf16),
            pltpu.VMEM((micro_count, length, hidden_units), bf16),
            pltpu.VMEM((micro_count, length, hidden_units), bf16),
            pltpu.VMEM((HEADS, length, length), bf16),
            pltpu.VMEM((length, width), f32),
            pltpu.VMEM((3, table_rows, width), bf16),
            pltpu.VMEM((4, 8, width), f32),
            pltpu.VMEM((table_rows, width), f32),
            pltpu.VMEM((4 * rows * rows, NORM_ROWS, width), f32),
            pltpu.VMEM(norm_full, f32),
            *(pltpu.VMEM(shape, bf16) for shape in full),
            pltpu.VMEM((NORM_ROWS, width), f32),
            pltpu.VMEM((NORM_ROWS, width), f32),
            *(pltpu.VMEM(shape, f32) for shape in full),
            pltpu.SemaphoreType.DMA((2,)),
            pltpu.SemaphoreType.DMA((micro_count,)),
            pltpu.SemaphoreType.DMA((2,)),
            pltpu.SemaphoreType.DMA((micro_count,)),
            pltpu.SemaphoreType.DMA,
            pltpu.SemaphoreType.DMA((2,)),
            pltpu.SemaphoreType.DMA,
            pltpu.SemaphoreType.DMA((units,)),
            pltpu.SemaphoreType.DMA((units, rows)),
            pltpu.SemaphoreType.DMA((units, planes)),
            pltpu.SemaphoreType.DMA((units, planes)),
            pltpu.SemaphoreType.DMA((units, rows)),
            pltpu.SemaphoreType.DMA(pieces),
            pltpu.SemaphoreType.DMA(pieces),
            pltpu.SemaphoreType.DMA(pieces),
            pltpu.SemaphoreType.DMA(pieces),
            pltpu.SemaphoreType.REGULAR,
            pltpu.SemaphoreType.REGULAR,
            pltpu.SemaphoreType.DMA((units, rows)),
            pltpu.SemaphoreType.DMA((units, rows)),
            pltpu.VMEM((2 + rows, table_rows, width), f32),
            pltpu.SemaphoreType.DMA((2 + rows + planes + stages // planes,)),
            pltpu.SemaphoreType.DMA((3 + rows,)),
            pltpu.VMEM((rows - 1, *norm_shard), f32),
            *(pltpu.VMEM((rows - 1, *shard.shape[1:]), bf16) for shard in shards),
            pltpu.SemaphoreType.DMA(pieces),
        ],
        compiler_params=pltpu.CompilerParams(
            vmem_limit_bytes=(64 << 20) - (192 << 10), collective_id=0, has_side_effects=True
        ),
    )(token_ids, order, timesteps, table, gain, bias, w_qkv, w_out, w_in, w_down)


def finish_kernel(planes, stages, *refs):
    table_ref, norm_ref, *totals = refs[:6]
    table_part, gain_part, bias_part, *results = refs[6:]
    section, plane = lax.axis_index("section"), lax.axis_index("dp")
    for total, result in zip(totals, results):
        result[0] = total[...].astype(jnp.float32)

    @pl.when(pl.program_id(0) == 0)
    def _():
        vocab, columns = table_part.shape
        part = jnp.zeros((vocab, columns), jnp.float32)
        for at in range(stages):
            block = table_ref[:vocab, at * columns : (at + 1) * columns]
            part = jnp.where(section == at, block, part)
        table_part[...] = part
        share = gain_part.shape[2]
        for kind, result in enumerate((gain_part, bias_part)):
            part = jnp.zeros((2, share), jnp.float32)
            for at in range(planes):
                start = kind * NORM_ROWS
                block = norm_ref[start : start + 2, at * share : (at + 1) * share]
                part = jnp.where(plane == at, block, part)
            result[0] = part


def run_finish(stages, planes, vocab, share, sums):
    f32 = jnp.float32
    steps = 2
    whole = [pl.BlockSpec(value.shape, lambda i: (0, 0)) for value in sums[:2]]
    blocks = [
        pl.BlockSpec((value.shape[0] // steps, value.shape[1]), lambda i: (i, 0))
        for value in sums[2:]
    ]
    out_blocks = [
        pl.BlockSpec((1, value.shape[0] // steps, value.shape[1]), lambda i: (0, i, 0))
        for value in sums[2:]
    ]
    columns = sums[0].shape[1] // stages
    return pl.pallas_call(
        functools.partial(finish_kernel, planes, stages),
        grid=(steps,),
        out_shape=(
            jax.ShapeDtypeStruct((vocab, columns), f32),
            jax.ShapeDtypeStruct((1, 2, share), f32),
            jax.ShapeDtypeStruct((1, 2, share), f32),
            *(jax.ShapeDtypeStruct((1, *value.shape), f32) for value in sums[2:]),
        ),
        in_specs=whole + blocks,
        out_specs=[
            pl.BlockSpec((vocab, columns), lambda i: (0, 0)),
            pl.BlockSpec((1, 2, share), lambda i: (0, 0, 0)),
            pl.BlockSpec((1, 2, share), lambda i: (0, 0, 0)),
            *out_blocks,
        ],
    )(*sums)


def body(token_ids, order, timesteps, table, norm_gain, norm_bias, w_qkv, w_out, w_in, w_down):
    stages, planes = lax.axis_size("section"), lax.axis_size("dp")
    sums = run_pipeline(
        stages,
        planes,
        token_ids,
        order,
        timesteps[:, 0],
        table,
        norm_gain,
        norm_bias,
        w_qkv,
        w_out,
        w_in,
        w_down,
    )
    return tuple(run_finish(stages, planes, table.shape[0], norm_gain.shape[2], sums[:6]))


def solution(mesh):
    in_specs = (
        P(None, "dp", None),
        P(None, "dp", None),
        P(None, "dp"),
        P(),
        P("section", None, "dp"),
        P("section", None, "dp"),
        P("section", "dp", None),
        P("section", "dp", None),
        P("section", "dp", None),
        P("section", "dp", None),
    )
    out_specs = (
        P(None, "section"),
        P("section", None, "dp"),
        P("section", None, "dp"),
        P("section", "dp", None),
        P("section", "dp", None),
        P("section", "dp", None),
        P("section", "dp", None),
    )
    return jax.shard_map(body, mesh=mesh, in_specs=in_specs, out_specs=out_specs, check_vma=False)
```

```python
import functools
import math

import jax
import jax.numpy as jnp
from jax import lax
from jax.experimental import pallas as pl
from jax.experimental.pallas import tpu as pltpu
from jax.sharding import PartitionSpec as P

HEADS = 8
EPSILON = 1e-05
EMBED_GAIN = 16.0
FF_CHUNK = 512
AHEAD = 3
WARM = 3
NORM_ROWS = 8
MESH = pl.DeviceIdType.MESH


def dot(left, right, left_dim, right_dim):
    return lax.dot_general(
        left, right, (((left_dim,), (right_dim,)), ((), ())), preferred_element_type=jnp.float32
    )


def unit_rows(values):
    average = jnp.mean(values, axis=-1, keepdims=True)
    centered = values - average
    variance = jnp.mean(centered * centered, axis=-1, keepdims=True)
    scale = lax.rsqrt(variance + EPSILON)
    return centered * scale, scale


def unit_back(gradient, unit, scale):
    first = jnp.mean(gradient, axis=-1, keepdims=True)
    second = jnp.mean(gradient * unit, axis=-1, keepdims=True)
    return scale * (gradient - first - unit * second)


def fold_rows(values):
    rows, columns = values.shape
    return jnp.sum(values.reshape(rows // 8, 8, columns), axis=0)


def chip_of(place, row, per_plane):
    return row * per_plane + lax.rem(place - lax.rem(row, per_plane) + per_plane, per_plane)


def start_copy(src, dst, send_sem, recv_sem, device, here):
    section, plane = device
    same = jnp.logical_and(section == here[0], plane == here[1])

    @pl.when(same)
    def _():
        pltpu.make_async_copy(src, dst, recv_sem).start()

    @pl.when(jnp.logical_not(same))
    def _():
        remote_copy(src, dst, send_sem, recv_sem, device).start()


def wait_sent(src, dst, send_sem, recv_sem, device, here):
    section, plane = device
    same = jnp.logical_and(section == here[0], plane == here[1])

    @pl.when(jnp.logical_not(same))
    def _():
        remote_copy(src, dst, send_sem, recv_sem, device).wait_send()


def remote_copy(src, dst, send_sem, recv_sem, device):
    return pltpu.make_async_remote_copy(
        src_ref=src,
        dst_ref=dst,
        send_sem=send_sem,
        recv_sem=recv_sem,
        device_id={"section": device[0], "dp": device[1]},
        device_id_type=MESH,
    )


def pipeline_kernel(
    stages,
    planes,
    ids_ref,
    order_ref,
    stamp_ref,
    table_ref,
    gain_shard,
    bias_shard,
    qkv_shard,
    out_shard,
    in_shard,
    down_shard,
    d_table_ref,
    norm_total,
    qkv_total,
    out_total,
    in_total,
    down_total,
    stash_ref,
    token_in_ref,
    norm_shard,
    token_ref,
    h_in,
    g_in,
    h_send,
    g_send,
    packed,
    mixed,
    middle,
    active,
    slope,
    attention_kept,
    work,
    table_parts,
    norm_sums,
    table_sum,
    norm_slots,
    norm_full,
    w_qkv_ref,
    w_out_ref,
    w_in_ref,
    w_down_ref,
    gain_ref,
    bias_ref,
    d_qkv_ref,
    d_out_ref,
    d_in_ref,
    d_down_ref,
    h_send_sem,
    h_recv_sem,
    g_send_sem,
    g_recv_sem,
    stash_sem,
    token_send_sem,
    token_recv_sem,
    load_sem,
    spread_send,
    spread_recv,
    plane_send,
    plane_recv,
    peer_send,
    peer_recv,
    core_send,
    core_recv,
    core_free,
    peer_free,
    total_send,
    total_recv,
    table_slots,
    table_send,
    table_recv,
    more_norm,
    more_qkv,
    more_out,
    more_in,
    more_down,
    direct_recv,
):
    micro_count, _, length = token_ref.shape
    vocab, width = table_ref.shape
    hidden_units = w_in_ref.shape[1]
    head_size = width // HEADS
    score_scale = 1.0 / math.sqrt(head_size)
    root = math.sqrt(2.0 / math.pi)
    pair_width = 2 * head_size
    bf16, f32 = jnp.bfloat16, jnp.float32

    per_plane, rows = stages // planes, planes // 2
    section, plane = lax.axis_index("section"), lax.axis_index("dp")
    here = (section, plane)
    chip, core = lax.div(section, 2), lax.rem(section, 2)
    row = lax.div(chip, per_plane)
    place = lax.rem(lax.rem(chip, per_plane) + row, per_plane)
    odd = lax.rem(plane, 2)
    turn = jnp.where(odd == 0, place, per_plane - 1 - place)
    stage = plane * per_plane + turn
    last = stages - 1
    lane_row = lax.rem(row - lax.rem(place, rows) * core + rows, rows)
    lane_index = 2 * lane_row + core

    def next_device():
        step = jnp.where(odd == 0, 1, -1)
        near_place = place + step
        near_row = lax.rem(row + core * step + rows, rows)
        near = 2 * chip_of(near_place + per_plane, near_row, per_plane) + core
        stays = turn < per_plane - 1
        return jnp.where(stays, near, section), jnp.where(stays, plane, plane + 1)

    def previous_device():
        step = jnp.where(odd == 0, -1, 1)
        near_place = place + step
        near_row = lax.rem(row + core * step + rows, rows)
        near = 2 * chip_of(near_place + per_plane, near_row, per_plane) + core
        stays = turn > 0
        return jnp.where(stays, near, section), jnp.where(stays, plane, plane - 1)

    ahead, behind = next_device(), previous_device()
    partner = (section + 1 - 2 * core, plane)

    def layer_device(layer, at_row, at_core):
        at_plane, at_turn = lax.div(layer, per_plane), lax.rem(layer, per_plane)
        at_place = jnp.where(lax.rem(at_plane, 2) == 0, at_turn, per_plane - 1 - at_turn)
        return 2 * chip_of(at_place, at_row, per_plane) + at_core, at_plane

    def layer_here(at_plane):
        at_turn = jnp.where(at_plane % 2 == 0, place, per_plane - 1 - place)
        return at_plane * per_plane + at_turn

    def peer(at_row):
        return layer_device(stage, at_row, core)

    home_plane = lax.div(section, per_plane)
    carries = lax.rem(plane, 2) == core

    barrier = pltpu.get_barrier_semaphore()
    greetings = []

    def greet(device, wanted=True):
        same = jnp.logical_and(device[0] == section, device[1] == plane)
        wanted = jnp.logical_and(wanted, jnp.logical_not(same))
        greetings.append(jnp.where(wanted, 1, 0))

        @pl.when(wanted)
        def _():
            pl.semaphore_signal(
                barrier,
                inc=1,
                device_id={"section": device[0], "dp": device[1]},
                device_id_type=MESH,
            )

    for other in range(planes):
        greet((section, other))
        greet((layer_here(other), plane), carries)
    for at_row in range(rows):
        owner = layer_device(section, at_row, lax.rem(plane, 2))
        greet((owner[0], plane))
        greet(owner)
        greet((stage, 2 * at_row + core))
        greet(peer(at_row))
    for at_place in range(per_plane):
        greet((2 * chip_of(at_place, row, per_plane) + core, plane))
    greet(partner)
    greet(ahead, stage < last)
    greet(behind, stage > 0)
    matrices = []
    for parts, *members in (
        (2, w_qkv_ref, d_qkv_ref, qkv_shard, qkv_total, packed, more_qkv),
        (1, w_out_ref, d_out_ref, out_shard, out_total, mixed, more_out),
        (2, w_in_ref, d_in_ref, in_shard, in_total, active, more_in),
        (2, w_down_ref, d_down_ref, down_shard, down_total, middle, more_down),
        (1, norm_full, norm_full, norm_shard, norm_total, norm_slots, more_norm),
    ):
        window = members[0].shape[1] // parts
        for part in range(parts):
            matrices.append((*members, pl.ds(part * window, window)))
    count = len(matrices)
    norms = count - 1
    heights = [matrix[0].shape[0] // (planes * rows) for matrix in matrices]

    def view(matrix, member, rows_of):
        return matrices[matrix][member].at[rows_of, matrices[matrix][-1]]

    def slot(matrix, index):
        buffer, height = matrices[matrix][4], heights[matrix]
        per_block = buffer.shape[1] // height
        block, inside = index // per_block, index % per_block
        if not isinstance(inside, int):
            inside = pl.multiple_of(inside * height, height)
        else:
            inside = inside * height
        return buffer.at[block, pl.ds(inside, height), matrices[matrix][-1]]

    def transit(matrix, index):
        return slot(matrix, 2 * (matrices[matrix][4].shape[1] // heights[matrix]) + index)

    def piece(matrix, quarter, at_row):
        height = heights[matrix]
        return pl.ds(pl.multiple_of((quarter * rows + at_row) * height, height), height)

    loads = []
    for matrix in range(norms):
        shard, window = matrices[matrix][2], matrices[matrix][-1]
        loads.append(
            pltpu.make_async_copy(
                shard.at[0, :, window],
                view(matrix, 1, pl.ds(0, shard.shape[1])),
                load_sem.at[matrix],
            )
        )
        loads[-1].start()

    for micro in range(micro_count):
        token_in_ref[micro, 0:1, :] = ids_ref[micro]
        token_in_ref[micro, 1:2, :] = order_ref[micro]
        token_in_ref[micro, 2:3, :] = jnp.full((1, length), stamp_ref[micro], jnp.int32)
    norm_shard[...] = jnp.zeros_like(norm_shard)
    share = gain_shard.shape[2]
    columns = lax.broadcasted_iota(jnp.int32, (2, width), 1)
    mine = jnp.logical_and(columns >= plane * share, columns < (plane + 1) * share)
    for kind, shard in enumerate((gain_shard, bias_shard)):
        spread_out = jnp.concatenate([shard[0]] * planes, axis=1)
        norm_shard[kind * NORM_ROWS : kind * NORM_ROWS + 2, :] = jnp.where(mine, spread_out, 0.0)

    table_rows = table_parts.shape[1]
    work[:table_rows, :] = jnp.zeros((table_rows, width), f32)
    work[:vocab, :] = table_ref[...]
    rest = work[:table_rows, :]
    for part in range(3):
        rounded = rest.astype(bf16)
        table_parts[part] = rounded
        rest = rest - rounded.astype(f32)
    norm_sums[...] = jnp.zeros_like(norm_sums)
    table_sum[...] = jnp.zeros_like(table_sum)
    def rounded(matrix):
        loads[matrix].wait()
        for at_row in range(rows):
            source = view(matrix, 1, pl.ds(at_row * heights[matrix], heights[matrix]))
            transit(matrix, planes + at_row)[...] = source[...].astype(bf16)

    rounded(0)
    pl.semaphore_wait(barrier, sum(greetings))

    gives_tokens = jnp.logical_and(place == 0, lane_index == plane)
    takes_tokens = jnp.logical_or(stage == 0, stage == last)

    def token_copy(index, target):
        return (
            token_in_ref,
            token_ref,
            token_send_sem.at[index],
            token_recv_sem,
            (section, target),
        )

    @pl.when(gives_tokens)
    def _():
        for index, target in enumerate((0, planes - 1)):
            start_copy(*token_copy(index, target), here)

    def spread_args(matrix, at_row):
        target, _ = layer_device(section, at_row, lax.rem(plane, 2))
        if matrix == norms:
            source = norm_shard.at[pl.ds(at_row * NORM_ROWS, NORM_ROWS)]
        else:
            source = transit(matrix, planes + at_row)
        return (
            source,
            transit(matrix, home_plane),
            spread_send.at[matrix, at_row],
            spread_recv.at[matrix, home_plane],
            (target, plane),
        )

    def plane_args(matrix, to_plane, from_plane):
        return (
            transit(matrix, to_plane),
            view(matrix, 0, piece(matrix, from_plane, row)),
            plane_send.at[matrix, to_plane],
            plane_recv.at[matrix, lax.div(from_plane, 2)],
            (section, to_plane),
        )

    def peer_args(matrix, quarter_pair, from_row, to_row):
        part = view(matrix, 0, piece(matrix, 2 * quarter_pair + core, from_row))
        return (
            part,
            part,
            peer_send.at[matrix, quarter_pair, to_row],
            peer_recv.at[matrix, quarter_pair, from_row],
            peer(to_row),
        )

    def core_args(matrix, quarter_pair, at_row, from_core):
        part = view(matrix, 0, piece(matrix, 2 * quarter_pair + from_core, at_row))
        return (
            part,
            part,
            core_send.at[matrix, quarter_pair, at_row],
            core_recv.at[matrix, quarter_pair, at_row],
            partner,
        )

    def spread(matrix):
        if matrix not in (0, norms):
            rounded(matrix)
        for at_row in range(rows):
            start_copy(*spread_args(matrix, at_row), here)

    def along_planes(matrix):
        @pl.when(carries)
        def _():
            for to_plane in range(planes):
                landed = transit(matrix, to_plane)
                remote_copy(
                    landed,
                    landed,
                    spread_send.at[matrix, 0],
                    spread_recv.at[matrix, to_plane],
                    partner,
                ).wait_recv()
                start_copy(*plane_args(matrix, to_plane, plane), here)

    def between_peers(matrix):
        for pair in range(rows):
            remote_copy(*plane_args(matrix, 0, 2 * pair + core)).wait_recv()
            for to_row in range(rows):
                @pl.when(to_row != row)
                def _():
                    remote_copy(*peer_args(matrix, pair, row, to_row)).start()

            remote_copy(*core_args(matrix, pair, row, core)).start()

    def between_cores(matrix):
        for pair in range(rows):
            for from_row in range(rows):
                @pl.when(from_row != row)
                def _():
                    remote_copy(*peer_args(matrix, pair, from_row, from_row)).wait_recv()
                    remote_copy(*core_args(matrix, pair, from_row, core)).start()

    def gathered(matrix):
        for pair in range(rows):
            for at_row in range(rows):
                remote_copy(*core_args(matrix, pair, at_row, 1 - core)).wait_recv()

    def gather_sent(matrix):
        for at_row in range(rows):
            wait_sent(*spread_args(matrix, at_row), here)

        @pl.when(carries)
        def _():
            for to_plane in range(planes):
                wait_sent(*plane_args(matrix, to_plane, plane), here)

        for pair in range(rows):
            for at_row in range(rows):
                @pl.when(at_row != row)
                def _():
                    remote_copy(*peer_args(matrix, pair, row, at_row)).wait_send()

                remote_copy(*core_args(matrix, pair, at_row, core)).wait_send()

    letters = lax.broadcasted_iota(jnp.int32, (table_rows, length), 0)
    lane = lax.broadcasted_iota(jnp.int32, (length, pair_width), 1)
    lower = lane < head_size

    def shown_rows(micro):
        rows_of = token_ref[micro]
        visible = rows_of[1:2] < rows_of[2:3]
        shown = jnp.where(visible, rows_of[0:1], vocab - 1)
        return (letters == shown).astype(bf16)

    def stacked(pair):
        zero = jnp.zeros_like(pair)
        return jnp.concatenate(
            [jnp.where(lower, pair, zero), jnp.where(lower, zero, pair)], axis=0
        )

    def load_hidden(micro):
        @pl.when(stage == 0)
        def _():
            hot = shown_rows(micro)
            total = dot(hot, table_parts[2], 0, 0)
            total = total + dot(hot, table_parts[1], 0, 0)
            total = total + dot(hot, table_parts[0], 0, 0)
            work[...] = total * EMBED_GAIN

        @pl.when(stage > 0)
        def _():
            work[...] = h_in[micro].astype(f32)

    def hidden_copy(micro, target):
        slot = lax.rem(micro, 2)
        return pltpu.make_async_remote_copy(
            src_ref=h_send.at[slot],
            dst_ref=h_in.at[micro],
            send_sem=h_send_sem.at[slot],
            recv_sem=h_recv_sem.at[micro],
            device_id={"section": target[0], "dp": target[1]},
            device_id_type=MESH,
        )

    def gradient_copy(micro, target):
        slot = lax.rem(micro, 2)
        return pltpu.make_async_remote_copy(
            src_ref=g_send.at[slot],
            dst_ref=g_in.at[micro],
            send_sem=g_send_sem.at[slot],
            recv_sem=g_recv_sem.at[micro],
            device_id={"section": target[0], "dp": target[1]},
            device_id_type=MESH,
        )

    def forward_attention(micro):
        load_hidden(micro)
        hidden = work[...]
        unit, _ = unit_rows(hidden)
        normed = (unit * gain_ref[0:1, :] + bias_ref[0:1, :]).astype(bf16)
        packed[micro] = dot(normed, w_qkv_ref[...], 1, 0).astype(bf16)
        pairs = HEADS // 2

        def block(member, pair):
            at = member * width + pair * pair_width
            return packed[micro, :, at : at + pair_width]

        def scores_of(pair):
            query = block(0, pair) * jnp.asarray(score_scale, bf16)
            return dot(stacked(query), block(1, pair), 1, 1)

        waiting = [scores_of(pair) for pair in range(AHEAD)]
        for pair in range(pairs):
            if pair + AHEAD < pairs:
                waiting.append(scores_of(pair + AHEAD))
            scores = waiting[pair]
            largest = jnp.max(scores, axis=-1, keepdims=True)
            powers = jnp.exp(scores - largest)
            total = jnp.sum(powers, axis=-1, keepdims=True)
            attention = (powers * (1.0 / total)).astype(bf16)
            attention_kept[2 * pair] = attention[:length]
            attention_kept[2 * pair + 1] = attention[length:]
            found = dot(attention, block(2, pair), 1, 0)
            at = pair * pair_width
            mixed[micro, :, at : at + pair_width] = jnp.where(
                lower, found[:length], found[length:]
            ).astype(bf16)
        pltpu.make_async_copy(attention_kept, stash_ref.at[micro], stash_sem).start()
        between = hidden + dot(mixed[micro], w_out_ref[...], 1, 0)
        high = between.astype(bf16)
        middle[2 * micro + 0] = high
        middle[2 * micro + 1] = (between - high.astype(f32)).astype(bf16)
        work[...] = between
        unit, _ = unit_rows(between)
        return (unit * gain_ref[1:2, :] + bias_ref[1:2, :]).astype(bf16)

    def forward_lift(micro, normed_two):
        for at in range(0, hidden_units, FF_CHUNK):
            lifted = dot(normed_two, w_in_ref[:, at : at + FF_CHUNK], 1, 0)
            bent = (root * 0.044715) * (lifted * lifted)
            half = 0.5 + 0.5 * jnp.tanh(lifted * (bent + root))
            gelu = lifted * half
            active[micro, :, at : at + FF_CHUNK] = gelu.astype(bf16)
            slope[micro, :, at : at + FF_CHUNK] = (
                half + gelu * ((1.0 - half) * (6.0 * bent + 2.0 * root))
            ).astype(bf16)
    def forward_end(micro):
        if stages > 1:
            @pl.when(jnp.logical_and(micro >= 2, stage < last))
            def _():
                hidden_copy(micro - 2, ahead).wait_send()
        slot = lax.rem(micro, 2)
        h_send[slot] = (work[...] + dot(active[micro], w_down_ref[...], 1, 0)).astype(bf16)
        if stages > 1:
            @pl.when(stage < last)
            def _():
                hidden_copy(micro, ahead).start()
        pltpu.make_async_copy(attention_kept, stash_ref.at[micro], stash_sem).wait()

    def forward(micro):
        if stages > 1:
            @pl.when(stage > 0)
            def _():
                hidden_copy(micro, behind).wait_recv()

        forward_lift(micro, forward_attention(micro))
        forward_end(micro)

    def set_norms():
        for kind, ref in enumerate((gain_ref, bias_ref)):
            total = jnp.zeros((NORM_ROWS, width), f32)
            for quarter in range(planes):
                start = (quarter * rows + kind) * NORM_ROWS
                total = total + norm_full[start : start + NORM_ROWS, :]
            ref[...] = total.astype(bf16).astype(f32)

    out_unit, in_unit = 2, 4
    steps_of_gather = (spread, along_planes, between_peers, between_cores, gathered)
    order = (norms, *range(norms))
    depths = (0, 1, 2, 4, 5)
    for turn_at in range(count + depths[-1]):
        for depth, action in zip(depths, steps_of_gather):
            if 0 <= turn_at - depth < count:
                action(order[turn_at - depth])
        done = turn_at - depths[-1]
        if done == 0:
            set_norms()
        if done == order.index(out_unit):
            @pl.when(takes_tokens)
            def _():
                remote_copy(*token_copy(0, 0)).wait_recv()

            @pl.when(stage == 0)
            def _():
                g_send[0] = forward_attention(0)

        if done == order.index(in_unit):
            @pl.when(stage == 0)
            def _():
                forward_lift(0, g_send[0])

        if 7 <= turn_at <= 10:
            sums = (d_qkv_ref, d_out_ref, d_in_ref, d_down_ref)[turn_at - 7]
            sums[...] = jnp.zeros_like(sums)
    @pl.when(stage == 0)
    def _():
        forward_end(0)

    for matrix in range(count):
        gather_sent(matrix)

    @pl.when(gives_tokens)
    def _():
        for index, target in enumerate((0, planes - 1)):
            wait_sent(*token_copy(index, target), here)


    def head(micro):
        unit, scale = unit_rows(h_send[lax.rem(micro, 2)].astype(f32))
        rounded = unit.astype(bf16)
        logits = dot(table_parts[0], rounded, 1, 1)
        logits = jnp.where(letters < vocab, logits, -jnp.inf)
        largest = jnp.max(logits, axis=0, keepdims=True)
        powers = jnp.exp(logits - largest)
        total = jnp.sum(powers, axis=0, keepdims=True)
        rows_of = token_ref[micro]
        stamp = rows_of[2:3]
        weight = jnp.where(rows_of[1:2] < stamp, 0.0, 1.0 / (length - stamp).astype(f32))
        target = (letters == rows_of[0:1]).astype(f32)
        g_logits = (weight * (powers / total - target)).astype(bf16)
        table_sum[...] += dot(g_logits, rounded, 1, 0)
        g_unit = dot(g_logits, table_parts[0], 0, 0)
        g_in[micro] = unit_back(g_unit, unit, scale).astype(bf16)

    def backward(micro):
        @pl.when(stage == last)
        def _():
            head(micro)

        if stages > 1:
            @pl.when(stage < last)
            def _():
                gradient_copy(micro, ahead).wait_recv()
        load = pltpu.make_async_copy(stash_ref.at[micro], attention_kept, stash_sem)
        load.start()
        g_out = g_in[micro]
        for at in range(0, hidden_units, FF_CHUNK):
            g_active = dot(g_out, w_down_ref[at : at + FF_CHUNK, :], 1, 1)
            slope[micro, :, at : at + FF_CHUNK] = (
                g_active * slope[micro, :, at : at + FF_CHUNK].astype(f32)
            ).astype(bf16)
        g_normed = dot(slope[micro], w_in_ref[...], 1, 1)
        unit, scale = unit_rows(middle[2 * micro + 0].astype(f32) + middle[2 * micro + 1].astype(f32))
        middle[2 * micro + 0] = (unit * gain_ref[1:2, :] + bias_ref[1:2, :]).astype(bf16)
        norm_sums[1] += fold_rows(g_normed * unit)
        norm_sums[3] += fold_rows(g_normed)
        g_middle = g_out.astype(f32) + unit_back(g_normed * gain_ref[1:2, :], unit, scale)
        g_attended = g_middle.astype(bf16)
        middle[2 * micro + 1] = g_attended
        g_mixed = dot(g_attended, w_out_ref[...], 1, 1).astype(bf16)
        load_hidden(micro)
        load.wait()
        pairs = HEADS // 2

        def block(member, pair):
            at = member * width + pair * pair_width
            return packed[micro, :, at : at + pair_width]

        def put(member, pair, value):
            at = member * width + pair * pair_width
            packed[micro, :, at : at + pair_width] = value.astype(bf16)

        def g_attention_of(pair):
            at = pair * pair_width
            g_pair = stacked(g_mixed[:, at : at + pair_width])
            return g_pair, dot(g_pair, block(2, pair), 1, 1)

        waiting = [g_attention_of(pair) for pair in range(AHEAD)]
        for pair in range(pairs):
            if pair + AHEAD < pairs:
                waiting.append(g_attention_of(pair + AHEAD))
            g_pair, g_attention = waiting[pair]
            low = attention_kept[2 * pair : 2 * pair + 2].reshape(2 * length, length)
            attention = low.astype(f32)
            inner = jnp.sum(attention * g_attention, axis=-1, keepdims=True)
            g_scores = (attention * (g_attention - inner)).astype(bf16)
            key, query = block(1, pair), stacked(block(0, pair))
            g_values = dot(low, g_pair, 0, 0)
            g_queries = dot(g_scores, key, 1, 0)
            g_keys = dot(g_scores, query, 0, 0)
            put(0, pair, jnp.where(lower, g_queries[:length], g_queries[length:]) * score_scale)
            put(1, pair, g_keys * score_scale)
            put(2, pair, g_values)
        g_normed = dot(packed[micro], w_qkv_ref[...], 1, 1)
        unit, scale = unit_rows(work[...])
        h_in[micro] = (unit * gain_ref[0:1, :] + bias_ref[0:1, :]).astype(bf16)
        g_hidden = g_middle + unit_back(g_normed * gain_ref[0:1, :], unit, scale)

        @pl.when(stage == 0)
        def _():
            hot = shown_rows(micro)
            high = g_hidden.astype(bf16)
            low = (g_hidden - high.astype(f32)).astype(bf16)
            table_sum[...] += EMBED_GAIN * (dot(hot, high, 1, 0) + dot(hot, low, 1, 0))

        if stages > 1:
            @pl.when(stage > 0)
            def _():
                @pl.when(micro >= 2)
                def _():
                    gradient_copy(micro - 2, behind).wait_send()

                g_send[lax.rem(micro, 2)] = g_hidden.astype(bf16)
                gradient_copy(micro, behind).start()

        norm_sums[0] += fold_rows(g_normed * unit)
        norm_sums[2] += fold_rows(g_normed)

    def weights(micro):
        d_down_ref[...] += dot(active[micro], g_in[micro], 0, 0)
        d_in_ref[...] += dot(middle[2 * micro + 0], slope[micro], 0, 0)
        d_out_ref[...] += dot(mixed[micro], middle[2 * micro + 1], 0, 0)
        d_qkv_ref[...] += dot(h_in[micro], packed[micro], 0, 0)

    warm = jnp.minimum(WARM * (last - stage), micro_count - 1)
    steps = 2 * micro_count

    def step(index, carry):
        b_micro = index - warm
        w_micro = index - micro_count

        @pl.when(jnp.logical_and(index < micro_count, jnp.logical_or(stage > 0, index > 0)))
        def _():
            forward(index)

        @pl.when(w_micro >= 0)
        def _():
            weights(w_micro)

        @pl.when(jnp.logical_and(b_micro >= 0, b_micro < micro_count))
        def _():
            backward(b_micro)

        return carry

    lax.fori_loop(0, steps, step, 0)

    if stages > 1:
        for micro in range(max(micro_count - 2, 0), micro_count):
            @pl.when(stage < last)
            def _():
                hidden_copy(micro, ahead).wait_send()

            @pl.when(stage > 0)
            def _():
                gradient_copy(micro, behind).wait_send()

    def table_copy(source, target, send, recv, device):
        return remote_copy(source, target, table_send.at[send], table_recv.at[recv], device)

    def lane_copy():
        return table_copy(table_sum, table_slots.at[0], 0, 0, (section, 0))

    def table_core_copy():
        return table_copy(table_sum, table_slots.at[1], 1, 1, partner)

    def table_peer_copy(from_row, to_row):
        return table_copy(
            table_sum, table_slots.at[2 + from_row], 2 + to_row, 2 + from_row, peer(to_row)
        )

    def table_down_copy(to_plane):
        return table_copy(
            d_table_ref, d_table_ref, 2 + rows + to_plane, 2 + rows, (section, to_plane)
        )

    def table_side_copy(to_place):
        target = 2 * chip_of(to_place, row, per_plane) + core
        return table_copy(
            d_table_ref, d_table_ref, 2 + rows + planes + to_place, 2 + rows, (target, plane)
        )

    @pl.when(stage == last)
    def _():
        lane_copy().start()

    def table_cores():
        @pl.when(stage == 0)
        def _():
            lane_copy().wait_recv()
            table_sum[...] += table_slots[0]
            table_core_copy().start()

    def table_peers():
        @pl.when(stage == 0)
        def _():
            table_core_copy().wait()
            table_sum[...] += table_slots[1]
            for to_row in range(rows):
                @pl.when(to_row != row)
                def _():
                    table_peer_copy(row, to_row).start()

    def table_side():
        for to_place in range(1, per_plane):
            table_side_copy(to_place).start()

    def table_down():
        @pl.when(stage == 0)
        def _():
            total = table_sum[...]
            for from_row in range(rows):
                @pl.when(from_row != row)
                def _():
                    table_peer_copy(from_row, from_row).wait_recv()

                total = total + jnp.where(from_row != row, table_slots[2 + from_row], 0.0)
            d_table_ref[...] = total
            for to_plane in range(1, planes):
                table_down_copy(to_plane).start()
            table_side()

    def table_done():
        @pl.when(place > 0)
        def _():
            table_side_copy(0).wait_recv()

        @pl.when(stage == last)
        def _():
            lane_copy().wait_send()

        @pl.when(stage == 0)
        def _():
            for to_row in range(rows):
                @pl.when(to_row != row)
                def _():
                    table_peer_copy(row, to_row).wait_send()

            for to_plane in range(1, planes):
                table_down_copy(to_plane).wait_send()

        @pl.when(place == 0)
        def _():
            for to_place in range(1, per_plane):
                table_side_copy(to_place).wait_send()

    for kind in range(2):
        totals = [
            jnp.sum(norm_sums[2 * kind + member], axis=0, keepdims=True) for member in range(2)
        ]
        block = jnp.concatenate(totals + [jnp.zeros((NORM_ROWS - 2, width), f32)], axis=0)
        for quarter in range(planes):
            start = (quarter * rows + kind) * NORM_ROWS
            norm_full[start : start + NORM_ROWS, :] = block

    pl.semaphore_signal(
        core_free, inc=1, device_id={"section": partner[0], "dp": partner[1]}, device_id_type=MESH
    )
    for at_row in range(rows):
        @pl.when(at_row != row)
        def _():
            far = peer(at_row)
            pl.semaphore_signal(
                peer_free, inc=1, device_id={"section": far[0], "dp": far[1]}, device_id_type=MESH
            )

    def direct_quarter(at_plane):
        return jnp.where(at_plane < planes - 1, at_plane + 1, at_plane - 1)

    def is_direct(pair):
        return 2 * pair + core == direct_quarter(plane)

    owns_direct = plane == direct_quarter(home_plane)

    def direct_landing(matrix, from_row, at_row):
        rows_of = pl.ds(at_row * heights[matrix], heights[matrix])
        if from_row == 0:
            return view(matrix, 3, rows_of)
        return matrices[matrix][5].at[from_row - 1, rows_of, matrices[matrix][-1]]

    def direct_args(matrix, pair, from_row, at_row):
        return (
            slot(matrix, 2 * rows * rows + pair * rows + at_row),
            direct_landing(matrix, from_row, at_row),
            peer_send.at[matrix, pair, at_row],
            direct_recv.at[matrix, from_row, at_row],
            (stage, 2 * pair + core),
        )

    def send_direct(matrix, pair, at_row):
        for from_row in range(rows):
            @pl.when(from_row == row)
            def _():
                remote_copy(*direct_args(matrix, pair, from_row, at_row)).start()

    def core_sum_args(matrix, pair, at_row):
        index = pair * rows + at_row
        return (
            slot(matrix, index),
            slot(matrix, rows * rows + index),
            core_send.at[matrix, pair, at_row],
            core_recv.at[matrix, pair, at_row],
            partner,
        )

    def peer_sum_args(matrix, pair, from_row, to_row):
        return (
            slot(matrix, 2 * rows * rows + pair * rows + to_row),
            slot(matrix, 3 * rows * rows + pair * rows + from_row),
            peer_send.at[matrix, pair, to_row],
            peer_recv.at[matrix, pair, from_row],
            peer(to_row),
        )

    def total_args(matrix, pair):
        height = heights[matrix]
        return (
            slot(matrix, 2 * rows * rows + pair * rows + row),
            view(matrix, 3, pl.ds(pl.multiple_of(row * height, height), height)),
            total_send.at[matrix, pair],
            total_recv.at[matrix, row],
            (stage, 2 * pair + core),
        )

    def give_core(matrix):
        for pair in range(rows):
            for at_row in range(rows):
                args = core_sum_args(matrix, pair, at_row)
                part = view(matrix, 1, piece(matrix, 2 * pair + 1 - core, at_row))
                args[0][...] = part[...].astype(args[0].dtype)
                remote_copy(*args).start()

    def give_peers(matrix):
        for pair in range(rows):
            for at_row in range(rows):
                remote_copy(*core_sum_args(matrix, pair, at_row)).wait_recv()
                landed = slot(matrix, rows * rows + pair * rows + at_row)
                part = view(matrix, 1, piece(matrix, 2 * pair + core, at_row))
                total = part[...] + landed[...].astype(f32)
                direct = is_direct(pair)

                @pl.when(direct)
                def _():
                    staged = slot(matrix, 2 * rows * rows + pair * rows + at_row)
                    staged[...] = total.astype(staged.dtype)
                    send_direct(matrix, pair, at_row)

                @pl.when(jnp.logical_and(jnp.logical_not(direct), at_row != row))
                def _():
                    args = peer_sum_args(matrix, pair, row, at_row)
                    args[0][...] = total.astype(args[0].dtype)
                    remote_copy(*args).start()

                @pl.when(jnp.logical_and(jnp.logical_not(direct), at_row == row))
                def _():
                    part[...] = total

    def give_total(matrix, pair):
        part = view(matrix, 1, piece(matrix, 2 * pair + core, row))
        for from_row in range(rows):
            @pl.when(from_row != row)
            def _():
                remote_copy(*peer_sum_args(matrix, pair, from_row, from_row)).wait_recv()
                landed = slot(matrix, 3 * rows * rows + pair * rows + from_row)
                part[...] += landed[...].astype(f32)

        args = total_args(matrix, pair)
        args[0][...] = part[...].astype(args[0].dtype)
        start_copy(*args, here)

    def give_totals(matrix):
        for pair in range(rows):
            @pl.when(jnp.logical_not(is_direct(pair)))
            def _():
                give_total(matrix, pair)

    def sent(matrix, pair):
        for at_row in range(rows):
            @pl.when(at_row != row)
            def _():
                remote_copy(*peer_sum_args(matrix, pair, row, at_row)).wait_send()

        wait_sent(*total_args(matrix, pair), here)

    def finish(matrix):
        height = heights[matrix]

        @pl.when(owns_direct)
        def _():
            for at_row in range(rows):
                for from_row in range(rows):
                    remote_copy(*direct_args(matrix, 0, from_row, at_row)).wait_recv()
                total = direct_landing(matrix, 0, at_row)
                value = total[...].astype(f32)
                for from_row in range(1, rows):
                    value = value + direct_landing(matrix, from_row, at_row)[...].astype(f32)
                total[...] = value.astype(total.dtype)

        @pl.when(jnp.logical_not(owns_direct))
        def _():
            for from_row in range(rows):
                part = view(matrix, 3, pl.ds(from_row * height, height))
                remote_copy(
                    part, part, total_send.at[matrix, 0], total_recv.at[matrix, from_row], partner
                ).wait_recv()

        for pair in range(rows):
            for at_row in range(rows):
                remote_copy(*core_sum_args(matrix, pair, at_row)).wait_send()

            @pl.when(is_direct(pair))
            def _():
                for at_row in range(rows):
                    remote_copy(*direct_args(matrix, pair, 0, at_row)).wait_send()

            @pl.when(jnp.logical_not(is_direct(pair)))
            def _():
                sent(matrix, pair)

    order = tuple(reversed(range(count)))
    table_cores()
    pl.semaphore_wait(core_free, 1)
    for position in range(count + 4):
        if position < count:
            give_core(order[position])
        if position == 1:
            table_peers()
            pl.semaphore_wait(peer_free, rows - 1)
        if 0 <= position - 1 < count:
            give_peers(order[position - 1])
        if 0 <= position - 4 < count:
            give_totals(order[position - 4])
        if position == 4:
            table_down()

    @pl.when(jnp.logical_and(place == 0, plane > 0))
    def _():
        table_down_copy(0).wait_recv()
        table_side()

    for matrix in order:
        finish(matrix)
    table_done()


def run_pipeline(stages, planes, token_ids, order, timesteps, table, gain, bias, *shards):
    w_qkv, w_out, w_in, w_down = shards
    micro_count, _, length = token_ids.shape
    width = table.shape[1]
    hidden_units = w_in.shape[2]
    rows = planes // 2
    table_rows = -(-table.shape[0] // 32) * 32
    bf16, f32 = jnp.bfloat16, jnp.float32
    vmem = pl.BlockSpec(memory_space=pltpu.VMEM)
    anywhere = pl.BlockSpec(memory_space=pl.ANY)
    scalars = pl.BlockSpec(memory_space=pltpu.SMEM)
    tokens = (micro_count, 3, length)
    norm_shard = (rows * NORM_ROWS, width)
    full = [(shard.shape[1] * planes, shard.shape[2]) for shard in shards]
    norm_full = (planes * rows * NORM_ROWS, width)
    outs = (
        jax.ShapeDtypeStruct((table_rows, width), f32),
        jax.ShapeDtypeStruct(norm_shard, f32),
        *(jax.ShapeDtypeStruct(shard.shape[1:], bf16) for shard in shards),
        jax.ShapeDtypeStruct((micro_count, HEADS, length, length), bf16),
    )
    rows_shape = (micro_count, length, width)
    units = 8
    pieces = (units, rows, rows)
    return pl.pallas_call(
        functools.partial(pipeline_kernel, stages, planes),
        out_shape=outs,
        in_specs=[vmem] * 2 + [scalars] + [vmem] * 3 + [anywhere] * 4,
        out_specs=[vmem] * 6 + [anywhere],
        scratch_shapes=[
            pltpu.VMEM(tokens, jnp.int32),
            pltpu.VMEM(norm_shard, f32),
            pltpu.VMEM(tokens, jnp.int32),
            pltpu.VMEM(rows_shape, bf16),
            pltpu.VMEM(rows_shape, bf16),
            pltpu.VMEM((2, length, width), bf16),
            pltpu.VMEM((2, length, width), bf16),
            pltpu.VMEM((micro_count, length, 3 * width), bf16),
            pltpu.VMEM(rows_shape, bf16),
            pltpu.VMEM((2 * micro_count, length, width), bf16),
            pltpu.VMEM((micro_count, length, hidden_units), bf16),
            pltpu.VMEM((micro_count, length, hidden_units), bf16),
            pltpu.VMEM((HEADS, length, length), bf16),
            pltpu.VMEM((length, width), f32),
            pltpu.VMEM((3, table_rows, width), bf16),
            pltpu.VMEM((4, 8, width), f32),
            pltpu.VMEM((table_rows, width), f32),
            pltpu.VMEM((4 * rows * rows, NORM_ROWS, width), f32),
            pltpu.VMEM(norm_full, f32),
            *(pltpu.VMEM(shape, bf16) for shape in full),
            pltpu.VMEM((NORM_ROWS, width), f32),
            pltpu.VMEM((NORM_ROWS, width), f32),
            *(pltpu.VMEM(shape, f32) for shape in full),
            pltpu.SemaphoreType.DMA((2,)),
            pltpu.SemaphoreType.DMA((micro_count,)),
            pltpu.SemaphoreType.DMA((2,)),
            pltpu.SemaphoreType.DMA((micro_count,)),
            pltpu.SemaphoreType.DMA,
            pltpu.SemaphoreType.DMA((2,)),
            pltpu.SemaphoreType.DMA,
            pltpu.SemaphoreType.DMA((units,)),
            pltpu.SemaphoreType.DMA((units, rows)),
            pltpu.SemaphoreType.DMA((units, planes)),
            pltpu.SemaphoreType.DMA((units, planes)),
            pltpu.SemaphoreType.DMA((units, rows)),
            pltpu.SemaphoreType.DMA(pieces),
            pltpu.SemaphoreType.DMA(pieces),
            pltpu.SemaphoreType.DMA(pieces),
            pltpu.SemaphoreType.DMA(pieces),
            pltpu.SemaphoreType.REGULAR,
            pltpu.SemaphoreType.REGULAR,
            pltpu.SemaphoreType.DMA((units, rows)),
            pltpu.SemaphoreType.DMA((units, rows)),
            pltpu.VMEM((2 + rows, table_rows, width), f32),
            pltpu.SemaphoreType.DMA((2 + rows + planes + stages // planes,)),
            pltpu.SemaphoreType.DMA((3 + rows,)),
            pltpu.VMEM((rows - 1, *norm_shard), f32),
            *(pltpu.VMEM((rows - 1, *shard.shape[1:]), bf16) for shard in shards),
            pltpu.SemaphoreType.DMA(pieces),
        ],
        compiler_params=pltpu.CompilerParams(
            vmem_limit_bytes=(64 << 20) - (192 << 10), collective_id=0, has_side_effects=True
        ),
    )(token_ids, order, timesteps, table, gain, bias, w_qkv, w_out, w_in, w_down)


def finish_kernel(planes, stages, *refs):
    table_ref, norm_ref, *totals = refs[:6]
    table_part, gain_part, bias_part, *results = refs[6:]
    section, plane = lax.axis_index("section"), lax.axis_index("dp")
    for total, result in zip(totals, results):
        result[0] = total[...].astype(jnp.float32)

    @pl.when(pl.program_id(0) == 0)
    def _():
        vocab, columns = table_part.shape
        part = jnp.zeros((vocab, columns), jnp.float32)
        for at in range(stages):
            block = table_ref[:vocab, at * columns : (at + 1) * columns]
            part = jnp.where(section == at, block, part)
        table_part[...] = part
        share = gain_part.shape[2]
        for kind, result in enumerate((gain_part, bias_part)):
            part = jnp.zeros((2, share), jnp.float32)
            for at in range(planes):
                start = kind * NORM_ROWS
                block = norm_ref[start : start + 2, at * share : (at + 1) * share]
                part = jnp.where(plane == at, block, part)
            result[0] = part


def run_finish(stages, planes, vocab, share, sums):
    f32 = jnp.float32
    steps = 1
    whole = [pl.BlockSpec(value.shape, lambda i: (0, 0)) for value in sums[:2]]
    blocks = [
        pl.BlockSpec((value.shape[0] // steps, value.shape[1]), lambda i: (i, 0))
        for value in sums[2:]
    ]
    out_blocks = [
        pl.BlockSpec((1, value.shape[0] // steps, value.shape[1]), lambda i: (0, i, 0))
        for value in sums[2:]
    ]
    columns = sums[0].shape[1] // stages
    return pl.pallas_call(
        functools.partial(finish_kernel, planes, stages),
        grid=(steps,),
        out_shape=(
            jax.ShapeDtypeStruct((vocab, columns), f32),
            jax.ShapeDtypeStruct((1, 2, share), f32),
            jax.ShapeDtypeStruct((1, 2, share), f32),
            *(jax.ShapeDtypeStruct((1, *value.shape), f32) for value in sums[2:]),
        ),
        in_specs=whole + blocks,
        out_specs=[
            pl.BlockSpec((vocab, columns), lambda i: (0, 0)),
            pl.BlockSpec((1, 2, share), lambda i: (0, 0, 0)),
            pl.BlockSpec((1, 2, share), lambda i: (0, 0, 0)),
            *out_blocks,
        ],
    )(*sums)


def body(token_ids, order, timesteps, table, norm_gain, norm_bias, w_qkv, w_out, w_in, w_down):
    stages, planes = lax.axis_size("section"), lax.axis_size("dp")
    sums = run_pipeline(
        stages,
        planes,
        token_ids,
        order,
        timesteps[:, 0],
        table,
        norm_gain,
        norm_bias,
        w_qkv,
        w_out,
        w_in,
        w_down,
    )
    return tuple(run_finish(stages, planes, table.shape[0], norm_gain.shape[2], sums[:6]))


def solution(mesh):
    in_specs = (
        P(None, "dp", None),
        P(None, "dp", None),
        P(None, "dp"),
        P(),
        P("section", None, "dp"),
        P("section", None, "dp"),
        P("section", "dp", None),
        P("section", "dp", None),
        P("section", "dp", None),
        P("section", "dp", None),
    )
    out_specs = (
        P(None, "section"),
        P("section", None, "dp"),
        P("section", None, "dp"),
        P("section", "dp", None),
        P("section", "dp", None),
        P("section", "dp", None),
        P("section", "dp", None),
    )
    return jax.shard_map(body, mesh=mesh, in_specs=in_specs, out_specs=out_specs, check_vma=False)
```
